32 devices in a mesh: groups: 2 (over x), wide: 8 (over z, y), narrow: 2 (over core).
Axes of the slice: x: 2, y: 2, z: 4, core: 2. Of those that a mesh axis runs over, the one named last changes fastest.
Arguments:
- voxels: bfloat16 [131072, 128], P(('groups', 'wide', 'narrow')), parts along dimension 0, may hold values from -6 to 6
- counts: int32 [32], P('groups'), parts along dimension 0, may hold values from 2048 to 4096, as said below
- neighbours: int32 [27, 131072], P(None, ('groups', 'wide', 'narrow')), parts along dimension 1, may hold values from -1 to 65535, as said below
- conv_weight: bfloat16 [2, 27, 128, 128], replicated, may hold values from -0.109375 to 0.109375
- linear_weight: bfloat16 [2, 128, 128], replicated, may hold values from -0.5 to 0.5
- destination: int32 [131072], P(('groups', 'wide', 'narrow')), parts along dimension 0, may hold values from 0 to 65535, as said below
Outputs:
- serial: bfloat16 [131072, 128], P(('groups', 'wide', 'narrow')), parts along dimension 0
The draws below stay inside these ranges and needn't reach their ends.
There are 2 independent parts, one for each index of `groups`. The reference program is written for one: setup_inputs(seed, part) draws one part's arguments, and reference() takes and returns one part's arrays. A program takes and returns all parts, laid end to end along the dimension named above; an argument that names none is the same for every part. Nothing has to cross between parts.
Inputs may be any that keep to these rules, and one draw needn't show every extreme that they name: `counts`: each device's block has 2048 to 4096 live rows, its first ones; some device is full in every draw. `neighbours`: an entry of column i is -1 or a row within 128 of i; offset 13 is row i itself; offsets 0 and 26 are rows i - 128 and i + 128 where those exist. `destination`: A permutation of the rows; the rows of one device go to every device, exactly 256 to each.
All inputs are finite; a program needn't handle non-finite values.
Results may differ from the reference program's by a relative error of at most 0.0056.
Values may be sent and summed in bfloat16 or wider, within the bound.
No kernel may reach another device: no remote copies, remote signals or barrier semaphores. Data moves between devices by JAX's collectives and lax.ppermute only.
A program may use at most 64 MiB of HBM per device.

```python
import jax
import jax.numpy as jnp
from jax import lax

C = 128
OFFSETS = 27
VOX_DEV = 4096
HALO = 128
SHARDS = 16
VOXELS = 65536


def draw_counts(key, part):
    key = jax.random.fold_in(key, 11)
    first, second = jax.random.split(key)
    values = jax.random.randint(first, (SHARDS,), VOX_DEV // 2, VOX_DEV + 1)
    fullest = jax.random.randint(second, (), 0, SHARDS)
    return jnp.where(jnp.arange(SHARDS) == fullest, VOX_DEV, values).astype(jnp.int32)


def draw_neighbours(key, part):
    key = jax.random.fold_in(key, 23)
    first, second = jax.random.split(key)
    row_ids = jnp.arange(VOXELS, dtype=jnp.int32)[None, :]
    offsets = jax.random.randint(first, (OFFSETS, VOXELS), -HALO, HALO + 1)
    present = jax.random.randint(second, (OFFSETS, VOXELS), 0, 2) == 1
    order = jnp.arange(OFFSETS, dtype=jnp.int32)[:, None]
    offsets = jnp.where(order == 13, 0, offsets)
    offsets = jnp.where(order == 0, -HALO, offsets)
    offsets = jnp.where(order == OFFSETS - 1, HALO, offsets)
    present = present | (order == 13) | (order == 0) | (order == OFFSETS - 1)
    targets = row_ids + offsets
    inside = (targets >= 0) & (targets < VOXELS) & present
    return jnp.where(inside, targets, -1).astype(jnp.int32)


def draw_destination(key, part):
    key = jax.random.fold_in(key, 37)
    first, second, third = jax.random.split(key, 3)
    capacity = VOX_DEV // SHARDS
    shifts = jax.random.permutation(first, SHARDS)
    source_perm = jax.vmap(lambda sub: jax.random.permutation(sub, VOX_DEV))(jax.random.split(second, SHARDS))
    target_perm = jax.vmap(lambda sub: jax.random.permutation(sub, VOX_DEV))(jax.random.split(third, SHARDS))
    source_dev = jnp.arange(SHARDS, dtype=jnp.int32)[:, None]
    bucket = source_perm // capacity
    within = source_perm % capacity
    target_dev = (source_dev + shifts[bucket]) % SHARDS
    target_row = target_perm[target_dev, bucket * capacity + within]
    return (target_dev * VOX_DEV + target_row).reshape(-1).astype(jnp.int32)


def shard_levels(own_key, dims, cuts, smallest, largest):
    loudness, own = 1.0, jax.random.fold_in(own_key, 6)
    for axis_at, parts in cuts:
        steps = jnp.exp(jax.random.uniform(jax.random.fold_in(own, axis_at), (parts,), jnp.float32, smallest / len(cuts), largest / len(cuts)))
        loudness = loudness * jnp.repeat(steps, dims[axis_at] // parts).reshape([-1 if axis == axis_at else 1 for axis in range(len(dims))])
    return loudness


def scatter_about(stream_key, extent, scale, limit, cuts=(), kind=jnp.bfloat16):
    values = scale * jax.random.normal(stream_key, extent, jnp.float32)
    if cuts:
        values = values * shard_levels(stream_key, extent, cuts, -0.22, 0.18)
    return jnp.clip(values, -limit, limit).astype(kind)


def setup_inputs(seed: int = 0, part: int = 0) -> dict:
    seeds = jax.random.split(jax.random.key(seed), 7)
    own_keys = jax.random.split(jax.random.fold_in(seeds[6], part), 7)
    return {
        "voxels": scatter_about(own_keys[0], (VOXELS, C), 1.0, 6.0, ((0, 16),)),
        "counts": draw_counts(jax.random.fold_in(jax.random.fold_in(seeds[6], part), 71), part),
        "neighbours": draw_neighbours(jax.random.fold_in(jax.random.fold_in(seeds[6], part), 71), part),
        "conv_weight": scatter_about(seeds[3], (2, OFFSETS, C, C), (OFFSETS * C) ** -0.5, 0.109375),
        "linear_weight": scatter_about(seeds[4], (2, C, C), C ** -0.5, 0.5),
        "destination": draw_destination(jax.random.fold_in(jax.random.fold_in(seeds[6], part), 71), part),
    }


def reference(voxels, counts, neighbours, conv_weight, linear_weight, destination):
    row_ids = jnp.arange(VOXELS, dtype=jnp.int32)
    live = row_ids % VOX_DEV < counts[row_ids // VOX_DEV]
    features = jnp.where(live[:, None], voxels, jnp.zeros_like(voxels))
    for layer_index in range(2):
        current = features

        def offset_term(running, pieces):
            targets, weight = pieces
            present = targets >= 0
            picked = current[jnp.where(present, targets, 0)]
            picked = jnp.where(present[:, None], picked, jnp.zeros_like(picked))
            return (running + jnp.dot(picked, weight, preferred_element_type=jnp.float32), None)
        start = jnp.zeros((VOXELS, C), jnp.float32)
        convolved, _ = lax.scan(offset_term, start, (neighbours, conv_weight[layer_index]))
        convolved = convolved.astype(jnp.bfloat16)
        projected = jnp.dot(convolved, linear_weight[layer_index], preferred_element_type=jnp.float32)
        average = lax.optimization_barrier(jnp.mean(projected, axis=1, keepdims=True))
        centred = projected - average
        spread = lax.optimization_barrier(jnp.mean(centred * centred, axis=1, keepdims=True))
        normed = centred / jnp.sqrt(spread + 1e-05)
        summed = current.astype(jnp.float32) + normed
        features = jnp.where(live[:, None], summed, jnp.zeros_like(summed)).astype(jnp.bfloat16)
    serial = jnp.zeros((VOXELS, C), jnp.bfloat16).at[destination].set(features)
    return serial
```

```python
import functools

import jax
import jax.numpy as jnp
from jax import lax
from jax.experimental import pallas as pl
from jax.experimental.pallas import tpu as pltpu
from jax.sharding import PartitionSpec as P

HALO = 128
BLOCK = 256
WINDOW = 512
BF16 = jnp.bfloat16
F32 = jnp.float32
ABSENT = 256
SMEM = pltpu.SMEM
VMEM = pltpu.VMEM


def params():
    return pltpu.CompilerParams(vmem_limit_bytes=48 * 1024 * 1024)


def selector(row, depth):
    shape = (depth, row.shape[1])
    places = lax.broadcasted_iota(jnp.int16, shape, 0)
    wanted = jnp.broadcast_to(row.astype(jnp.int16), shape)
    return jnp.where(places == wanted, BF16(1), BF16(0))


def dot(a, b):
    return jnp.dot(a, b, preferred_element_type=F32)


def live_lanes(first, width, rows, before, own, after):
    at = first + lax.broadcasted_iota(jnp.int32, (1, width), 1)
    limit = jnp.where(at < 0, before - rows, jnp.where(at < rows, own, after + rows))
    return at < limit


def layer_block(window, targets, weight, linear, live, picked):
    offsets = targets.shape[0]
    channels = linear.shape[0]
    static = {0: 0, offsets // 2: HALO, offsets - 1: 2 * HALO}
    for k in range(offsets):
        if k in static:
            got = window(static[k], BLOCK)
        else:
            got = dot(window(0, WINDOW), selector(targets[k : k + 1, :], WINDOW)).astype(BF16)
        picked[k * channels : (k + 1) * channels, :] = got
    convolved = dot(weight, picked[...]).astype(BF16)
    projected = dot(linear, convolved)
    average = jnp.mean(projected, axis=0, keepdims=True)
    centred = projected - average
    spread = jnp.mean(centred * centred, axis=0, keepdims=True)
    summed = window(HALO, BLOCK).astype(F32) + centred * lax.rsqrt(spread + 1e-05)
    return jnp.where(live, summed, 0.0).astype(BF16)


def turn_weights(weight_ref, turned):
    offsets, channels = weight_ref.shape[1], weight_ref.shape[2]
    for k in range(offsets):
        turned[:, k * channels : (k + 1) * channels] = weight_ref[0, k].T


def device_counts(place_ref, counts_ref):
    own = place_ref[0]
    last = counts_ref.shape[0] - 1
    before = jnp.where(own > 0, counts_ref[jnp.maximum(own - 1, 0)], 0)
    after = jnp.where(own < last, counts_ref[jnp.minimum(own + 1, last)], 0)
    return own, before, counts_ref[own], after


def slots_body(destination_ref, perm_ref, target_ref, shards):
    rows = destination_ref.shape[1]
    capacity = rows // shards
    lanes = 128
    groups = rows // lanes
    tile = 256
    earlier = (
        lax.broadcasted_iota(jnp.int32, (tile, tile), 0) < lax.broadcasted_iota(jnp.int32, (tile, tile), 1)
    ).astype(F32).astype(BF16)
    ones = jnp.ones((tile, tile), BF16)
    devices = lax.broadcasted_iota(jnp.int32, (shards, tile), 0)
    before = (devices * capacity).astype(F32)
    total = jnp.zeros((4 * groups, lanes), F32)
    for c in range(rows // tile):
        goal = destination_ref[:, c * tile : (c + 1) * tile]
        device = goal >> (rows.bit_length() - 1)
        place = goal & (rows - 1)
        member = (jnp.broadcast_to(device, (shards, tile)) == devices).astype(F32)
        member16 = member.astype(BF16)
        slot = jnp.sum(member * (dot(member16, earlier) + before), axis=0, keepdims=True).astype(jnp.int32)
        before = before + dot(member16, ones)
        row = c * tile + lax.broadcasted_iota(jnp.int32, (1, tile), 1)
        total = total + scatter_term(slot, (row, place), groups)
    perm_ref[...] = joined(total, 0, groups)
    target_ref[...] = joined(total, 1, groups)


def scatter_term(at, values, groups):
    tile = at.shape[1]
    high = (lax.broadcasted_iota(jnp.int32, (groups, tile), 0) == jnp.broadcast_to(at >> 7, (groups, tile))).astype(F32)
    low = (lax.broadcasted_iota(jnp.int32, (128, tile), 0) == jnp.broadcast_to(at & 127, (128, tile))).astype(F32)
    parts = []
    for value in values:
        parts.append(high * (value >> 6).astype(F32))
        parts.append(high * (value & 63).astype(F32))
    left = jnp.concatenate(parts, axis=0).astype(BF16)
    return lax.dot_general(left, low.astype(BF16), (((1,), (1,)), ((), ())), preferred_element_type=F32)


def joined(total, n, groups):
    high = total[2 * n * groups : (2 * n + 1) * groups, :]
    low = total[(2 * n + 1) * groups : (2 * n + 2) * groups, :]
    return (high * 64.0 + low).astype(jnp.int32)


def inner_kernel(
    shards, place_ref, counts_ref, voxels_ref, near_ref, weight_ref, linear_ref, destination_ref,
    act_ref, next_ref, perm_ref, target_ref, turned, picked,
):
    rows, channels = voxels_ref.shape
    own, before, count, after = device_counts(place_ref, counts_ref)
    slots_body(destination_ref, perm_ref, target_ref, shards)
    turn_weights(weight_ref, turned)
    for c in range(rows // BLOCK):
        live = live_lanes(c * BLOCK, BLOCK, rows, before, count, after)
        block = voxels_ref[c * BLOCK : (c + 1) * BLOCK, :].T
        act_ref[:, c * BLOCK : (c + 1) * BLOCK] = jnp.where(live, block.astype(F32), 0.0).astype(BF16)
    linear = linear_ref[0].T

    def step(b, _):
        first = pl.multiple_of(b * BLOCK, BLOCK)
        middle = pl.multiple_of(first + HALO, HALO)
        targets = jnp.maximum(near_ref[:, pl.ds(middle, BLOCK)] - (own * rows + first), -1)
        window = lambda at, n: act_ref[:, pl.ds(pl.multiple_of(first + at, HALO), n)]
        live = live_lanes(middle, BLOCK, rows, before, count, after)
        next_ref[:, pl.ds(first, BLOCK)] = layer_block(window, targets, turned[...], linear, live, picked)
        return 0

    lax.fori_loop(0, rows // BLOCK - 1, step, 0)


def outer_kernel(
    place_ref, counts_ref, low_ref, high_ref, act_ref, inner_ref, near_ref, weight0_ref, weight1_ref, linear_ref,
    perm_ref, send_ref, turned, picked, edge, padded, last,
):
    channels, rows = act_ref.shape
    own, before, count, after = device_counts(place_ref, counts_ref)
    extent = 2 * HALO
    turn_weights(weight0_ref, turned)
    linear = linear_ref[0].T
    lanes = lax.broadcasted_iota(jnp.int32, (1, HALO), 1)

    def reached(halo_ref, base):
        relative = halo_ref[extent : extent + near_ref.shape[0], :].astype(F32).astype(jnp.int32)
        return jnp.where(relative == ABSENT, -1, relative + lanes + base)

    def masked(halo_ref, first):
        live = live_lanes(first, extent, rows, before, count, after)
        return jnp.where(live, halo_ref[0:extent, :].T.astype(F32), 0.0).astype(BF16)

    window = lambda at, n: edge[:, at : at + n]

    edge[:, 0:extent] = masked(low_ref, -extent)
    edge[:, extent:] = act_ref[:, 0:extent]
    targets = jnp.concatenate(
        [reached(low_ref, HALO), jnp.maximum(near_ref[:, 0:HALO] - own * rows + extent, -1)], axis=1
    )
    live = live_lanes(-HALO, BLOCK, rows, before, count, after)
    padded[:, 0:BLOCK] = layer_block(window, targets, turned[...], linear, live, picked)

    edge[:, 0:extent] = act_ref[:, rows - extent : rows]
    edge[:, extent:] = masked(high_ref, rows)
    targets = jnp.concatenate(
        [jnp.maximum(near_ref[:, rows - HALO : rows] - own * rows - (rows - extent), -1), reached(high_ref, 2 * HALO)],
        axis=1,
    )
    live = live_lanes(rows - HALO, BLOCK, rows, before, count, after)
    padded[:, rows : rows + BLOCK] = layer_block(window, targets, turned[...], linear, live, picked)
    padded[:, BLOCK:rows] = inner_ref[...]

    turn_weights(weight1_ref, turned)
    linear = linear_ref[1].T

    def step(b, _):
        first = pl.multiple_of(b * BLOCK, BLOCK)
        targets = jnp.maximum(near_ref[:, pl.ds(first, BLOCK)] - (own * rows + first - HALO), -1)
        window = lambda at, n: padded[:, pl.ds(pl.multiple_of(first + at, HALO), n)]
        live = live_lanes(first, BLOCK, rows, before, count, after)
        last[:, pl.ds(first, BLOCK)] = layer_block(window, targets, turned[...], linear, live, picked)
        return 0

    lax.fori_loop(0, rows // BLOCK, step, 0)
    reorder(last, perm_ref, send_ref)


def reorder(source, from_ref, out_ref):
    channels, rows = source.shape

    def step(b, _):
        pair = from_ref[pl.ds(b * 2, 2), :]
        wanted = jnp.concatenate([pair[0:1, :], pair[1:2, :]], axis=1)
        total = jnp.zeros((channels, BLOCK), F32)
        for w in range(rows // WINDOW):
            total = total + dot(source[:, w * WINDOW : (w + 1) * WINDOW], selector(wanted - w * WINDOW, WINDOW))
        out_ref[pl.ds(pl.multiple_of(b * BLOCK, BLOCK), BLOCK), :] = total.astype(BF16).T
        return 0

    lax.fori_loop(0, rows // BLOCK, step, 0)


def inverse_kernel(places_ref, from_ref):
    groups = places_ref.shape[0]
    total = jnp.zeros((2 * groups, 128), F32)
    lanes = lax.broadcasted_iota(jnp.int32, (1, 128), 1)
    for g in range(groups):
        total = total + scatter_term(places_ref[g : g + 1, :], (g * 128 + lanes,), groups)
    from_ref[...] = joined(total, 0, groups)


def final_kernel(from_ref, got_ref, out_ref, turned):
    rows = got_ref.shape[0]
    for c in range(rows // BLOCK):
        turned[:, c * BLOCK : (c + 1) * BLOCK] = got_ref[c * BLOCK : (c + 1) * BLOCK, :].T
    reorder(turned, from_ref, out_ref)


def local(voxels, counts, neighbours, conv_weight, linear_weight, destination):
    rows, channels = voxels.shape
    offsets = neighbours.shape[0]
    both = ("wide", "narrow")
    shards = lax.axis_size(both)
    own = lax.axis_index(both)
    place = jnp.reshape(own, (1,)).astype(jnp.int32)
    extent = 2 * HALO
    struct = jax.ShapeDtypeStruct
    vmem = pl.BlockSpec(memory_space=VMEM)
    smem = pl.BlockSpec(memory_space=SMEM)

    def packed(first_voxel, first_near):
        near = lax.slice_in_dim(neighbours, first_near, first_near + HALO, axis=1)
        ids = own * rows + first_near + jnp.arange(HALO, dtype=jnp.int32)[None, :]
        relative = jnp.where(near >= 0, near - ids, ABSENT).astype(BF16)
        pad = jnp.zeros((32 - offsets, channels), BF16)
        return jnp.concatenate(
            [lax.slice_in_dim(voxels, first_voxel, first_voxel + extent, axis=0), relative, pad], axis=0
        )

    forward = [(i, i + 1) for i in range(shards - 1)]
    backward = [(target, source) for source, target in forward]
    low = lax.ppermute(packed(rows - extent, rows - HALO), both, forward)
    high = lax.ppermute(packed(0, 0), both, backward)

    def weight_spec(layer):
        return pl.BlockSpec((1,) + conv_weight.shape[1:], lambda i: (layer, 0, 0, 0))

    whole = lambda shape: pl.BlockSpec(shape, lambda i: (0,) * len(shape))
    act, inner, perm, target = pl.pallas_call(
        functools.partial(inner_kernel, shards),
        grid=(1,),
        out_shape=(
            struct((channels, rows), BF16),
            struct((channels, rows - BLOCK), BF16),
            struct((rows // 128, 128), jnp.int32),
            struct((rows // 128, 128), jnp.int32),
        ),
        in_specs=[
            smem, smem, whole(voxels.shape), whole(neighbours.shape), weight_spec(0), whole(linear_weight.shape),
            whole((1, rows)),
        ],
        out_specs=(
            whole((channels, rows)), whole((channels, rows - BLOCK)), whole((rows // 128, 128)), whole((rows // 128, 128)),
        ),
        scratch_shapes=[VMEM((channels, offsets * channels), BF16), VMEM((offsets * channels, BLOCK), BF16)],
        compiler_params=params(),
        cost_estimate=pl.CostEstimate(flops=20_000_000_000, bytes_accessed=6_000_000, transcendentals=0),
        name="first_layer",
    )(place, counts, voxels, neighbours, conv_weight, linear_weight, destination.reshape(1, rows))

    targets = lax.all_gather(target, both, axis=0, tiled=False)

    send = pl.pallas_call(
        outer_kernel,
        grid=(1,),
        out_shape=struct((rows, channels), BF16),
        in_specs=[
            smem, smem, whole(low.shape), whole(high.shape), whole((channels, rows)), whole((channels, rows - BLOCK)),
            whole(neighbours.shape), weight_spec(0), weight_spec(1), whole(linear_weight.shape),
            whole((rows // 128, 128)),
        ],
        out_specs=whole((rows, channels)),
        scratch_shapes=[
            VMEM((channels, offsets * channels), BF16),
            VMEM((offsets * channels, BLOCK), BF16),
            VMEM((channels, WINDOW), BF16),
            VMEM((channels, rows + 2 * HALO), BF16),
            VMEM((channels, rows), BF16),
        ],
        compiler_params=params(),
        cost_estimate=pl.CostEstimate(flops=30_000_000_000, bytes_accessed=8_000_000, transcendentals=0),
        name="second_layer",
    )(place, counts, low, high, act, inner, neighbours, conv_weight, conv_weight, linear_weight, perm)

    got = lax.all_to_all(
        send.reshape(shards, rows // shards, channels), both, split_axis=0, concat_axis=0, tiled=True
    ).reshape(rows, channels)

    per_device = rows // shards // 128
    mine = lax.dynamic_slice_in_dim(targets, own * per_device, per_device, axis=1).reshape(rows // 128, 128)
    source = pl.pallas_call(
        inverse_kernel,
        out_shape=struct((rows // 128, 128), jnp.int32),
        in_specs=[vmem],
        out_specs=vmem,
        compiler_params=params(),
        name="sources",
    )(mine)
    return pl.pallas_call(
        final_kernel,
        out_shape=struct((rows, channels), BF16),
        in_specs=[vmem, vmem],
        out_specs=vmem,
        scratch_shapes=[VMEM((channels, rows), BF16)],
        compiler_params=params(),
        name="hilbert_order",
    )(source, got)


def solution(mesh):
    in_specs = (
        P(("groups", "wide", "narrow"), None),
        P("groups"),
        P(None, ("groups", "wide", "narrow")),
        P(),
        P(),
        P(("groups", "wide", "narrow")),
    )
    out_specs = P(("groups", "wide", "narrow"), None)
    return jax.shard_map(local, mesh=mesh, in_specs=in_specs, out_specs=out_specs, check_vma=False)
```

```python
import functools

import jax
import jax.numpy as jnp
from jax import lax
from jax.experimental import pallas as pl
from jax.experimental.pallas import tpu as pltpu
from jax.sharding import PartitionSpec as P

HALO = 128
BLOCK = 256
WINDOW = 512
BF16 = jnp.bfloat16
F32 = jnp.float32
ABSENT = 256
SMEM = pltpu.SMEM
VMEM = pltpu.VMEM


def params():
    return pltpu.CompilerParams(vmem_limit_bytes=48 * 1024 * 1024)


def selector(row, depth):
    shape = (depth, row.shape[1])
    places = lax.broadcasted_iota(jnp.int16, shape, 0)
    wanted = jnp.broadcast_to(row.astype(jnp.int16), shape)
    return jnp.where(places == wanted, BF16(1), BF16(0))


def dot(a, b):
    return jnp.dot(a, b, preferred_element_type=F32)


def live_lanes(first, width, rows, before, own, after):
    at = first + lax.broadcasted_iota(jnp.int32, (1, width), 1)
    limit = jnp.where(at < 0, before - rows, jnp.where(at < rows, own, after + rows))
    return at < limit


def lane_pick(block, lanes):
    numbers = lax.GatherDimensionNumbers(
        offset_dims=(), collapsed_slice_dims=(1,), start_index_map=(1,),
        operand_batching_dims=(0,), start_indices_batching_dims=(0,),
    )
    index = jnp.broadcast_to(lanes.astype(jnp.int16), block.shape)
    return lax.gather(block, index[..., None], numbers, (1, 1), mode=lax.GatherScatterMode.PROMISE_IN_BOUNDS)


def gather_block(window, targets, picked):
    offsets = targets.shape[0]
    channels = picked.shape[0] // offsets
    static = {0: 0, offsets // 2: HALO, offsets - 1: 2 * HALO}
    turn = 0
    for k in range(offsets):
        at = slice(k * channels, (k + 1) * channels)
        if k in static:
            picked[at, :] = window(static[k], BLOCK)
            continue
        turn += 1
        row = targets[k : k + 1, :]
        if turn % 2:
            picked[at, :] = dot(window(0, WINDOW), selector(row, WINDOW)).astype(BF16)
            continue
        for half in range(2):
            part = row[:, half * HALO : (half + 1) * HALO]
            lanes = part & (HALO - 1)
            chunk = jnp.broadcast_to((part >> 7).astype(jnp.int16), (channels, HALO))
            total = jnp.zeros((channels, HALO), BF16)
            for j in range(half, half + 3):
                total = jnp.where(chunk == j, lane_pick(window(j * HALO, HALO), lanes), total)
            picked[at, half * HALO : (half + 1) * HALO] = total


def finish_block(current, weight, linear, live, picked):
    convolved = dot(weight, picked[...]).astype(BF16)
    projected = dot(linear, convolved)
    average = jnp.mean(projected, axis=0, keepdims=True)
    centred = projected - average
    spread = jnp.mean(centred * centred, axis=0, keepdims=True)
    summed = current.astype(F32) + centred * lax.rsqrt(spread + 1e-05)
    return jnp.where(live, summed, 0.0).astype(BF16)


def turn_weights(weight_ref, turned):
    offsets, channels = weight_ref.shape[1], weight_ref.shape[2]
    for k in range(offsets):
        turned[:, k * channels : (k + 1) * channels] = weight_ref[0, k].T


def device_counts(place_ref, counts_ref):
    own = place_ref[0]
    last = counts_ref.shape[0] - 1
    before = jnp.where(own > 0, counts_ref[jnp.maximum(own - 1, 0)], 0)
    after = jnp.where(own < last, counts_ref[jnp.minimum(own + 1, last)], 0)
    return own, before, counts_ref[own], after


def slots_body(destination_ref, perm_ref, high_ref, low_ref, shards):
    rows = destination_ref.shape[1]
    capacity = rows // shards
    lanes = 128
    groups = rows // lanes
    tile = 256
    earlier = (
        lax.broadcasted_iota(jnp.int32, (tile, tile), 0) < lax.broadcasted_iota(jnp.int32, (tile, tile), 1)
    ).astype(F32).astype(BF16)
    ones = jnp.ones((tile, tile), BF16)
    devices = lax.broadcasted_iota(jnp.int32, (shards, tile), 0)
    before = (devices * capacity).astype(F32)
    total = jnp.zeros((4 * groups, lanes), F32)
    for c in range(rows // tile):
        goal = destination_ref[:, c * tile : (c + 1) * tile]
        device = goal >> (rows.bit_length() - 1)
        place = goal & (rows - 1)
        member = (jnp.broadcast_to(device, (shards, tile)) == devices).astype(F32)
        member16 = member.astype(BF16)
        slot = jnp.sum(member * (dot(member16, earlier) + before), axis=0, keepdims=True).astype(jnp.int32)
        before = before + dot(member16, ones)
        row = c * tile + lax.broadcasted_iota(jnp.int32, (1, tile), 1)
        total = total + scatter_term(slot, (row, place), groups)
    perm_ref[...] = joined(total, 0, groups)
    high_ref[...] = total[2 * groups : 3 * groups, :]
    low_ref[...] = total[3 * groups :, :]


def scatter_term(at, values, groups):
    tile = at.shape[1]
    high = (lax.broadcasted_iota(jnp.int32, (groups, tile), 0) == jnp.broadcast_to(at >> 7, (groups, tile))).astype(F32)
    low = (lax.broadcasted_iota(jnp.int32, (128, tile), 0) == jnp.broadcast_to(at & 127, (128, tile))).astype(F32)
    parts = []
    for value in values:
        parts.append(high * (value >> 6).astype(F32))
        parts.append(high * (value & 63).astype(F32))
    left = jnp.concatenate(parts, axis=0).astype(BF16)
    return lax.dot_general(left, low.astype(BF16), (((1,), (1,)), ((), ())), preferred_element_type=F32)


def joined(total, n, groups):
    high = total[2 * n * groups : (2 * n + 1) * groups, :]
    low = total[(2 * n + 1) * groups : (2 * n + 2) * groups, :]
    return (high * 64.0 + low).astype(jnp.int32)


def inner_kernel(
    shards, place_ref, counts_ref, voxels_ref, near_ref, weight_ref, linear_ref, destination_ref,
    act_ref, next_ref, perm_ref, high_ref, low_ref, turned, even, odd,
):
    rows, channels = voxels_ref.shape
    own, before, count, after = device_counts(place_ref, counts_ref)
    slots_body(destination_ref, perm_ref, high_ref, low_ref, shards)
    turn_weights(weight_ref, turned)
    for c in range(rows // BLOCK):
        live = live_lanes(c * BLOCK, BLOCK, rows, before, count, after)
        block = voxels_ref[c * BLOCK : (c + 1) * BLOCK, :].T
        act_ref[:, c * BLOCK : (c + 1) * BLOCK] = jnp.where(live, block.astype(F32), 0.0).astype(BF16)
    linear = linear_ref[0].T

    def gather(b, picked):
        first = pl.multiple_of((b - 1) * BLOCK, BLOCK)
        targets = jnp.maximum(near_ref[:, pl.ds(pl.multiple_of(first + HALO, HALO), BLOCK)] - (own * rows + first), -1)
        gather_block(lambda at, n: act_ref[:, pl.ds(pl.multiple_of(first + at, HALO), n)], targets, picked)

    def finish(b, picked):
        first = b * BLOCK - HALO
        current = act_ref[:, pl.ds(pl.multiple_of(jnp.maximum(first, 0), HALO), BLOCK)]
        live = live_lanes(first, BLOCK, rows, before, count, after)
        next_ref[:, pl.ds(pl.multiple_of(b * BLOCK, BLOCK), BLOCK)] = finish_block(
            current, turned[...], linear, live, picked
        )

    blocks = rows // BLOCK
    odd[...] = jnp.zeros_like(odd)

    def step(t, _):
        gather(2 * t + 1, even)
        finish(2 * t, odd)
        gather(2 * t + 2, odd)
        finish(2 * t + 1, even)
        return 0

    lax.fori_loop(0, (blocks - 2) // 2, step, 0)
    gather(blocks - 1, even)
    finish(blocks - 2, odd)
    finish(blocks - 1, even)


def outer_kernel(
    place_ref, counts_ref, low_ref, high_ref, act_ref, inner_ref, near_ref, weight0_ref, weight1_ref, linear_ref,
    perm_ref, place_high_ref, place_low_ref, send_ref, turned, even, odd, edge, padded, last,
):
    channels, rows = act_ref.shape
    own, before, count, after = device_counts(place_ref, counts_ref)
    extent = 2 * HALO
    turn_weights(weight0_ref, turned)
    linear = linear_ref[0].T
    lanes = lax.broadcasted_iota(jnp.int32, (1, HALO), 1)

    def reached(halo_ref, base):
        relative = halo_ref[extent : extent + near_ref.shape[0], :].astype(F32).astype(jnp.int32)
        return jnp.where(relative == ABSENT, -1, relative + lanes + base)

    def masked(halo_ref, first):
        live = live_lanes(first, extent, rows, before, count, after)
        return jnp.where(live, halo_ref[0:extent, :].T.astype(F32), 0.0).astype(BF16)

    edges = (edge.at[:, 0:WINDOW], edge.at[:, WINDOW:])
    edges[0][:, 0:extent] = masked(low_ref, -extent)
    edges[0][:, extent:] = act_ref[:, 0:extent]
    edges[1][:, 0:extent] = act_ref[:, rows - extent : rows]
    edges[1][:, extent:] = masked(high_ref, rows)
    near = (
        jnp.concatenate(
            [reached(low_ref, HALO), jnp.maximum(near_ref[:, 0:HALO] - own * rows + extent, -1)], axis=1
        ),
        jnp.concatenate(
            [
                jnp.maximum(near_ref[:, rows - HALO : rows] - own * rows - (rows - extent), -1),
                reached(high_ref, 2 * HALO),
            ],
            axis=1,
        ),
    )
    picks = (even, odd)
    for n in range(2):
        gather_block(lambda at, size: edges[n][:, at : at + size], near[n], picks[n])
    for n in range(2):
        at = n * rows
        live = live_lanes(at - HALO, BLOCK, rows, before, count, after)
        padded[:, at : at + BLOCK] = finish_block(
            edges[n][:, HALO : HALO + BLOCK], turned[...], linear, live, picks[n]
        )
    padded[:, BLOCK:rows] = inner_ref[:, BLOCK:rows]

    turn_weights(weight1_ref, turned)
    linear = linear_ref[1].T

    def gather(b, picked):
        first = pl.multiple_of(b * BLOCK, BLOCK)
        targets = jnp.maximum(near_ref[:, pl.ds(first, BLOCK)] - (own * rows + first - HALO), -1)
        gather_block(lambda at, n: padded[:, pl.ds(pl.multiple_of(first + at, HALO), n)], targets, picked)

    def finish(b, picked):
        first = b * BLOCK
        current = padded[:, pl.ds(pl.multiple_of(jnp.maximum(first, 0) + HALO, HALO), BLOCK)]
        live = live_lanes(first, BLOCK, rows, before, count, after)
        last[:, pl.ds(pl.multiple_of(first + BLOCK, BLOCK), BLOCK)] = finish_block(
            current, turned[...], linear, live, picked
        )

    def step(t, _):
        gather(2 * t, even)
        finish(2 * t - 1, odd)
        gather(2 * t + 1, odd)
        finish(2 * t, even)
        return 0

    lax.fori_loop(0, rows // BLOCK // 2, step, 0)
    finish(rows // BLOCK - 1, odd)

    shards, depth, _ = send_ref.shape
    capacity = rows // shards
    pieces = BLOCK // capacity

    def store(b, block):
        for p in range(pieces):
            send_ref[b * pieces + p, 0:capacity, :] = block[p * capacity : (p + 1) * capacity, :]

    reorder(last.at[:, BLOCK:], perm_ref, store)
    held = capacity // 128
    pad = jnp.zeros((depth - capacity - 2 * held, 128), F32)
    for d in range(shards):
        at = slice(d * held, (d + 1) * held)
        extra = jnp.concatenate([place_high_ref[at, :], place_low_ref[at, :], pad], axis=0)
        send_ref[d, capacity:, :] = extra.astype(BF16)


def reorder(source, from_ref, store):
    channels, rows = source.shape
    unroll = 4

    def one(b):
        pair = from_ref[pl.ds(b * 2, 2), :]
        wanted = jnp.concatenate([pair[0:1, :], pair[1:2, :]], axis=1)
        total = jnp.zeros((channels, BLOCK), F32)
        for w in range(rows // WINDOW):
            total = total + dot(source[:, w * WINDOW : (w + 1) * WINDOW], selector(wanted - w * WINDOW, WINDOW))
        store(b, total.astype(BF16).T)

    def step(t, _):
        for u in range(unroll):
            one(t * unroll + u)
        return 0

    lax.fori_loop(0, rows // BLOCK // unroll, step, 0)


def final_kernel(got_ref, out_ref, turned, from_ref):
    rows = out_ref.shape[0]
    shards = got_ref.shape[0]
    groups = rows // 128
    capacity = rows // shards
    held = capacity // 128
    lanes = lax.broadcasted_iota(jnp.int32, (1, 128), 1)
    total = jnp.zeros((2 * groups, 128), F32)
    for s in range(shards):
        turned[:, s * capacity : (s + 1) * capacity] = got_ref[s, 0:capacity, :].T
        extra = got_ref[s, capacity:, :].astype(F32)
        place = (extra[0:held, :] * 64.0 + extra[held : 2 * held, :]).astype(jnp.int32)
        for h in range(held):
            total = total + scatter_term(place[h : h + 1, :], (s * capacity + h * 128 + lanes,), groups)
    from_ref[...] = joined(total, 0, groups)

    def store(b, block):
        out_ref[pl.ds(pl.multiple_of(b * BLOCK, BLOCK), BLOCK), :] = block

    reorder(turned, from_ref, store)


def local(voxels, counts, neighbours, conv_weight, linear_weight, destination):
    rows, channels = voxels.shape
    offsets = neighbours.shape[0]
    both = ("wide", "narrow")
    shards = lax.axis_size(both)
    own = lax.axis_index(both)
    place = jnp.reshape(own, (1,)).astype(jnp.int32)
    extent = 2 * HALO
    struct = jax.ShapeDtypeStruct
    vmem = pl.BlockSpec(memory_space=VMEM)
    smem = pl.BlockSpec(memory_space=SMEM)

    def packed(first_voxel, first_near):
        near = lax.slice_in_dim(neighbours, first_near, first_near + HALO, axis=1)
        ids = own * rows + first_near + jnp.arange(HALO, dtype=jnp.int32)[None, :]
        relative = jnp.where(near >= 0, near - ids, ABSENT).astype(BF16)
        pad = jnp.zeros((32 - offsets, channels), BF16)
        return jnp.concatenate(
            [lax.slice_in_dim(voxels, first_voxel, first_voxel + extent, axis=0), relative, pad], axis=0
        )

    forward = [(i, i + 1) for i in range(shards - 1)]
    backward = [(target, source) for source, target in forward]
    low = lax.ppermute(packed(rows - extent, rows - HALO), both, forward)
    high = lax.ppermute(packed(0, 0), both, backward)

    def weight_spec(layer):
        return pl.BlockSpec((1,) + conv_weight.shape[1:], lambda i: (layer, 0, 0, 0))

    whole = lambda shape: pl.BlockSpec(shape, lambda i: (0,) * len(shape))
    table = (rows // 128, 128)
    padded = (channels, rows + BLOCK)
    picked = VMEM((offsets * channels, BLOCK), BF16)
    turned = VMEM((channels, offsets * channels), BF16)
    act, inner, perm, place_high, place_low = pl.pallas_call(
        functools.partial(inner_kernel, shards),
        grid=(1,),
        out_shape=(
            struct((channels, rows), BF16), struct(padded, BF16), struct(table, jnp.int32), struct(table, F32),
            struct(table, F32),
        ),
        in_specs=[
            smem, smem, whole(voxels.shape), whole(neighbours.shape), weight_spec(0), whole(linear_weight.shape),
            whole((1, rows)),
        ],
        out_specs=(whole((channels, rows)), whole(padded), whole(table), whole(table), whole(table)),
        scratch_shapes=[turned, picked, picked],
        compiler_params=params(),
        cost_estimate=pl.CostEstimate(flops=20_000_000_000, bytes_accessed=6_000_000, transcendentals=0),
        name="first_layer",
    )(place, counts, voxels, neighbours, conv_weight, linear_weight, destination.reshape(1, rows))

    depth = rows // shards + 16
    send = pl.pallas_call(
        outer_kernel,
        grid=(1,),
        out_shape=struct((shards, depth, channels), BF16),
        in_specs=[
            smem, smem, whole(low.shape), whole(high.shape), whole((channels, rows)), whole(padded),
            whole(neighbours.shape), weight_spec(0), weight_spec(1), whole(linear_weight.shape),
            whole(table), whole(table), whole(table),
        ],
        out_specs=whole((shards, depth, channels)),
        scratch_shapes=[
            turned,
            picked,
            picked,
            VMEM((channels, 2 * WINDOW), BF16),
            VMEM(padded, BF16),
            VMEM(padded, BF16),
        ],
        compiler_params=params(),
        cost_estimate=pl.CostEstimate(flops=30_000_000_000, bytes_accessed=8_000_000, transcendentals=0),
        name="second_layer",
    )(
        place, counts, low, high, act, inner, neighbours, conv_weight, conv_weight, linear_weight, perm, place_high,
        place_low,
    )

    got = lax.all_to_all(send, both, split_axis=0, concat_axis=0, tiled=True)
    return pl.pallas_call(
        final_kernel,
        out_shape=struct((rows, channels), BF16),
        in_specs=[vmem],
        out_specs=vmem,
        scratch_shapes=[VMEM((channels, rows), BF16), VMEM(table, jnp.int32)],
        compiler_params=params(),
        name="hilbert_order",
    )(got)


def solution(mesh):
    in_specs = (
        P(("groups", "wide", "narrow"), None),
        P("groups"),
        P(None, ("groups", "wide", "narrow")),
        P(),
        P(),
        P(("groups", "wide", "narrow")),
    )
    out_specs = P(("groups", "wide", "narrow"), None)
    return jax.shard_map(local, mesh=mesh, in_specs=in_specs, out_specs=out_specs, check_vma=False)
```

```python
import functools

import jax
import jax.numpy as jnp
from jax import lax
from jax.experimental import pallas as pl
from jax.experimental.pallas import tpu as pltpu
from jax.sharding import PartitionSpec as P

HALO = 128
BLOCK = 256
WINDOW = 512
BF16 = jnp.bfloat16
F32 = jnp.float32
ABSENT = 256
SMEM = pltpu.SMEM
VMEM = pltpu.VMEM


def params():
    return pltpu.CompilerParams(vmem_limit_bytes=48 * 1024 * 1024)


def selector(row, depth):
    shape = (depth, row.shape[1])
    places = lax.broadcasted_iota(jnp.int16, shape, 0)
    wanted = jnp.broadcast_to(row.astype(jnp.int16), shape)
    return jnp.where(places == wanted, BF16(1), BF16(0))


def dot(a, b):
    return jnp.dot(a, b, preferred_element_type=F32)


def live_lanes(first, width, rows, before, own, after):
    at = first + lax.broadcasted_iota(jnp.int32, (1, width), 1)
    limit = jnp.where(at < 0, before - rows, jnp.where(at < rows, own, after + rows))
    return at < limit


def lane_pick(block, lanes):
    numbers = lax.GatherDimensionNumbers(
        offset_dims=(), collapsed_slice_dims=(1,), start_index_map=(1,),
        operand_batching_dims=(0,), start_indices_batching_dims=(0,),
    )
    index = jnp.broadcast_to(lanes.astype(jnp.int16), block.shape)
    return lax.gather(block, index[..., None], numbers, (1, 1), mode=lax.GatherScatterMode.PROMISE_IN_BOUNDS)


def gather_block(window, targets, picked):
    offsets = targets.shape[0]
    channels = picked.shape[0] // offsets
    static = {0: 0, offsets // 2: HALO, offsets - 1: 2 * HALO}
    turn = 0
    for k in range(offsets):
        at = slice(k * channels, (k + 1) * channels)
        if k in static:
            picked[at, :] = window(static[k], BLOCK)
            continue
        turn += 1
        row = targets[k : k + 1, :]
        if turn % 2:
            picked[at, :] = dot(window(0, WINDOW), selector(row, WINDOW)).astype(BF16)
            continue
        for half in range(2):
            part = row[:, half * HALO : (half + 1) * HALO]
            lanes = part & (HALO - 1)
            chunk = jnp.broadcast_to((part >> 7).astype(jnp.int16), (channels, HALO))
            total = jnp.zeros((channels, HALO), BF16)
            for j in range(half, half + 3):
                total = jnp.where(chunk == j, lane_pick(window(j * HALO, HALO), lanes), total)
            picked[at, half * HALO : (half + 1) * HALO] = total


def norm_block(current, convolved, linear, live):
    projected = dot(linear, convolved)
    average = jnp.mean(projected, axis=0, keepdims=True)
    centred = projected - average
    spread = jnp.mean(centred * centred, axis=0, keepdims=True)
    summed = current.astype(F32) + centred * lax.rsqrt(spread + 1e-05)
    return jnp.where(live, summed, 0.0).astype(BF16)


def columns(start):
    return pl.ds(pl.multiple_of(start, HALO), BLOCK)


def turn_weights(weight_ref, layer, turned):
    offsets, channels = weight_ref.shape[1], weight_ref.shape[2]
    for k in range(offsets):
        turned[:, k * channels : (k + 1) * channels] = weight_ref[layer, k].T


def device_counts(place_ref, counts_ref):
    own = place_ref[0]
    last = counts_ref.shape[0] - 1
    before = jnp.where(own > 0, counts_ref[jnp.maximum(own - 1, 0)], 0)
    after = jnp.where(own < last, counts_ref[jnp.minimum(own + 1, last)], 0)
    return own, before, counts_ref[own], after


def slots_body(destination_ref, perm_ref, high_ref, low_ref, shards):
    rows = destination_ref.shape[1]
    capacity = rows // shards
    lanes = 128
    groups = rows // lanes
    tile = 256
    earlier = (
        lax.broadcasted_iota(jnp.int32, (tile, tile), 0) < lax.broadcasted_iota(jnp.int32, (tile, tile), 1)
    ).astype(F32).astype(BF16)
    ones = jnp.ones((tile, tile), BF16)
    devices = lax.broadcasted_iota(jnp.int32, (shards, tile), 0)
    before = (devices * capacity).astype(F32)
    total = jnp.zeros((4 * groups, lanes), F32)
    for c in range(rows // tile):
        goal = destination_ref[:, c * tile : (c + 1) * tile]
        device = goal >> (rows.bit_length() - 1)
        place = goal & (rows - 1)
        member = (jnp.broadcast_to(device, (shards, tile)) == devices).astype(F32)
        member16 = member.astype(BF16)
        slot = jnp.sum(member * (dot(member16, earlier) + before), axis=0, keepdims=True).astype(jnp.int32)
        before = before + dot(member16, ones)
        row = c * tile + lax.broadcasted_iota(jnp.int32, (1, tile), 1)
        total = total + scatter_term(slot, (row, place), groups)
    perm_ref[...] = joined(total, 0, groups)
    high_ref[...] = total[2 * groups : 3 * groups, :]
    low_ref[...] = total[3 * groups :, :]


def scatter_term(at, values, groups):
    tile = at.shape[1]
    high = (lax.broadcasted_iota(jnp.int32, (groups, tile), 0) == jnp.broadcast_to(at >> 7, (groups, tile))).astype(F32)
    low = (lax.broadcasted_iota(jnp.int32, (128, tile), 0) == jnp.broadcast_to(at & 127, (128, tile))).astype(F32)
    parts = []
    for value in values:
        parts.append(high * (value >> 6).astype(F32))
        parts.append(high * (value & 63).astype(F32))
    left = jnp.concatenate(parts, axis=0).astype(BF16)
    return lax.dot_general(left, low.astype(BF16), (((1,), (1,)), ((), ())), preferred_element_type=F32)


def joined(total, n, groups):
    high = total[2 * n * groups : (2 * n + 1) * groups, :]
    low = total[(2 * n + 1) * groups : (2 * n + 2) * groups, :]
    return (high * 64.0 + low).astype(jnp.int32)


def inner_kernel(
    shards, place_ref, counts_ref, voxels_hbm, near_hbm, weight_hbm, linear_ref, destination_hbm,
    act_ref, next_ref, perm_ref, high_ref, low_ref, turned_ref,
    voxels_ref, near_ref, weight_ref, destination_ref, even, odd, conv, sems,
):
    copies = [
        pltpu.make_async_copy(source, target, sems.at[n])
        for n, (source, target) in enumerate(
            (
                (destination_hbm, destination_ref),
                (voxels_hbm, voxels_ref),
                (near_hbm, near_ref),
                (weight_hbm, weight_ref),
            )
        )
    ]
    for copy in copies:
        copy.start()
    rows, channels = voxels_ref.shape
    own, before, count, after = device_counts(place_ref, counts_ref)
    copies[0].wait()
    slots_body(destination_ref, perm_ref, high_ref, low_ref, shards)
    copies[1].wait()
    for c in range(rows // BLOCK):
        live = live_lanes(c * BLOCK, BLOCK, rows, before, count, after)
        block = voxels_ref[c * BLOCK : (c + 1) * BLOCK, :].T
        act_ref[:, c * BLOCK : (c + 1) * BLOCK] = jnp.where(live, block.astype(F32), 0.0).astype(BF16)
    linear = linear_ref[0].T
    copies[3].wait()
    for layer in range(2):
        turn_weights(weight_ref, layer, turned_ref.at[layer])
    copies[2].wait()

    def gather(b, picked):
        first = (b - 1) * BLOCK
        targets = jnp.maximum(near_ref[:, columns(first + HALO)] - (own * rows + first), -1)
        gather_block(lambda at, n: act_ref[:, pl.ds(pl.multiple_of(first + at, HALO), n)], targets, picked)

    def convolve(b, picked):
        conv[:, columns(b * BLOCK)] = dot(turned_ref[0], picked[...]).astype(BF16)

    blocks = rows // BLOCK

    def step(t, _):
        gather(2 * t + 1, even)
        convolve(2 * t, odd)
        gather(2 * t + 2, odd)
        convolve(2 * t + 1, even)
        return 0

    lax.fori_loop(0, (blocks - 2) // 2, step, 0)
    gather(blocks - 1, even)
    convolve(blocks - 2, odd)
    convolve(blocks - 1, even)

    def norm(b):
        first = b * BLOCK - HALO
        live = live_lanes(first, BLOCK, rows, before, count, after)
        next_ref[:, columns(b * BLOCK)] = norm_block(
            act_ref[:, columns(first)], conv[:, columns(b * BLOCK)], linear, live
        )

    in_turn(1, blocks, norm)


def in_turn(first, last, body):
    count = last - first
    unroll = max(u for u in range(1, 6) if count % u == 0)

    def step(t, _):
        for u in range(unroll):
            body(first + t * unroll + u)
        return 0

    lax.fori_loop(0, count // unroll, step, 0)


def outer_kernel(
    place_ref, counts_ref, low_ref, high_ref, act_ref, inner_ref, near_ref, turned_ref, linear_ref,
    perm_ref, place_high_ref, place_low_ref, send_ref, even, odd, edge, padded, conv, last,
):
    channels, rows = act_ref.shape
    own, before, count, after = device_counts(place_ref, counts_ref)
    extent = 2 * HALO
    linear = linear_ref[0].T
    lanes = lax.broadcasted_iota(jnp.int32, (1, HALO), 1)

    def reached(halo_ref, base):
        relative = halo_ref[extent : extent + near_ref.shape[0], :].astype(F32).astype(jnp.int32)
        return jnp.where(relative == ABSENT, -1, relative + lanes + base)

    def masked(halo_ref, first):
        live = live_lanes(first, extent, rows, before, count, after)
        return jnp.where(live, halo_ref[0:extent, :].T.astype(F32), 0.0).astype(BF16)

    edges = (edge.at[:, 0:WINDOW], edge.at[:, WINDOW:])
    edges[0][:, 0:extent] = masked(low_ref, -extent)
    edges[0][:, extent:] = act_ref[:, 0:extent]
    edges[1][:, 0:extent] = act_ref[:, rows - extent : rows]
    edges[1][:, extent:] = masked(high_ref, rows)
    near = (
        jnp.concatenate(
            [reached(low_ref, HALO), jnp.maximum(near_ref[:, 0:HALO] - own * rows + extent, -1)], axis=1
        ),
        jnp.concatenate(
            [
                jnp.maximum(near_ref[:, rows - HALO : rows] - own * rows - (rows - extent), -1),
                reached(high_ref, 2 * HALO),
            ],
            axis=1,
        ),
    )
    picks = (even, odd)
    for n in range(2):
        gather_block(lambda at, size: edges[n][:, at : at + size], near[n], picks[n])
    for n in range(2):
        conv[:, n * BLOCK : (n + 1) * BLOCK] = dot(turned_ref[0], picks[n][...]).astype(BF16)
    for n in range(2):
        at = n * rows
        live = live_lanes(at - HALO, BLOCK, rows, before, count, after)
        padded[:, at : at + BLOCK] = norm_block(
            edges[n][:, HALO : HALO + BLOCK], conv[:, n * BLOCK : (n + 1) * BLOCK], linear, live
        )
    padded[:, BLOCK:rows] = inner_ref[:, BLOCK:rows]

    linear = linear_ref[1].T

    def gather(b, picked):
        first = b * BLOCK
        targets = jnp.maximum(near_ref[:, columns(first)] - (own * rows + first - HALO), -1)
        gather_block(lambda at, n: padded[:, pl.ds(pl.multiple_of(first + at, HALO), n)], targets, picked)

    def convolve(b, picked):
        conv[:, columns((b + 1) * BLOCK)] = dot(turned_ref[1], picked[...]).astype(BF16)

    def step(t, _):
        gather(2 * t, even)
        convolve(2 * t - 1, odd)
        gather(2 * t + 1, odd)
        convolve(2 * t, even)
        return 0

    blocks = rows // BLOCK
    lax.fori_loop(0, blocks // 2, step, 0)
    convolve(blocks - 1, odd)

    def norm(b):
        first = b * BLOCK
        live = live_lanes(first, BLOCK, rows, before, count, after)
        last[:, columns(first)] = norm_block(
            padded[:, columns(first + HALO)], conv[:, columns(first + BLOCK)], linear, live
        )

    in_turn(0, blocks, norm)

    shards, depth, _ = send_ref.shape
    capacity = rows // shards
    pieces = BLOCK // capacity

    def store(b, block):
        for p in range(pieces):
            send_ref[b * pieces + p, 0:capacity, :] = block[p * capacity : (p + 1) * capacity, :]

    reorder(last, perm_ref, store)
    held = capacity // 128
    pad = jnp.zeros((depth - capacity - 2 * held, 128), F32)
    for d in range(shards):
        at = slice(d * held, (d + 1) * held)
        extra = jnp.concatenate([place_high_ref[at, :], place_low_ref[at, :], pad], axis=0)
        send_ref[d, capacity:, :] = extra.astype(BF16)


def reorder(source, from_ref, store, dots=6, unroll=8):
    channels, rows = source.shape
    windows = rows // WINDOW

    def one(b):
        pair = from_ref[pl.ds(b * 2, 2), :]
        wanted = jnp.concatenate([pair[0:1, :], pair[1:2, :]], axis=1)
        total = jnp.zeros((channels, BLOCK), F32)
        halves = [jnp.zeros((channels, 128), BF16) for _ in range(2)]
        lanes = [pair[h : h + 1, :] & 127 for h in range(2)]
        chunks = [jnp.broadcast_to((pair[h : h + 1, :] >> 7).astype(jnp.int16), (channels, 128)) for h in range(2)]
        rest = [(j, h) for j in range(dots * WINDOW // 128, rows // 128) for h in range(2)]
        done = 0
        for w in range(dots):
            total = total + dot(source[:, w * WINDOW : (w + 1) * WINDOW], selector(wanted - w * WINDOW, WINDOW))
            until = len(rest) * (w + 1) // dots
            for j, h in rest[done:until]:
                halves[h] = jnp.where(
                    chunks[h] == j, lane_pick(source[:, j * 128 : (j + 1) * 128], lanes[h]), halves[h]
                )
            done = until
        store(b, (total + jnp.concatenate(halves, axis=1).astype(F32)).astype(BF16).T)

    def step(t, _):
        for u in range(unroll):
            one(t * unroll + u)
        return 0

    lax.fori_loop(0, rows // BLOCK // unroll, step, 0)


def final_kernel(got_ref, out_ref, turned, from_ref):
    rows = out_ref.shape[0]
    shards = got_ref.shape[0]
    groups = rows // 128
    capacity = rows // shards
    held = capacity // 128
    lanes = lax.broadcasted_iota(jnp.int32, (1, 128), 1)
    total = jnp.zeros((2 * groups, 128), F32)
    for s in range(shards):
        turned[:, s * capacity : (s + 1) * capacity] = got_ref[s, 0:capacity, :].T
        extra = got_ref[s, capacity:, :].astype(F32)
        place = (extra[0:held, :] * 64.0 + extra[held : 2 * held, :]).astype(jnp.int32)
        for h in range(held):
            total = total + scatter_term(place[h : h + 1, :], (s * capacity + h * 128 + lanes,), groups)
    from_ref[...] = joined(total, 0, groups)

    def store(b, block):
        out_ref[pl.ds(pl.multiple_of(b * BLOCK, BLOCK), BLOCK), :] = block

    reorder(turned, from_ref, store)


def local(voxels, counts, neighbours, conv_weight, linear_weight, destination):
    rows, channels = voxels.shape
    offsets = neighbours.shape[0]
    both = ("wide", "narrow")
    shards = lax.axis_size(both)
    own = lax.axis_index(both)
    place = jnp.reshape(own, (1,)).astype(jnp.int32)
    extent = 2 * HALO
    struct = jax.ShapeDtypeStruct
    vmem = pl.BlockSpec(memory_space=VMEM)
    smem = pl.BlockSpec(memory_space=SMEM)

    def packed(first_voxel, first_near):
        near = lax.slice_in_dim(neighbours, first_near, first_near + HALO, axis=1)
        ids = own * rows + first_near + jnp.arange(HALO, dtype=jnp.int32)[None, :]
        relative = jnp.where(near >= 0, near - ids, ABSENT).astype(BF16)
        pad = jnp.zeros((32 - offsets, channels), BF16)
        return jnp.concatenate(
            [lax.slice_in_dim(voxels, first_voxel, first_voxel + extent, axis=0), relative, pad], axis=0
        )

    forward = [(i, i + 1) for i in range(shards - 1)]
    backward = [(target, source) for source, target in forward]
    low = lax.ppermute(packed(rows - extent, rows - HALO), both, forward)
    high = lax.ppermute(packed(0, 0), both, backward)

    table = (rows // 128, 128)
    padded = (channels, rows + BLOCK)
    picked = VMEM((offsets * channels, BLOCK), BF16)
    turned = (2, channels, offsets * channels)
    hbm = pl.BlockSpec(memory_space=pltpu.HBM)
    act, inner, perm, place_high, place_low, weights = pl.pallas_call(
        functools.partial(inner_kernel, shards),
        out_shape=(
            struct((channels, rows), BF16), struct(padded, BF16), struct(table, jnp.int32), struct(table, F32),
            struct(table, F32), struct(turned, BF16),
        ),
        in_specs=[smem, smem, hbm, hbm, hbm, vmem, hbm],
        out_specs=(vmem,) * 6,
        scratch_shapes=[
            VMEM(voxels.shape, BF16), VMEM(neighbours.shape, jnp.int32), VMEM(conv_weight.shape, BF16),
            VMEM((1, rows), jnp.int32), picked, picked, VMEM(padded, BF16), pltpu.SemaphoreType.DMA((4,)),
        ],
        compiler_params=params(),
        cost_estimate=pl.CostEstimate(flops=20_000_000_000, bytes_accessed=6_000_000, transcendentals=0),
        name="first_layer",
    )(place, counts, voxels, neighbours, conv_weight, linear_weight, destination.reshape(1, rows))

    depth = rows // shards + 16
    send = pl.pallas_call(
        outer_kernel,
        out_shape=struct((shards, depth, channels), BF16),
        in_specs=[smem, smem] + [vmem] * 10,
        out_specs=vmem,
        scratch_shapes=[
            picked,
            picked,
            VMEM((channels, 2 * WINDOW), BF16),
            VMEM(padded, BF16),
            VMEM(padded, BF16),
            VMEM((channels, rows), BF16),
        ],
        compiler_params=params(),
        cost_estimate=pl.CostEstimate(flops=30_000_000_000, bytes_accessed=8_000_000, transcendentals=0),
        name="second_layer",
    )(place, counts, low, high, act, inner, neighbours, weights, linear_weight, perm, place_high, place_low)

    got = lax.all_to_all(send, both, split_axis=0, concat_axis=0, tiled=True)
    return pl.pallas_call(
        final_kernel,
        out_shape=struct((rows, channels), BF16),
        in_specs=[vmem],
        out_specs=vmem,
        scratch_shapes=[VMEM((channels, rows), BF16), VMEM(table, jnp.int32)],
        compiler_params=params(),
        name="hilbert_order",
    )(got)


def solution(mesh):
    in_specs = (
        P(("groups", "wide", "narrow"), None),
        P("groups"),
        P(None, ("groups", "wide", "narrow")),
        P(),
        P(),
        P(("groups", "wide", "narrow")),
    )
    out_specs = P(("groups", "wide", "narrow"), None)
    return jax.shard_map(local, mesh=mesh, in_specs=in_specs, out_specs=out_specs, check_vma=False)
```

```python
import functools

import jax
import jax.numpy as jnp
from jax import lax
from jax.experimental import pallas as pl
from jax.experimental.pallas import tpu as pltpu
from jax.sharding import PartitionSpec as P

HALO = 128
BLOCK = 256
WINDOW = 512
BF16 = jnp.bfloat16
F32 = jnp.float32
ABSENT = 256
SMEM = pltpu.SMEM
VMEM = pltpu.VMEM


def params(mebibytes=48):
    return pltpu.CompilerParams(vmem_limit_bytes=mebibytes * 1024 * 1024)


def selector(row, depth):
    shape = (depth, row.shape[1])
    places = lax.broadcasted_iota(jnp.int16, shape, 0)
    wanted = jnp.broadcast_to(row.astype(jnp.int16), shape)
    return jnp.where(places == wanted, BF16(1), BF16(0))


def dot(a, b):
    return jnp.dot(a, b, preferred_element_type=F32)


def live_lanes(first, width, rows, before, own, after):
    at = first + lax.broadcasted_iota(jnp.int32, (1, width), 1)
    limit = jnp.where(at < 0, before - rows, jnp.where(at < rows, own, after + rows))
    return at < limit


def lane_pick(block, lanes):
    numbers = lax.GatherDimensionNumbers(
        offset_dims=(), collapsed_slice_dims=(1,), start_index_map=(1,),
        operand_batching_dims=(0,), start_indices_batching_dims=(0,),
    )
    index = jnp.broadcast_to(lanes.astype(jnp.int16), block.shape)
    return lax.gather(block, index[..., None], numbers, (1, 1), mode=lax.GatherScatterMode.PROMISE_IN_BOUNDS)


def gather_block(window, targets, picked):
    offsets = targets.shape[0]
    channels = picked.shape[0] // offsets
    static = {0: 0, offsets // 2: HALO, offsets - 1: 2 * HALO}
    turn = 0
    for k in range(offsets):
        at = slice(k * channels, (k + 1) * channels)
        if k in static:
            picked[at, :] = window(static[k], BLOCK)
            continue
        turn += 1
        row = targets[k : k + 1, :]
        if turn % 2:
            picked[at, :] = dot(window(0, WINDOW), selector(row, WINDOW)).astype(BF16)
            continue
        for half in range(2):
            part = row[:, half * HALO : (half + 1) * HALO]
            lanes = part & (HALO - 1)
            chunk = jnp.broadcast_to((part >> 7).astype(jnp.int16), (channels, HALO))
            total = jnp.zeros((channels, HALO), BF16)
            for j in range(half, half + 3):
                total = jnp.where(chunk == j, lane_pick(window(j * HALO, HALO), lanes), total)
            picked[at, half * HALO : (half + 1) * HALO] = total


def norm_block(current, convolved, linear, live):
    projected = dot(linear, convolved)
    average = jnp.mean(projected, axis=0, keepdims=True)
    centred = projected - average
    spread = jnp.mean(centred * centred, axis=0, keepdims=True)
    summed = current.astype(F32) + centred * lax.rsqrt(spread + 1e-05)
    return jnp.where(live, summed, 0.0).astype(BF16)


def columns(start):
    return pl.ds(pl.multiple_of(start, HALO), BLOCK)


def turn_weights(weight_ref, layer, turned):
    offsets, channels = weight_ref.shape[1], weight_ref.shape[2]
    for k in range(offsets):
        turned[:, k * channels : (k + 1) * channels] = weight_ref[layer, k].T


def device_counts(place_ref, counts_ref):
    own = place_ref[0]
    last = counts_ref.shape[0] - 1
    before = jnp.where(own > 0, counts_ref[jnp.maximum(own - 1, 0)], 0)
    after = jnp.where(own < last, counts_ref[jnp.minimum(own + 1, last)], 0)
    return own, before, counts_ref[own], after


def slots_tile(c, destination_ref, before_ref, total_ref):
    rows = destination_ref.shape[1]
    shards, tile = before_ref.shape
    groups = rows // 128
    earlier = (
        lax.broadcasted_iota(jnp.int32, (tile, tile), 0) < lax.broadcasted_iota(jnp.int32, (tile, tile), 1)
    ).astype(F32).astype(BF16)
    devices = lax.broadcasted_iota(jnp.int32, (shards, tile), 0)
    goal = destination_ref[:, columns(c * tile)]
    device = goal >> (rows.bit_length() - 1)
    place = goal & (rows - 1)
    member = (jnp.broadcast_to(device, (shards, tile)) == devices).astype(F32)
    member16 = member.astype(BF16)
    before = before_ref[...]
    slot = jnp.sum(member * (dot(member16, earlier) + before), axis=0, keepdims=True).astype(jnp.int32)
    before_ref[...] = before + dot(member16, jnp.ones((tile, tile), BF16))
    row = c * tile + lax.broadcasted_iota(jnp.int32, (1, tile), 1)
    total_ref[...] += scatter_term(slot, (row, place), groups)


def scatter_term(at, values, groups):
    tile = at.shape[1]
    high = (lax.broadcasted_iota(jnp.int32, (groups, tile), 0) == jnp.broadcast_to(at >> 7, (groups, tile))).astype(F32)
    low = (lax.broadcasted_iota(jnp.int32, (128, tile), 0) == jnp.broadcast_to(at & 127, (128, tile))).astype(F32)
    parts = []
    for value in values:
        parts.append(high * (value >> 6).astype(F32))
        parts.append(high * (value & 63).astype(F32))
    left = jnp.concatenate(parts, axis=0).astype(BF16)
    return lax.dot_general(left, low.astype(BF16), (((1,), (1,)), ((), ())), preferred_element_type=F32)


def joined(total, n, groups):
    high = total[2 * n * groups : (2 * n + 1) * groups, :]
    low = total[(2 * n + 1) * groups : (2 * n + 2) * groups, :]
    return (high * 64.0 + low).astype(jnp.int32)


def edges_kernel(place_ref, voxels_hbm, near_hbm, first_ref, last_ref, near_first, near_last, sems):
    rows = voxels_hbm.shape[0]
    extent = 2 * HALO
    copies = [
        pltpu.make_async_copy(source, target, sems.at[n])
        for n, (source, target) in enumerate(
            (
                (near_hbm.at[:, 0:HALO], near_first),
                (near_hbm.at[:, rows - HALO : rows], near_last),
                (voxels_hbm.at[0:extent, :], first_ref.at[0:extent, :]),
                (voxels_hbm.at[rows - extent : rows, :], last_ref.at[0:extent, :]),
            )
        )
    ]
    for copy in copies:
        copy.start()
    own = place_ref[0]
    lanes = lax.broadcasted_iota(jnp.int32, (1, HALO), 1)
    for n, (near_ref, out_ref, first) in enumerate(((near_first, first_ref, 0), (near_last, last_ref, rows - HALO))):
        copies[n].wait()
        near = near_ref[...]
        relative = jnp.where(near >= 0, near - (own * rows + first + lanes), ABSENT).astype(F32)
        pad = jnp.zeros((out_ref.shape[0] - extent - near.shape[0], HALO), F32)
        out_ref[extent:, :] = jnp.concatenate([relative, pad], axis=0).astype(BF16)
    copies[2].wait()
    copies[3].wait()


def inner_kernel(
    shards, place_ref, counts_ref, voxels_ref, near_ref, weight_hbm, linear_ref, destination_ref,
    act_ref, next_ref, perm_ref, high_ref, low_ref, turned_ref,
    weight_ref, even, odd, conv, before_ref, total_ref, sem,
):
    weights_in = pltpu.make_async_copy(weight_hbm, weight_ref, sem)
    weights_in.start()
    rows, channels = voxels_ref.shape
    own, before, count, after = device_counts(place_ref, counts_ref)
    before_ref[...] = (lax.broadcasted_iota(jnp.int32, before_ref.shape, 0) * (rows // shards)).astype(F32)
    total_ref[...] = jnp.zeros_like(total_ref)
    slots = lambda c: slots_tile(c, destination_ref, before_ref, total_ref)
    slots(0)
    slots(1)
    for c in range(rows // BLOCK):
        live = live_lanes(c * BLOCK, BLOCK, rows, before, count, after)
        block = voxels_ref[c * BLOCK : (c + 1) * BLOCK, :].T
        act_ref[:, c * BLOCK : (c + 1) * BLOCK] = jnp.where(live, block.astype(F32), 0.0).astype(BF16)
    weights_in.wait()
    for layer in range(2):
        turn_weights(weight_ref, layer, turned_ref.at[layer])
    linear = linear_ref[0].T

    def gather(b, picked):
        first = (b - 1) * BLOCK
        targets = jnp.maximum(near_ref[:, columns(first + HALO)] - (own * rows + first), -1)
        gather_block(lambda at, n: act_ref[:, pl.ds(pl.multiple_of(first + at, HALO), n)], targets, picked)

    def convolve(b, picked):
        conv[:, columns(b * BLOCK)] = dot(turned_ref[0], picked[...]).astype(BF16)

    blocks = rows // BLOCK

    def step(t, _):
        gather(2 * t + 1, even)
        slots(2 * t + 2)
        convolve(2 * t, odd)
        gather(2 * t + 2, odd)
        slots(2 * t + 3)
        convolve(2 * t + 1, even)
        return 0

    lax.fori_loop(0, (blocks - 2) // 2, step, 0)
    gather(blocks - 1, even)
    convolve(blocks - 2, odd)
    convolve(blocks - 1, even)

    def norm(b):
        first = b * BLOCK - HALO
        live = live_lanes(first, BLOCK, rows, before, count, after)
        next_ref[:, columns(b * BLOCK)] = norm_block(
            act_ref[:, columns(first)], conv[:, columns(b * BLOCK)], linear, live
        )

    in_turn(1, blocks, norm)
    groups = rows // 128
    perm_ref[...] = joined(total_ref[...], 0, groups)
    high_ref[...] = total_ref[2 * groups : 3 * groups, :]
    low_ref[...] = total_ref[3 * groups :, :]


def in_turn(first, last, body):
    count = last - first
    unroll = max(u for u in range(1, 6) if count % u == 0)

    def step(t, _):
        for u in range(unroll):
            body(first + t * unroll + u)
        return 0

    lax.fori_loop(0, count // unroll, step, 0)


def outer_kernel(
    place_ref, counts_ref, low_ref, high_ref, act_ref, inner_ref, near_ref, turned_ref, linear_ref,
    perm_ref, place_high_ref, place_low_ref, send_ref, even, odd, edge, padded, conv, last,
):
    channels, rows = act_ref.shape
    own, before, count, after = device_counts(place_ref, counts_ref)
    extent = 2 * HALO
    linear = linear_ref[0].T
    lanes = lax.broadcasted_iota(jnp.int32, (1, HALO), 1)

    def reached(halo_ref, base):
        relative = halo_ref[extent : extent + near_ref.shape[0], :].astype(F32).astype(jnp.int32)
        return jnp.where(relative == ABSENT, -1, relative + lanes + base)

    def masked(halo_ref, first):
        live = live_lanes(first, extent, rows, before, count, after)
        return jnp.where(live, halo_ref[0:extent, :].T.astype(F32), 0.0).astype(BF16)

    edges = (edge.at[:, 0:WINDOW], edge.at[:, WINDOW:])
    edges[0][:, 0:extent] = masked(low_ref, -extent)
    edges[0][:, extent:] = act_ref[:, 0:extent]
    edges[1][:, 0:extent] = act_ref[:, rows - extent : rows]
    edges[1][:, extent:] = masked(high_ref, rows)
    near = (
        jnp.concatenate(
            [reached(low_ref, HALO), jnp.maximum(near_ref[:, 0:HALO] - own * rows + extent, -1)], axis=1
        ),
        jnp.concatenate(
            [
                jnp.maximum(near_ref[:, rows - HALO : rows] - own * rows - (rows - extent), -1),
                reached(high_ref, 2 * HALO),
            ],
            axis=1,
        ),
    )
    picks = (even, odd)
    for n in range(2):
        gather_block(lambda at, size: edges[n][:, at : at + size], near[n], picks[n])
    for n in range(2):
        conv[:, n * BLOCK : (n + 1) * BLOCK] = dot(turned_ref[0], picks[n][...]).astype(BF16)
    for n in range(2):
        at = n * rows
        live = live_lanes(at - HALO, BLOCK, rows, before, count, after)
        padded[:, at : at + BLOCK] = norm_block(
            edges[n][:, HALO : HALO + BLOCK], conv[:, n * BLOCK : (n + 1) * BLOCK], linear, live
        )
    padded[:, BLOCK:rows] = inner_ref[:, BLOCK:rows]

    linear = linear_ref[1].T

    def gather(b, picked):
        first = b * BLOCK
        targets = jnp.maximum(near_ref[:, columns(first)] - (own * rows + first - HALO), -1)
        gather_block(lambda at, n: padded[:, pl.ds(pl.multiple_of(first + at, HALO), n)], targets, picked)

    def convolve(b, picked):
        conv[:, columns((b + 1) * BLOCK)] = dot(turned_ref[1], picked[...]).astype(BF16)

    def step(t, _):
        gather(2 * t, even)
        convolve(2 * t - 1, odd)
        gather(2 * t + 1, odd)
        convolve(2 * t, even)
        return 0

    blocks = rows // BLOCK
    lax.fori_loop(0, blocks // 2, step, 0)
    convolve(blocks - 1, odd)

    def norm(b):
        first = b * BLOCK
        live = live_lanes(first, BLOCK, rows, before, count, after)
        last[:, columns(first)] = norm_block(
            padded[:, columns(first + HALO)], conv[:, columns(first + BLOCK)], linear, live
        )

    in_turn(0, blocks, norm)

    shards, depth, _ = send_ref.shape
    capacity = rows // shards
    pieces = BLOCK // capacity

    def store(b, block):
        for p in range(pieces):
            send_ref[b * pieces + p, 0:capacity, :] = block[p * capacity : (p + 1) * capacity, :]

    reorder(last, perm_ref, store)
    held = capacity // 128
    pad = jnp.zeros((depth - capacity - 2 * held, 128), F32)
    for d in range(shards):
        at = slice(d * held, (d + 1) * held)
        extra = jnp.concatenate([place_high_ref[at, :], place_low_ref[at, :], pad], axis=0)
        send_ref[d, capacity:, :] = extra.astype(BF16)


def reorder(source, from_ref, store, dots=6, unroll=8):
    channels, rows = source.shape
    windows = rows // WINDOW

    def one(b):
        pair = from_ref[pl.ds(b * 2, 2), :]
        wanted = jnp.concatenate([pair[0:1, :], pair[1:2, :]], axis=1)
        total = jnp.zeros((channels, BLOCK), F32)
        halves = [jnp.zeros((channels, 128), BF16) for _ in range(2)]
        lanes = [pair[h : h + 1, :] & 127 for h in range(2)]
        chunks = [jnp.broadcast_to((pair[h : h + 1, :] >> 7).astype(jnp.int16), (channels, 128)) for h in range(2)]
        rest = [(j, h) for j in range(dots * WINDOW // 128, rows // 128) for h in range(2)]
        done = 0
        for w in range(dots):
            total = total + dot(source[:, w * WINDOW : (w + 1) * WINDOW], selector(wanted - w * WINDOW, WINDOW))
            until = len(rest) * (w + 1) // dots
            for j, h in rest[done:until]:
                halves[h] = jnp.where(
                    chunks[h] == j, lane_pick(source[:, j * 128 : (j + 1) * 128], lanes[h]), halves[h]
                )
            done = until
        store(b, (total + jnp.concatenate(halves, axis=1).astype(F32)).astype(BF16).T)

    def step(t, _):
        for u in range(unroll):
            one(t * unroll + u)
        return 0

    lax.fori_loop(0, rows // BLOCK // unroll, step, 0)


def final_kernel(got_ref, out_ref, turned, from_ref):
    rows = out_ref.shape[0]
    shards = got_ref.shape[0]
    groups = rows // 128
    capacity = rows // shards
    held = capacity // 128
    lanes = lax.broadcasted_iota(jnp.int32, (1, 128), 1)
    total = jnp.zeros((2 * groups, 128), F32)
    for s in range(shards):
        turned[:, s * capacity : (s + 1) * capacity] = got_ref[s, 0:capacity, :].T
        extra = got_ref[s, capacity:, :].astype(F32)
        place = (extra[0:held, :] * 64.0 + extra[held : 2 * held, :]).astype(jnp.int32)
        for h in range(held):
            total = total + scatter_term(place[h : h + 1, :], (s * capacity + h * 128 + lanes,), groups)
    from_ref[...] = joined(total, 0, groups)

    def store(b, block):
        out_ref[pl.ds(pl.multiple_of(b * BLOCK, BLOCK), BLOCK), :] = block

    reorder(turned, from_ref, store)


def local(voxels, counts, neighbours, conv_weight, linear_weight, destination):
    rows, channels = voxels.shape
    offsets = neighbours.shape[0]
    both = ("wide", "narrow")
    shards = lax.axis_size(both)
    own = lax.axis_index(both)
    place = jnp.reshape(own, (1,)).astype(jnp.int32)
    extent = 2 * HALO
    struct = jax.ShapeDtypeStruct
    vmem = pl.BlockSpec(memory_space=VMEM)
    smem = pl.BlockSpec(memory_space=SMEM)
    hbm = pl.BlockSpec(memory_space=pltpu.HBM)

    packed = struct((extent + 32, channels), BF16)
    first, final = pl.pallas_call(
        edges_kernel,
        out_shape=(packed, packed),
        in_specs=[smem, hbm, hbm],
        out_specs=(vmem, vmem),
        scratch_shapes=[VMEM((offsets, HALO), jnp.int32), VMEM((offsets, HALO), jnp.int32), pltpu.SemaphoreType.DMA((4,))],
        cost_estimate=pl.CostEstimate(flops=20_000_000_000, bytes_accessed=500_000, transcendentals=0),
        compiler_params=params(60),
        name="edges",
    )(place, voxels, neighbours)
    forward = [(i, i + 1) for i in range(shards - 1)]
    backward = [(target, source) for source, target in forward]
    low = lax.ppermute(final, both, forward)
    high = lax.ppermute(first, both, backward)

    table = (rows // 128, 128)
    padded = (channels, rows + BLOCK)
    picked = VMEM((offsets * channels, BLOCK), BF16)
    turned = (2, channels, offsets * channels)
    act, inner, perm, place_high, place_low, weights = pl.pallas_call(
        functools.partial(inner_kernel, shards),
        out_shape=(
            struct((channels, rows), BF16), struct(padded, BF16), struct(table, jnp.int32), struct(table, F32),
            struct(table, F32), struct(turned, BF16),
        ),
        in_specs=[smem, smem, vmem, vmem, hbm, vmem, vmem],
        out_specs=(vmem,) * 6,
        scratch_shapes=[
            VMEM(conv_weight.shape, BF16), picked, picked, VMEM(padded, BF16), VMEM((shards, BLOCK), F32),
            VMEM((4 * rows // 128, 128), F32), pltpu.SemaphoreType.DMA,
        ],
        compiler_params=params(),
        cost_estimate=pl.CostEstimate(flops=20_000_000_000, bytes_accessed=6_000_000, transcendentals=0),
        name="first_layer",
    )(place, counts, voxels, neighbours, conv_weight, linear_weight, destination.reshape(1, rows))

    depth = rows // shards + 16
    send = pl.pallas_call(
        outer_kernel,
        out_shape=struct((shards, depth, channels), BF16),
        in_specs=[smem, smem] + [vmem] * 10,
        out_specs=vmem,
        scratch_shapes=[
            picked,
            picked,
            VMEM((channels, 2 * WINDOW), BF16),
            VMEM(padded, BF16),
            VMEM(padded, BF16),
            VMEM((channels, rows), BF16),
        ],
        compiler_params=params(),
        cost_estimate=pl.CostEstimate(flops=30_000_000_000, bytes_accessed=8_000_000, transcendentals=0),
        name="second_layer",
    )(place, counts, low, high, act, inner, neighbours, weights, linear_weight, perm, place_high, place_low)

    got = lax.all_to_all(send, both, split_axis=0, concat_axis=0, tiled=True)
    return pl.pallas_call(
        final_kernel,
        out_shape=struct((rows, channels), BF16),
        in_specs=[vmem],
        out_specs=vmem,
        scratch_shapes=[VMEM((channels, rows), BF16), VMEM(table, jnp.int32)],
        compiler_params=params(),
        name="hilbert_order",
    )(got)


def solution(mesh):
    in_specs = (
        P(("groups", "wide", "narrow"), None),
        P("groups"),
        P(None, ("groups", "wide", "narrow")),
        P(),
        P(),
        P(("groups", "wide", "narrow")),
    )
    out_specs = P(("groups", "wide", "narrow"), None)
    return jax.shard_map(local, mesh=mesh, in_specs=in_specs, out_specs=out_specs, check_vma=False)
```

```python
import functools

import jax
import jax.numpy as jnp
from jax import lax
from jax.experimental import pallas as pl
from jax.experimental.pallas import tpu as pltpu
from jax.sharding import PartitionSpec as P

HALO = 128
BLOCK = 256
WINDOW = 512
BF16 = jnp.bfloat16
F32 = jnp.float32
ABSENT = 256
SMEM = pltpu.SMEM
VMEM = pltpu.VMEM


def params(mebibytes=48):
    return pltpu.CompilerParams(vmem_limit_bytes=mebibytes * 1024 * 1024)


def selector(row, depth):
    shape = (depth, row.shape[1])
    places = lax.broadcasted_iota(jnp.int16, shape, 0)
    wanted = jnp.broadcast_to(row.astype(jnp.int16), shape)
    return jnp.where(places == wanted, BF16(1), BF16(0))


def dot(a, b):
    return jnp.dot(a, b, preferred_element_type=F32)


def live_lanes(first, width, rows, before, own, after):
    at = first + lax.broadcasted_iota(jnp.int32, (1, width), 1)
    limit = jnp.where(at < 0, before - rows, jnp.where(at < rows, own, after + rows))
    return at < limit


def lane_pick(block, lanes):
    numbers = lax.GatherDimensionNumbers(
        offset_dims=(), collapsed_slice_dims=(1,), start_index_map=(1,),
        operand_batching_dims=(0,), start_indices_batching_dims=(0,),
    )
    index = jnp.broadcast_to(lanes.astype(jnp.int16), block.shape)
    return lax.gather(block, index[..., None], numbers, (1, 1), mode=lax.GatherScatterMode.PROMISE_IN_BOUNDS)


def gather_block(window, targets, picked):
    offsets = targets.shape[0]
    channels = picked.shape[0] // offsets
    static = {0: 0, offsets // 2: HALO, offsets - 1: 2 * HALO}
    turn = 0
    for k in range(offsets):
        at = slice(k * channels, (k + 1) * channels)
        if k in static:
            picked[at, :] = window(static[k], BLOCK)
            continue
        turn += 1
        row = targets[k : k + 1, :]
        if turn % 2:
            picked[at, :] = dot(window(0, WINDOW), selector(row, WINDOW)).astype(BF16)
            continue
        for half in range(2):
            part = row[:, half * HALO : (half + 1) * HALO]
            lanes = part & (HALO - 1)
            chunk = jnp.broadcast_to((part >> 7).astype(jnp.int16), (channels, HALO))
            total = jnp.zeros((channels, HALO), BF16)
            for j in range(half, half + 3):
                total = jnp.where(chunk == j, lane_pick(window(j * HALO, HALO), lanes), total)
            picked[at, half * HALO : (half + 1) * HALO] = total


def norm_block(current, convolved, linear, live):
    projected = dot(linear, convolved)
    average = jnp.mean(projected, axis=0, keepdims=True)
    centred = projected - average
    spread = jnp.mean(centred * centred, axis=0, keepdims=True)
    summed = current.astype(F32) + centred * lax.rsqrt(spread + 1e-05)
    return jnp.where(live, summed, 0.0).astype(BF16)


def columns(start):
    return pl.ds(pl.multiple_of(start, HALO), BLOCK)


def turn_weights(weight_ref, layer, turned):
    offsets, channels = weight_ref.shape[1], weight_ref.shape[2]
    for k in range(offsets):
        turned[:, k * channels : (k + 1) * channels] = weight_ref[layer, k].T


def device_counts(place_ref, counts_ref):
    own = place_ref[0]
    last = counts_ref.shape[0] - 1
    before = jnp.where(own > 0, counts_ref[jnp.maximum(own - 1, 0)], 0)
    after = jnp.where(own < last, counts_ref[jnp.minimum(own + 1, last)], 0)
    return own, before, counts_ref[own], after


def slots_table(destination_ref, shards):
    rows = destination_ref.shape[1]
    capacity = rows // shards
    groups = rows // 128
    tile = 256
    earlier = (
        lax.broadcasted_iota(jnp.int32, (tile, tile), 0) < lax.broadcasted_iota(jnp.int32, (tile, tile), 1)
    ).astype(F32).astype(BF16)
    ones = jnp.ones((tile, tile), BF16)
    devices = lax.broadcasted_iota(jnp.int32, (shards, tile), 0)
    before = (devices * capacity).astype(F32)
    total = jnp.zeros((4 * groups, 128), F32)
    for c in range(rows // tile):
        goal = destination_ref[:, c * tile : (c + 1) * tile]
        device = goal >> (rows.bit_length() - 1)
        place = goal & (rows - 1)
        member = (jnp.broadcast_to(device, (shards, tile)) == devices).astype(F32)
        member16 = member.astype(BF16)
        slot = jnp.sum(member * (dot(member16, earlier) + before), axis=0, keepdims=True).astype(jnp.int32)
        before = before + dot(member16, ones)
        row = c * tile + lax.broadcasted_iota(jnp.int32, (1, tile), 1)
        total = total + scatter_term(slot, (row, place), groups)
    return total


def scatter_term(at, values, groups):
    tile = at.shape[1]
    high = (lax.broadcasted_iota(jnp.int32, (groups, tile), 0) == jnp.broadcast_to(at >> 7, (groups, tile))).astype(F32)
    low = (lax.broadcasted_iota(jnp.int32, (128, tile), 0) == jnp.broadcast_to(at & 127, (128, tile))).astype(F32)
    parts = []
    for value in values:
        parts.append(high * (value >> 6).astype(F32))
        parts.append(high * (value & 63).astype(F32))
    left = jnp.concatenate(parts, axis=0).astype(BF16)
    return lax.dot_general(left, low.astype(BF16), (((1,), (1,)), ((), ())), preferred_element_type=F32)


def joined(total, n, groups):
    high = total[2 * n * groups : (2 * n + 1) * groups, :]
    low = total[(2 * n + 1) * groups : (2 * n + 2) * groups, :]
    return (high * 64.0 + low).astype(jnp.int32)


def edges_kernel(place_ref, voxels_hbm, near_hbm, first_ref, last_ref, near_first, near_last, sems):
    rows = voxels_hbm.shape[0]
    extent = 2 * HALO
    copies = [
        pltpu.make_async_copy(source, target, sems.at[n])
        for n, (source, target) in enumerate(
            (
                (near_hbm.at[:, 0:HALO], near_first),
                (near_hbm.at[:, rows - HALO : rows], near_last),
                (voxels_hbm.at[0:extent, :], first_ref.at[0:extent, :]),
                (voxels_hbm.at[rows - extent : rows, :], last_ref.at[0:extent, :]),
            )
        )
    ]
    for copy in copies:
        copy.start()
    own = place_ref[0]
    lanes = lax.broadcasted_iota(jnp.int32, (1, HALO), 1)
    for n, (near_ref, out_ref, first) in enumerate(((near_first, first_ref, 0), (near_last, last_ref, rows - HALO))):
        copies[n].wait()
        near = near_ref[...]
        relative = jnp.where(near >= 0, near - (own * rows + first + lanes), ABSENT).astype(F32)
        pad = jnp.zeros((out_ref.shape[0] - extent - near.shape[0], HALO), F32)
        out_ref[extent:, :] = jnp.concatenate([relative, pad], axis=0).astype(BF16)
    copies[2].wait()
    copies[3].wait()


def inner_kernel(
    shards, place_ref, counts_ref, voxels_ref, near_ref, weight_hbm, linear_ref, destination_ref,
    act_ref, next_ref, perm_ref, high_ref, low_ref, turned_ref,
    weight_ref, even, odd, conv, sem,
):
    weights_in = pltpu.make_async_copy(weight_hbm, weight_ref, sem)
    weights_in.start()
    rows, channels = voxels_ref.shape
    own, before, count, after = device_counts(place_ref, counts_ref)
    groups = rows // 128
    total = slots_table(destination_ref, shards)
    perm_ref[...] = joined(total, 0, groups)
    high_ref[...] = total[2 * groups : 3 * groups, :]
    low_ref[...] = total[3 * groups :, :]
    for c in range(rows // BLOCK):
        live = live_lanes(c * BLOCK, BLOCK, rows, before, count, after)
        block = voxels_ref[c * BLOCK : (c + 1) * BLOCK, :].T
        act_ref[:, c * BLOCK : (c + 1) * BLOCK] = jnp.where(live, block.astype(F32), 0.0).astype(BF16)
    weights_in.wait()
    for layer in range(2):
        turn_weights(weight_ref, layer, turned_ref.at[layer])
    linear = linear_ref[0].T

    def gather(b, picked):
        first = (b - 1) * BLOCK
        targets = jnp.maximum(near_ref[:, columns(first + HALO)] - (own * rows + first), -1)
        gather_block(lambda at, n: act_ref[:, pl.ds(pl.multiple_of(first + at, HALO), n)], targets, picked)

    def convolve(b, picked):
        conv[:, columns(b * BLOCK)] = dot(turned_ref[0], picked[...]).astype(BF16)

    blocks = rows // BLOCK

    def step(t, _):
        gather(2 * t + 1, even)
        convolve(2 * t, odd)
        gather(2 * t + 2, odd)
        convolve(2 * t + 1, even)
        return 0

    lax.fori_loop(0, (blocks - 2) // 2, step, 0)
    gather(blocks - 1, even)
    convolve(blocks - 2, odd)
    convolve(blocks - 1, even)

    def norm(b):
        first = b * BLOCK - HALO
        live = live_lanes(first, BLOCK, rows, before, count, after)
        next_ref[:, columns(b * BLOCK)] = norm_block(
            act_ref[:, columns(first)], conv[:, columns(b * BLOCK)], linear, live
        )

    in_turn(1, blocks, norm)


def in_turn(first, last, body):
    count = last - first
    unroll = max(u for u in range(1, 6) if count % u == 0)

    def step(t, _):
        for u in range(unroll):
            body(first + t * unroll + u)
        return 0

    lax.fori_loop(0, count // unroll, step, 0)


def outer_kernel(
    place_ref, counts_ref, low_ref, high_ref, act_ref, inner_ref, near_ref, turned_ref, linear_ref,
    perm_ref, place_high_ref, place_low_ref, send_ref, even, odd, edge, edge_conv, padded, conv, last,
):
    channels, rows = act_ref.shape
    own, before, count, after = device_counts(place_ref, counts_ref)
    extent = 2 * HALO
    lanes = lax.broadcasted_iota(jnp.int32, (1, HALO), 1)

    def reached(halo_ref, base):
        relative = halo_ref[extent : extent + near_ref.shape[0], :].astype(F32).astype(jnp.int32)
        return jnp.where(relative == ABSENT, -1, relative + lanes + base)

    def masked(halo_ref, first):
        live = live_lanes(first, extent, rows, before, count, after)
        return jnp.where(live, halo_ref[0:extent, :].T.astype(F32), 0.0).astype(BF16)

    edges = (edge.at[:, 0:WINDOW], edge.at[:, WINDOW:])
    edges[0][:, 0:extent] = masked(low_ref, -extent)
    edges[0][:, extent:] = act_ref[:, 0:extent]
    edges[1][:, 0:extent] = act_ref[:, rows - extent : rows]
    edges[1][:, extent:] = masked(high_ref, rows)
    near = (
        jnp.concatenate(
            [reached(low_ref, HALO), jnp.maximum(near_ref[:, 0:HALO] - own * rows + extent, -1)], axis=1
        ),
        jnp.concatenate(
            [
                jnp.maximum(near_ref[:, rows - HALO : rows] - own * rows - (rows - extent), -1),
                reached(high_ref, 2 * HALO),
            ],
            axis=1,
        ),
    )
    blocks = rows // BLOCK
    padded[:, BLOCK:rows] = inner_ref[:, BLOCK:rows]

    def gather_edge(n, picked):
        gather_block(lambda at, size: edges[n][:, at : at + size], near[n], picked)

    def convolve_edge(n, picked):
        edge_conv[:, n * BLOCK : (n + 1) * BLOCK] = dot(turned_ref[0], picked[...]).astype(BF16)

    def norm_edge(n):
        at = n * rows
        live = live_lanes(at - HALO, BLOCK, rows, before, count, after)
        padded[:, at : at + BLOCK] = norm_block(
            edges[n][:, HALO : HALO + BLOCK], edge_conv[:, n * BLOCK : (n + 1) * BLOCK], linear_ref[0].T, live
        )

    def gather(b, picked):
        first = b * BLOCK
        targets = jnp.maximum(near_ref[:, columns(first)] - (own * rows + first - HALO), -1)
        gather_block(lambda at, n: padded[:, pl.ds(pl.multiple_of(first + at, HALO), n)], targets, picked)

    def convolve(b, picked):
        conv[:, columns(b * BLOCK)] = dot(turned_ref[1], picked[...]).astype(BF16)

    gather_edge(0, even)
    gather_edge(1, odd)
    convolve_edge(0, even)
    gather(1, even)
    convolve_edge(1, odd)

    def step(t, _):
        gather(2 * t + 2, odd)
        convolve(2 * t + 1, even)
        gather(2 * t + 3, even)
        convolve(2 * t + 2, odd)
        return 0

    lax.fori_loop(0, (blocks - 4) // 2, step, 0)
    norm_edge(0)
    norm_edge(1)
    gather(blocks - 2, odd)
    convolve(blocks - 3, even)
    gather(0, even)
    convolve(blocks - 2, odd)
    gather(blocks - 1, odd)
    convolve(0, even)
    convolve(blocks - 1, odd)
    linear = linear_ref[1].T

    def norm(b):
        first = b * BLOCK
        live = live_lanes(first, BLOCK, rows, before, count, after)
        last[:, columns(first)] = norm_block(
            padded[:, columns(first + HALO)], conv[:, columns(first)], linear, live
        )

    in_turn(0, blocks, norm)

    shards, depth, _ = send_ref.shape
    capacity = rows // shards
    pieces = BLOCK // capacity

    def store(b, block):
        for p in range(pieces):
            send_ref[b * pieces + p, 0:capacity, :] = block[p * capacity : (p + 1) * capacity, :]

    reorder(last, perm_ref, store)
    held = capacity // 128
    pad = jnp.zeros((depth - capacity - 2 * held, 128), F32)
    for d in range(shards):
        at = slice(d * held, (d + 1) * held)
        extra = jnp.concatenate([place_high_ref[at, :], place_low_ref[at, :], pad], axis=0)
        send_ref[d, capacity:, :] = extra.astype(BF16)


def reorder(source, from_ref, store, dots=6, unroll=16):
    channels, rows = source.shape
    windows = rows // WINDOW

    def one(b):
        pair = from_ref[pl.ds(b * 2, 2), :]
        wanted = jnp.concatenate([pair[0:1, :], pair[1:2, :]], axis=1)
        total = jnp.zeros((channels, BLOCK), F32)
        halves = [jnp.zeros((channels, 128), BF16) for _ in range(2)]
        lanes = [pair[h : h + 1, :] & 127 for h in range(2)]
        chunks = [jnp.broadcast_to((pair[h : h + 1, :] >> 7).astype(jnp.int16), (channels, 128)) for h in range(2)]
        rest = [(j, h) for j in range(dots * WINDOW // 128, rows // 128) for h in range(2)]
        done = 0
        for w in range(dots):
            total = total + dot(source[:, w * WINDOW : (w + 1) * WINDOW], selector(wanted - w * WINDOW, WINDOW))
            until = len(rest) * (w + 1) // dots
            for j, h in rest[done:until]:
                halves[h] = jnp.where(
                    chunks[h] == j, lane_pick(source[:, j * 128 : (j + 1) * 128], lanes[h]), halves[h]
                )
            done = until
        store(b, (total + jnp.concatenate(halves, axis=1).astype(F32)).astype(BF16).T)

    def step(t, _):
        for u in range(unroll):
            one(t * unroll + u)
        return 0

    lax.fori_loop(0, rows // BLOCK // unroll, step, 0)


def final_kernel(got_ref, out_ref, turned, from_ref):
    rows = out_ref.shape[0]
    shards = got_ref.shape[0]
    groups = rows // 128
    capacity = rows // shards
    held = capacity // 128
    lanes = lax.broadcasted_iota(jnp.int32, (1, capacity), 1)
    total = jnp.zeros((2 * groups, 128), F32)
    for s in range(shards):
        turned[:, s * capacity : (s + 1) * capacity] = got_ref[s, 0:capacity, :].T
        extra = got_ref[s, capacity:, :].astype(F32)
        place = (extra[0:held, :] * 64.0 + extra[held : 2 * held, :]).astype(jnp.int32)
        place = jnp.concatenate([place[h : h + 1, :] for h in range(held)], axis=1)
        total = total + scatter_term(place, (s * capacity + lanes,), groups)
    from_ref[...] = joined(total, 0, groups)

    def store(b, block):
        out_ref[pl.ds(pl.multiple_of(b * BLOCK, BLOCK), BLOCK), :] = block

    reorder(turned, from_ref, store)


def local(voxels, counts, neighbours, conv_weight, linear_weight, destination):
    rows, channels = voxels.shape
    offsets = neighbours.shape[0]
    both = ("wide", "narrow")
    shards = lax.axis_size(both)
    own = lax.axis_index(both)
    place = jnp.reshape(own, (1,)).astype(jnp.int32)
    extent = 2 * HALO
    struct = jax.ShapeDtypeStruct
    vmem = pl.BlockSpec(memory_space=VMEM)
    smem = pl.BlockSpec(memory_space=SMEM)
    hbm = pl.BlockSpec(memory_space=pltpu.HBM)

    packed = struct((extent + 32, channels), BF16)
    first, final = pl.pallas_call(
        edges_kernel,
        out_shape=(packed, packed),
        in_specs=[smem, hbm, hbm],
        out_specs=(vmem, vmem),
        scratch_shapes=[VMEM((offsets, HALO), jnp.int32), VMEM((offsets, HALO), jnp.int32), pltpu.SemaphoreType.DMA((4,))],
        cost_estimate=pl.CostEstimate(flops=20_000_000_000, bytes_accessed=500_000, transcendentals=0),
        compiler_params=params(60),
        name="edges",
    )(place, voxels, neighbours)
    forward = [(i, i + 1) for i in range(shards - 1)]
    backward = [(target, source) for source, target in forward]
    low = lax.ppermute(final, both, forward)
    high = lax.ppermute(first, both, backward)

    table = (rows // 128, 128)
    padded = (channels, rows + BLOCK)
    picked = VMEM((offsets * channels, BLOCK), BF16)
    turned = (2, channels, offsets * channels)
    act, inner, perm, place_high, place_low, weights = pl.pallas_call(
        functools.partial(inner_kernel, shards),
        out_shape=(
            struct((channels, rows), BF16), struct(padded, BF16), struct(table, jnp.int32), struct(table, F32),
            struct(table, F32), struct(turned, BF16),
        ),
        in_specs=[smem, smem, vmem, vmem, hbm, vmem, vmem],
        out_specs=(vmem,) * 6,
        scratch_shapes=[
            VMEM(conv_weight.shape, BF16), picked, picked, VMEM(padded, BF16), pltpu.SemaphoreType.DMA,
        ],
        compiler_params=params(),
        cost_estimate=pl.CostEstimate(flops=20_000_000_000, bytes_accessed=6_000_000, transcendentals=0),
        name="first_layer",
    )(place, counts, voxels, neighbours, conv_weight, linear_weight, destination.reshape(1, rows))

    depth = rows // shards + 16
    send = pl.pallas_call(
        outer_kernel,
        out_shape=struct((shards, depth, channels), BF16),
        in_specs=[smem, smem] + [vmem] * 10,
        out_specs=vmem,
        scratch_shapes=[
            picked,
            picked,
            VMEM((channels, 2 * WINDOW), BF16),
            VMEM((channels, 2 * BLOCK), BF16),
            VMEM(padded, BF16),
            VMEM((channels, rows), BF16),
            VMEM((channels, rows), BF16),
        ],
        compiler_params=params(),
        cost_estimate=pl.CostEstimate(flops=30_000_000_000, bytes_accessed=8_000_000, transcendentals=0),
        name="second_layer",
    )(place, counts, low, high, act, inner, neighbours, weights, linear_weight, perm, place_high, place_low)

    got = lax.all_to_all(send, both, split_axis=0, concat_axis=0, tiled=True)
    return pl.pallas_call(
        final_kernel,
        out_shape=struct((rows, channels), BF16),
        in_specs=[vmem],
        out_specs=vmem,
        scratch_shapes=[VMEM((channels, rows), BF16), VMEM(table, jnp.int32)],
        compiler_params=params(),
        name="hilbert_order",
    )(got)


def solution(mesh):
    in_specs = (
        P(("groups", "wide", "narrow"), None),
        P("groups"),
        P(None, ("groups", "wide", "narrow")),
        P(),
        P(),
        P(("groups", "wide", "narrow")),
    )
    out_specs = P(("groups", "wide", "narrow"), None)
    return jax.shard_map(local, mesh=mesh, in_specs=in_specs, out_specs=out_specs, check_vma=False)
```

```python
import functools

import jax
import jax.numpy as jnp
from jax import lax
from jax.experimental import pallas as pl
from jax.experimental.pallas import tpu as pltpu
from jax.sharding import PartitionSpec as P

HALO = 128
BLOCK = 256
WINDOW = 512
BF16 = jnp.bfloat16
F32 = jnp.float32
ABSENT = 256
SMEM = pltpu.SMEM
VMEM = pltpu.VMEM


def params(mebibytes=48):
    return pltpu.CompilerParams(vmem_limit_bytes=mebibytes * 1024 * 1024)


def selector(row, depth):
    shape = (depth, row.shape[1])
    places = lax.broadcasted_iota(jnp.int16, shape, 0)
    wanted = jnp.broadcast_to(row.astype(jnp.int16), shape)
    return jnp.where(places == wanted, BF16(1), BF16(0))


def dot(a, b):
    return jnp.dot(a, b, preferred_element_type=F32)


def live_lanes(first, width, rows, before, own, after):
    at = first + lax.broadcasted_iota(jnp.int32, (1, width), 1)
    limit = jnp.where(at < 0, before - rows, jnp.where(at < rows, own, after + rows))
    return at < limit


def lane_pick(block, lanes):
    numbers = lax.GatherDimensionNumbers(
        offset_dims=(), collapsed_slice_dims=(1,), start_index_map=(1,),
        operand_batching_dims=(0,), start_indices_batching_dims=(0,),
    )
    index = jnp.broadcast_to(lanes.astype(jnp.int16), block.shape)
    return lax.gather(block, index[..., None], numbers, (1, 1), mode=lax.GatherScatterMode.PROMISE_IN_BOUNDS)


def gather_block(window, targets, picked):
    offsets = targets.shape[0]
    channels = picked.shape[0] // offsets
    static = {0: 0, offsets // 2: HALO, offsets - 1: 2 * HALO}
    turn = 0
    for k in range(offsets):
        at = slice(k * channels, (k + 1) * channels)
        if k in static:
            picked[at, :] = window(static[k], BLOCK)
            continue
        turn += 1
        row = targets[k : k + 1, :]
        if turn % 2:
            picked[at, :] = dot(window(0, WINDOW), selector(row, WINDOW)).astype(BF16)
            continue
        for half in range(2):
            part = row[:, half * HALO : (half + 1) * HALO]
            lanes = part & (HALO - 1)
            chunk = jnp.broadcast_to((part >> 7).astype(jnp.int16), (channels, HALO))
            total = jnp.zeros((channels, HALO), BF16)
            for j in range(half, half + 3):
                total = jnp.where(chunk == j, lane_pick(window(j * HALO, HALO), lanes), total)
            picked[at, half * HALO : (half + 1) * HALO] = total


def norm_block(current, convolved, linear, live):
    projected = dot(linear, convolved)
    average = jnp.mean(projected, axis=0, keepdims=True)
    centred = projected - average
    spread = jnp.mean(centred * centred, axis=0, keepdims=True)
    summed = current.astype(F32) + centred * lax.rsqrt(spread + 1e-05)
    return jnp.where(live, summed, 0.0).astype(BF16)


def columns(start):
    return pl.ds(pl.multiple_of(start, HALO), BLOCK)


def turn_weights(weight_ref, layer, turned):
    offsets, channels = weight_ref.shape[1], weight_ref.shape[2]
    for k in range(offsets):
        turned[:, k * channels : (k + 1) * channels] = weight_ref[layer, k].T


def device_counts(place_ref, counts_ref):
    own = place_ref[0]
    last = counts_ref.shape[0] - 1
    before = jnp.where(own > 0, counts_ref[jnp.maximum(own - 1, 0)], 0)
    after = jnp.where(own < last, counts_ref[jnp.minimum(own + 1, last)], 0)
    return own, before, counts_ref[own], after


def slots_table(destination_ref, shards):
    rows = destination_ref.shape[1]
    capacity = rows // shards
    groups = rows // 128
    tile = 256
    earlier = (
        lax.broadcasted_iota(jnp.int32, (tile, tile), 0) < lax.broadcasted_iota(jnp.int32, (tile, tile), 1)
    ).astype(F32).astype(BF16)
    devices = lax.broadcasted_iota(jnp.int32, (shards, tile), 0)
    tiles = rows // tile
    goals = [destination_ref[:, c * tile : (c + 1) * tile] for c in range(tiles)]
    members = [
        (jnp.broadcast_to(goal >> (rows.bit_length() - 1), (shards, tile)) == devices).astype(F32) for goal in goals
    ]
    stacked = jnp.concatenate([member.astype(BF16) for member in members], axis=0)
    ranks = dot(stacked, earlier)
    sums = dot(stacked, jnp.ones((tile, tile), BF16))
    before = (devices * capacity).astype(F32)
    total = jnp.zeros((4 * groups, 128), F32)
    for c in range(tiles):
        part = slice(c * shards, (c + 1) * shards)
        slot = jnp.sum(members[c] * (ranks[part, :] + before), axis=0, keepdims=True).astype(jnp.int32)
        before = before + sums[part, :]
        row = c * tile + lax.broadcasted_iota(jnp.int32, (1, tile), 1)
        total = total + scatter_term(slot, (row, goals[c] & (rows - 1)), groups)
    return total


def scatter_term(at, values, groups):
    high = selector(at >> 7, groups)
    parts = []
    for value in values:
        for part in (value >> 6, value & 63):
            parts.append(high * jnp.broadcast_to(part.astype(F32).astype(BF16), high.shape))
    left = jnp.concatenate(parts, axis=0)
    low = selector(at & 127, 128)
    return lax.dot_general(left, low, (((1,), (1,)), ((), ())), preferred_element_type=F32)


def joined(total, n, groups):
    high = total[2 * n * groups : (2 * n + 1) * groups, :]
    low = total[(2 * n + 1) * groups : (2 * n + 2) * groups, :]
    return (high * 64.0 + low).astype(jnp.int32)


def edges_kernel(place_ref, voxels_hbm, near_hbm, first_ref, last_ref, near_first, near_last, sems):
    rows = voxels_hbm.shape[0]
    extent = 2 * HALO
    copies = [
        pltpu.make_async_copy(source, target, sems.at[n])
        for n, (source, target) in enumerate(
            (
                (near_hbm.at[:, 0:HALO], near_first),
                (near_hbm.at[:, rows - HALO : rows], near_last),
                (voxels_hbm.at[0:extent, :], first_ref.at[0:extent, :]),
                (voxels_hbm.at[rows - extent : rows, :], last_ref.at[0:extent, :]),
            )
        )
    ]
    for copy in copies:
        copy.start()
    own = place_ref[0]
    lanes = lax.broadcasted_iota(jnp.int32, (1, HALO), 1)
    for n, (near_ref, out_ref, first) in enumerate(((near_first, first_ref, 0), (near_last, last_ref, rows - HALO))):
        copies[n].wait()
        near = near_ref[...]
        relative = jnp.where(near >= 0, near - (own * rows + first + lanes), ABSENT).astype(F32)
        pad = jnp.zeros((out_ref.shape[0] - extent - near.shape[0], HALO), F32)
        out_ref[extent:, :] = jnp.concatenate([relative, pad], axis=0).astype(BF16)
    copies[2].wait()
    copies[3].wait()


def inner_kernel(
    shards, place_ref, counts_ref, voxels_ref, near_ref, weight_hbm, linear_ref, destination_ref,
    act_ref, next_ref, perm_ref, high_ref, low_ref, turned_ref,
    weight_ref, even, odd, conv, sem,
):
    weights_in = pltpu.make_async_copy(weight_hbm, weight_ref, sem)
    weights_in.start()
    rows, channels = voxels_ref.shape
    own, before, count, after = device_counts(place_ref, counts_ref)
    groups = rows // 128
    total = slots_table(destination_ref, shards)
    perm_ref[...] = joined(total, 0, groups)
    high_ref[...] = total[2 * groups : 3 * groups, :]
    low_ref[...] = total[3 * groups :, :]
    for c in range(rows // BLOCK):
        live = live_lanes(c * BLOCK, BLOCK, rows, before, count, after)
        block = voxels_ref[c * BLOCK : (c + 1) * BLOCK, :].T
        act_ref[:, c * BLOCK : (c + 1) * BLOCK] = jnp.where(live, block.astype(F32), 0.0).astype(BF16)
    weights_in.wait()
    for layer in range(2):
        turn_weights(weight_ref, layer, turned_ref.at[layer])
    linear = linear_ref[0].T

    def gather(b, picked):
        first = (b - 1) * BLOCK
        targets = jnp.maximum(near_ref[:, columns(first + HALO)] - (own * rows + first), -1)
        gather_block(lambda at, n: act_ref[:, pl.ds(pl.multiple_of(first + at, HALO), n)], targets, picked)

    def convolve(b, picked):
        conv[:, columns(b * BLOCK)] = dot(turned_ref[0], picked[...]).astype(BF16)

    blocks = rows // BLOCK

    def step(t, _):
        gather(2 * t + 1, even)
        convolve(2 * t, odd)
        gather(2 * t + 2, odd)
        convolve(2 * t + 1, even)
        return 0

    lax.fori_loop(0, (blocks - 2) // 2, step, 0)
    gather(blocks - 1, even)
    convolve(blocks - 2, odd)
    convolve(blocks - 1, even)

    def norm(b):
        first = b * BLOCK - HALO
        live = live_lanes(first, BLOCK, rows, before, count, after)
        next_ref[:, columns(b * BLOCK)] = norm_block(
            act_ref[:, columns(first)], conv[:, columns(b * BLOCK)], linear, live
        )

    in_turn(1, blocks, norm)


def in_turn(first, last, body, most=16):
    count = last - first
    unroll = max(u for u in range(1, most + 1) if count % u == 0)

    def step(t, _):
        for u in range(unroll):
            body(first + t * unroll + u)
        return 0

    lax.fori_loop(0, count // unroll, step, 0)


def outer_kernel(
    place_ref, counts_ref, low_ref, high_ref, act_ref, inner_ref, near_ref, turned_ref, linear_ref,
    perm_ref, place_high_ref, place_low_ref, send_ref, even, odd, edge, edge_conv, padded, conv, last,
):
    channels, rows = act_ref.shape
    own, before, count, after = device_counts(place_ref, counts_ref)
    extent = 2 * HALO
    lanes = lax.broadcasted_iota(jnp.int32, (1, HALO), 1)

    def reached(halo_ref, base):
        relative = halo_ref[extent : extent + near_ref.shape[0], :].astype(F32).astype(jnp.int32)
        return jnp.where(relative == ABSENT, -1, relative + lanes + base)

    def masked(halo_ref, first):
        live = live_lanes(first, extent, rows, before, count, after)
        return jnp.where(live, halo_ref[0:extent, :].T.astype(F32), 0.0).astype(BF16)

    edges = (edge.at[:, 0:WINDOW], edge.at[:, WINDOW:])
    edges[0][:, 0:extent] = masked(low_ref, -extent)
    edges[0][:, extent:] = act_ref[:, 0:extent]
    edges[1][:, 0:extent] = act_ref[:, rows - extent : rows]
    edges[1][:, extent:] = masked(high_ref, rows)
    near = (
        jnp.concatenate(
            [reached(low_ref, HALO), jnp.maximum(near_ref[:, 0:HALO] - own * rows + extent, -1)], axis=1
        ),
        jnp.concatenate(
            [
                jnp.maximum(near_ref[:, rows - HALO : rows] - own * rows - (rows - extent), -1),
                reached(high_ref, 2 * HALO),
            ],
            axis=1,
        ),
    )
    blocks = rows // BLOCK
    padded[:, BLOCK:rows] = inner_ref[:, BLOCK:rows]

    def gather_edge(n, picked):
        gather_block(lambda at, size: edges[n][:, at : at + size], near[n], picked)

    def convolve_edge(n, picked):
        edge_conv[:, n * BLOCK : (n + 1) * BLOCK] = dot(turned_ref[0], picked[...]).astype(BF16)

    def norm_edge(n):
        at = n * rows
        live = live_lanes(at - HALO, BLOCK, rows, before, count, after)
        padded[:, at : at + BLOCK] = norm_block(
            edges[n][:, HALO : HALO + BLOCK], edge_conv[:, n * BLOCK : (n + 1) * BLOCK], linear_ref[0].T, live
        )

    def gather(b, picked):
        first = b * BLOCK
        targets = jnp.maximum(near_ref[:, columns(first)] - (own * rows + first - HALO), -1)
        gather_block(lambda at, n: padded[:, pl.ds(pl.multiple_of(first + at, HALO), n)], targets, picked)

    def convolve(b, picked):
        conv[:, columns(b * BLOCK)] = dot(turned_ref[1], picked[...]).astype(BF16)

    gather_edge(0, even)
    gather_edge(1, odd)
    convolve_edge(0, even)
    gather(1, even)
    convolve_edge(1, odd)

    def step(t, _):
        gather(2 * t + 2, odd)
        convolve(2 * t + 1, even)
        gather(2 * t + 3, even)
        convolve(2 * t + 2, odd)
        return 0

    lax.fori_loop(0, (blocks - 4) // 2, step, 0)
    norm_edge(0)
    norm_edge(1)
    gather(blocks - 2, odd)
    convolve(blocks - 3, even)
    gather(0, even)
    convolve(blocks - 2, odd)
    gather(blocks - 1, odd)
    convolve(0, even)
    convolve(blocks - 1, odd)
    linear = linear_ref[1].T

    def norm(b):
        first = b * BLOCK
        live = live_lanes(first, BLOCK, rows, before, count, after)
        last[:, columns(first)] = norm_block(
            padded[:, columns(first + HALO)], conv[:, columns(first)], linear, live
        )

    in_turn(0, blocks, norm)

    shards, depth, _ = send_ref.shape
    capacity = rows // shards
    pieces = BLOCK // capacity

    def store(b, block):
        for p in range(pieces):
            send_ref[b * pieces + p, 0:capacity, :] = block[p * capacity : (p + 1) * capacity, :]

    reorder(last, perm_ref, store)
    held = capacity // 128
    pad = jnp.zeros((depth - capacity - 2 * held, 128), F32)
    for d in range(shards):
        at = slice(d * held, (d + 1) * held)
        extra = jnp.concatenate([place_high_ref[at, :], place_low_ref[at, :], pad], axis=0)
        send_ref[d, capacity:, :] = extra.astype(BF16)


def reorder(source, from_ref, store, dots=6, unroll=16):
    channels, rows = source.shape
    windows = rows // WINDOW

    def one(b):
        pair = from_ref[pl.ds(b * 2, 2), :]
        wanted = jnp.concatenate([pair[0:1, :], pair[1:2, :]], axis=1)
        total = jnp.zeros((channels, BLOCK), F32)
        halves = [jnp.zeros((channels, 128), BF16) for _ in range(2)]
        lanes = [pair[h : h + 1, :] & 127 for h in range(2)]
        chunks = [jnp.broadcast_to((pair[h : h + 1, :] >> 7).astype(jnp.int16), (channels, 128)) for h in range(2)]
        rest = [(j, h) for j in range(dots * WINDOW // 128, rows // 128) for h in range(2)]
        done = 0
        for w in range(dots):
            total = total + dot(source[:, w * WINDOW : (w + 1) * WINDOW], selector(wanted - w * WINDOW, WINDOW))
            until = len(rest) * (w + 1) // dots
            for j, h in rest[done:until]:
                halves[h] = jnp.where(
                    chunks[h] == j, lane_pick(source[:, j * 128 : (j + 1) * 128], lanes[h]), halves[h]
                )
            done = until
        store(b, (total + jnp.concatenate(halves, axis=1).astype(F32)).astype(BF16).T)

    def step(t, _):
        for u in range(unroll):
            one(t * unroll + u)
        return 0

    lax.fori_loop(0, rows // BLOCK // unroll, step, 0)


def final_kernel(got_ref, out_hbm, out_ref, turned, from_ref, sems):
    rows = out_ref.shape[0]
    shards = got_ref.shape[0]
    groups = rows // 128
    capacity = rows // shards
    held = capacity // 128
    lanes = lax.broadcasted_iota(jnp.int32, (1, capacity), 1)
    total = jnp.zeros((2 * groups, 128), F32)
    for s in range(shards):
        turned[:, s * capacity : (s + 1) * capacity] = got_ref[s, 0:capacity, :].T
        extra = got_ref[s, capacity:, :].astype(F32)
        place = (extra[0:held, :] * 64.0 + extra[held : 2 * held, :]).astype(jnp.int32)
        place = jnp.concatenate([place[h : h + 1, :] for h in range(held)], axis=1)
        total = total + scatter_term(place, (s * capacity + lanes,), groups)
    from_ref[...] = joined(total, 0, groups)

    def copy(b):
        at = pl.ds(pl.multiple_of(b * BLOCK, BLOCK), BLOCK)
        return pltpu.make_async_copy(out_ref.at[at, :], out_hbm.at[at, :], sems.at[b])

    def store(b, block):
        out_ref[pl.ds(pl.multiple_of(b * BLOCK, BLOCK), BLOCK), :] = block
        copy(b).start()

    reorder(turned, from_ref, store)
    for b in range(rows // BLOCK):
        copy(b).wait()


def local(voxels, counts, neighbours, conv_weight, linear_weight, destination):
    rows, channels = voxels.shape
    offsets = neighbours.shape[0]
    both = ("wide", "narrow")
    shards = lax.axis_size(both)
    own = lax.axis_index(both)
    place = jnp.reshape(own, (1,)).astype(jnp.int32)
    extent = 2 * HALO
    struct = jax.ShapeDtypeStruct
    vmem = pl.BlockSpec(memory_space=VMEM)
    smem = pl.BlockSpec(memory_space=SMEM)
    hbm = pl.BlockSpec(memory_space=pltpu.HBM)

    packed = struct((extent + 32, channels), BF16)
    first, final = pl.pallas_call(
        edges_kernel,
        out_shape=(packed, packed),
        in_specs=[smem, hbm, hbm],
        out_specs=(vmem, vmem),
        scratch_shapes=[VMEM((offsets, HALO), jnp.int32), VMEM((offsets, HALO), jnp.int32), pltpu.SemaphoreType.DMA((4,))],
        cost_estimate=pl.CostEstimate(flops=20_000_000_000, bytes_accessed=500_000, transcendentals=0),
        compiler_params=params(60),
        name="edges",
    )(place, voxels, neighbours)
    forward = [(i, i + 1) for i in range(shards - 1)]
    backward = [(target, source) for source, target in forward]
    low = lax.ppermute(final, both, forward)
    high = lax.ppermute(first, both, backward)

    table = (rows // 128, 128)
    padded = (channels, rows + BLOCK)
    picked = VMEM((offsets * channels, BLOCK), BF16)
    turned = (2, channels, offsets * channels)
    act, inner, perm, place_high, place_low, weights = pl.pallas_call(
        functools.partial(inner_kernel, shards),
        out_shape=(
            struct((channels, rows), BF16), struct(padded, BF16), struct(table, jnp.int32), struct(table, F32),
            struct(table, F32), struct(turned, BF16),
        ),
        in_specs=[smem, smem, vmem, vmem, hbm, vmem, vmem],
        out_specs=(vmem,) * 6,
        scratch_shapes=[
            VMEM(conv_weight.shape, BF16), picked, picked, VMEM(padded, BF16), pltpu.SemaphoreType.DMA,
        ],
        compiler_params=params(),
        cost_estimate=pl.CostEstimate(flops=20_000_000_000, bytes_accessed=6_000_000, transcendentals=0),
        name="first_layer",
    )(place, counts, voxels, neighbours, conv_weight, linear_weight, destination.reshape(1, rows))

    depth = rows // shards + 16
    send = pl.pallas_call(
        outer_kernel,
        out_shape=struct((shards, depth, channels), BF16),
        in_specs=[smem, smem] + [vmem] * 10,
        out_specs=vmem,
        scratch_shapes=[
            picked,
            picked,
            VMEM((channels, 2 * WINDOW), BF16),
            VMEM((channels, 2 * BLOCK), BF16),
            VMEM(padded, BF16),
            VMEM((channels, rows), BF16),
            VMEM((channels, rows), BF16),
        ],
        compiler_params=params(),
        cost_estimate=pl.CostEstimate(flops=30_000_000_000, bytes_accessed=8_000_000, transcendentals=0),
        name="second_layer",
    )(place, counts, low, high, act, inner, neighbours, weights, linear_weight, perm, place_high, place_low)

    got = lax.all_to_all(send, both, split_axis=0, concat_axis=0, tiled=True)
    return pl.pallas_call(
        final_kernel,
        out_shape=struct((rows, channels), BF16),
        in_specs=[vmem],
        out_specs=hbm,
        scratch_shapes=[
            VMEM((rows, channels), BF16), VMEM((channels, rows), BF16), VMEM(table, jnp.int32),
            pltpu.SemaphoreType.DMA((rows // BLOCK,)),
        ],
        compiler_params=params(),
        name="hilbert_order",
    )(got)


def solution(mesh):
    in_specs = (
        P(("groups", "wide", "narrow"), None),
        P("groups"),
        P(None, ("groups", "wide", "narrow")),
        P(),
        P(),
        P(("groups", "wide", "narrow")),
    )
    out_specs = P(("groups", "wide", "narrow"), None)
    return jax.shard_map(local, mesh=mesh, in_specs=in_specs, out_specs=out_specs, check_vma=False)
```

```python
import functools

import jax
import jax.numpy as jnp
from jax import lax
from jax.experimental import pallas as pl
from jax.experimental.pallas import tpu as pltpu
from jax.sharding import PartitionSpec as P

HALO = 128
BLOCK = 256
WINDOW = 512
BF16 = jnp.bfloat16
F32 = jnp.float32
ABSENT = 256
SMEM = pltpu.SMEM
VMEM = pltpu.VMEM


def params(mebibytes=48):
    return pltpu.CompilerParams(vmem_limit_bytes=mebibytes * 1024 * 1024)


def selector(row, depth):
    shape = (depth, row.shape[1])
    places = lax.broadcasted_iota(jnp.int16, shape, 0)
    wanted = jnp.broadcast_to(row.astype(jnp.int16), shape)
    return jnp.where(places == wanted, BF16(1), BF16(0))


def dot(a, b):
    return jnp.dot(a, b, preferred_element_type=F32)


def live_lanes(first, width, rows, before, own, after):
    at = first + lax.broadcasted_iota(jnp.int32, (1, width), 1)
    limit = jnp.where(at < 0, before - rows, jnp.where(at < rows, own, after + rows))
    return at < limit


def lane_pick(block, lanes):
    numbers = lax.GatherDimensionNumbers(
        offset_dims=(), collapsed_slice_dims=(1,), start_index_map=(1,),
        operand_batching_dims=(0,), start_indices_batching_dims=(0,),
    )
    index = jnp.broadcast_to(lanes.astype(jnp.int16), block.shape)
    return lax.gather(block, index[..., None], numbers, (1, 1), mode=lax.GatherScatterMode.PROMISE_IN_BOUNDS)


def gather_block(window, targets, picked):
    offsets = targets.shape[0]
    channels = picked.shape[0] // offsets
    static = {0: 0, offsets // 2: HALO, offsets - 1: 2 * HALO}
    turn = 0
    for k in range(offsets):
        at = slice(k * channels, (k + 1) * channels)
        if k in static:
            picked[at, :] = window(static[k], BLOCK)
            continue
        turn += 1
        row = targets[k : k + 1, :]
        if turn % 2:
            picked[at, :] = dot(window(0, WINDOW), selector(row, WINDOW)).astype(BF16)
            continue
        for half in range(2):
            part = row[:, half * HALO : (half + 1) * HALO]
            lanes = part & (HALO - 1)
            chunk = jnp.broadcast_to((part >> 7).astype(jnp.int16), (channels, HALO))
            total = jnp.zeros((channels, HALO), BF16)
            for j in range(half, half + 3):
                total = jnp.where(chunk == j, lane_pick(window(j * HALO, HALO), lanes), total)
            picked[at, half * HALO : (half + 1) * HALO] = total


def norm_block(current, convolved, linear, live):
    projected = dot(linear, convolved)
    average = jnp.mean(projected, axis=0, keepdims=True)
    centred = projected - average
    spread = jnp.mean(centred * centred, axis=0, keepdims=True)
    summed = current.astype(F32) + centred * lax.rsqrt(spread + 1e-05)
    return jnp.where(live, summed, 0.0).astype(BF16)


def columns(start):
    return pl.ds(pl.multiple_of(start, HALO), BLOCK)


def turn_weights(weight_ref, layer, turned):
    offsets, channels = weight_ref.shape[1], weight_ref.shape[2]
    for k in range(offsets):
        turned[:, k * channels : (k + 1) * channels] = weight_ref[layer, k].T


def device_counts(place_ref, counts_ref):
    own = place_ref[0]
    last = counts_ref.shape[0] - 1
    before = jnp.where(own > 0, counts_ref[jnp.maximum(own - 1, 0)], 0)
    after = jnp.where(own < last, counts_ref[jnp.minimum(own + 1, last)], 0)
    return own, before, counts_ref[own], after


def slots_table(destination_ref, shards):
    rows = destination_ref.shape[1]
    capacity = rows // shards
    groups = rows // 128
    tile = 256
    earlier = (
        lax.broadcasted_iota(jnp.int32, (tile, tile), 0) < lax.broadcasted_iota(jnp.int32, (tile, tile), 1)
    ).astype(F32).astype(BF16)
    devices = lax.broadcasted_iota(jnp.int32, (shards, tile), 0)
    tiles = rows // tile
    goals = [destination_ref[:, c * tile : (c + 1) * tile] for c in range(tiles)]
    members = [
        (jnp.broadcast_to(goal >> (rows.bit_length() - 1), (shards, tile)) == devices).astype(F32) for goal in goals
    ]
    stacked = jnp.concatenate([member.astype(BF16) for member in members], axis=0)
    ranks = dot(stacked, earlier)
    sums = dot(stacked, jnp.ones((tile, tile), BF16))
    before = (devices * capacity).astype(F32)
    total = jnp.zeros((4 * groups, 128), F32)
    for c in range(tiles):
        part = slice(c * shards, (c + 1) * shards)
        slot = jnp.sum(members[c] * (ranks[part, :] + before), axis=0, keepdims=True).astype(jnp.int32)
        before = before + sums[part, :]
        row = c * tile + lax.broadcasted_iota(jnp.int32, (1, tile), 1)
        total = total + scatter_term(slot, (row, goals[c] & (rows - 1)), groups)
    return total


def scatter_term(at, values, groups):
    high = selector(at >> 7, groups)
    parts = []
    for value in values:
        for part in (value >> 6, value & 63):
            parts.append(high * jnp.broadcast_to(part.astype(F32).astype(BF16), high.shape))
    left = jnp.concatenate(parts, axis=0)
    low = selector(at & 127, 128)
    return lax.dot_general(left, low, (((1,), (1,)), ((), ())), preferred_element_type=F32)


def joined(total, n, groups):
    high = total[2 * n * groups : (2 * n + 1) * groups, :]
    low = total[(2 * n + 1) * groups : (2 * n + 2) * groups, :]
    return (high * 64.0 + low).astype(jnp.int32)


def edges_kernel(place_ref, voxels_hbm, near_hbm, pair_ref, side_ref, near_pair, near_side, sems):
    rows = voxels_hbm.shape[0]
    extent = 2 * HALO
    own = place_ref[0]
    odd = own & 1
    parts = ((pair_ref, near_pair, 1 - odd), (side_ref, near_side, odd))
    copies = []
    for n, (out_ref, near_ref, upper) in enumerate(parts):
        near_at = pl.ds(pl.multiple_of(upper * (rows - HALO), HALO), HALO)
        voxels_at = pl.ds(pl.multiple_of(upper * (rows - extent), extent), extent)
        copies.append(pltpu.make_async_copy(near_hbm.at[:, near_at], near_ref, sems.at[n]))
        copies.append(pltpu.make_async_copy(voxels_hbm.at[voxels_at, :], out_ref.at[0:extent, :], sems.at[2 + n]))
    for copy in copies:
        copy.start()
    lanes = lax.broadcasted_iota(jnp.int32, (1, HALO), 1)
    for n, (out_ref, near_ref, upper) in enumerate(parts):
        copies[2 * n].wait()
        near = near_ref[...]
        relative = jnp.where(near >= 0, near - (own * rows + upper * (rows - HALO) + lanes), ABSENT).astype(F32)
        pad = jnp.zeros((out_ref.shape[0] - extent - near.shape[0], HALO), F32)
        out_ref[extent:, :] = jnp.concatenate([relative, pad], axis=0).astype(BF16)
    copies[1].wait()
    copies[3].wait()


def inner_kernel(
    shards, place_ref, counts_ref, voxels_ref, near_ref, weight_hbm, linear_ref, destination_ref,
    act_ref, next_ref, perm_ref, high_ref, low_ref, turned_ref,
    weight_ref, even, odd, conv, sems,
):
    weights_in = [
        pltpu.make_async_copy(weight_hbm.at[layer], weight_ref.at[layer], sems.at[layer]) for layer in range(2)
    ]
    for copy in weights_in:
        copy.start()
    rows, channels = voxels_ref.shape
    own, before, count, after = device_counts(place_ref, counts_ref)
    groups = rows // 128
    total = slots_table(destination_ref, shards)
    perm_ref[...] = joined(total, 0, groups)
    high_ref[...] = total[2 * groups : 3 * groups, :]
    low_ref[...] = total[3 * groups :, :]
    for c in range(rows // BLOCK):
        live = live_lanes(c * BLOCK, BLOCK, rows, before, count, after)
        block = voxels_ref[c * BLOCK : (c + 1) * BLOCK, :].T
        act_ref[:, c * BLOCK : (c + 1) * BLOCK] = jnp.where(live, block.astype(F32), 0.0).astype(BF16)
    weights_in[0].wait()
    turn_weights(weight_ref, 0, turned_ref.at[0])
    linear = linear_ref[0].T

    def gather(b, picked):
        first = (b - 1) * BLOCK
        targets = jnp.maximum(near_ref[:, columns(first + HALO)] - (own * rows + first), -1)
        gather_block(lambda at, n: act_ref[:, pl.ds(pl.multiple_of(first + at, HALO), n)], targets, picked)

    def convolve(b, picked):
        conv[:, columns(b * BLOCK)] = dot(turned_ref[0], picked[...]).astype(BF16)

    blocks = rows // BLOCK

    def step(t, _):
        gather(2 * t + 1, even)
        convolve(2 * t, odd)
        gather(2 * t + 2, odd)
        convolve(2 * t + 1, even)
        return 0

    lax.fori_loop(0, (blocks - 2) // 2, step, 0)
    gather(blocks - 1, even)
    convolve(blocks - 2, odd)
    convolve(blocks - 1, even)

    def norm(b):
        first = b * BLOCK - HALO
        live = live_lanes(first, BLOCK, rows, before, count, after)
        next_ref[:, columns(b * BLOCK)] = norm_block(
            act_ref[:, columns(first)], conv[:, columns(b * BLOCK)], linear, live
        )

    in_turn(1, blocks, norm)
    weights_in[1].wait()
    turn_weights(weight_ref, 1, turned_ref.at[1])


def in_turn(first, last, body, most=16):
    count = last - first
    unroll = max(u for u in range(1, most + 1) if count % u == 0)

    def step(t, _):
        for u in range(unroll):
            body(first + t * unroll + u)
        return 0

    lax.fori_loop(0, count // unroll, step, 0)


def outer_kernel(
    place_ref, counts_ref, pair_ref, side_ref, act_ref, inner_ref, near_ref, turned_ref, linear_ref,
    perm_ref, place_high_ref, place_low_ref, send_ref, low_ref, high_ref, even, odd, edge, edge_conv, padded, conv, last,
):
    channels, rows = act_ref.shape
    own, before, count, after = device_counts(place_ref, counts_ref)

    @pl.when(own & 1 == 0)
    def _():
        low_ref[...] = side_ref[...]
        high_ref[...] = pair_ref[...]

    @pl.when(own & 1 == 1)
    def _():
        low_ref[...] = pair_ref[...]
        high_ref[...] = side_ref[...]

    extent = 2 * HALO
    lanes = lax.broadcasted_iota(jnp.int32, (1, HALO), 1)

    def reached(halo_ref, base):
        relative = halo_ref[extent : extent + near_ref.shape[0], :].astype(F32).astype(jnp.int32)
        return jnp.where(relative == ABSENT, -1, relative + lanes + base)

    def masked(halo_ref, first):
        live = live_lanes(first, extent, rows, before, count, after)
        return jnp.where(live, halo_ref[0:extent, :].T.astype(F32), 0.0).astype(BF16)

    edges = (edge.at[:, 0:WINDOW], edge.at[:, WINDOW:])
    edges[0][:, 0:extent] = masked(low_ref, -extent)
    edges[0][:, extent:] = act_ref[:, 0:extent]
    edges[1][:, 0:extent] = act_ref[:, rows - extent : rows]
    edges[1][:, extent:] = masked(high_ref, rows)
    near = (
        jnp.concatenate(
            [reached(low_ref, HALO), jnp.maximum(near_ref[:, 0:HALO] - own * rows + extent, -1)], axis=1
        ),
        jnp.concatenate(
            [
                jnp.maximum(near_ref[:, rows - HALO : rows] - own * rows - (rows - extent), -1),
                reached(high_ref, 2 * HALO),
            ],
            axis=1,
        ),
    )
    blocks = rows // BLOCK
    padded[:, BLOCK:rows] = inner_ref[:, BLOCK:rows]

    def gather_edge(n, picked):
        gather_block(lambda at, size: edges[n][:, at : at + size], near[n], picked)

    def convolve_edge(n, picked):
        edge_conv[:, n * BLOCK : (n + 1) * BLOCK] = dot(turned_ref[0], picked[...]).astype(BF16)

    def norm_edge(n):
        at = n * rows
        live = live_lanes(at - HALO, BLOCK, rows, before, count, after)
        padded[:, at : at + BLOCK] = norm_block(
            edges[n][:, HALO : HALO + BLOCK], edge_conv[:, n * BLOCK : (n + 1) * BLOCK], linear_ref[0].T, live
        )

    def gather(b, picked):
        first = b * BLOCK
        targets = jnp.maximum(near_ref[:, columns(first)] - (own * rows + first - HALO), -1)
        gather_block(lambda at, n: padded[:, pl.ds(pl.multiple_of(first + at, HALO), n)], targets, picked)

    def convolve(b, picked):
        conv[:, columns(b * BLOCK)] = dot(turned_ref[1], picked[...]).astype(BF16)

    gather_edge(0, even)
    gather_edge(1, odd)
    convolve_edge(0, even)
    gather(1, even)
    convolve_edge(1, odd)

    def step(t, _):
        gather(2 * t + 2, odd)
        convolve(2 * t + 1, even)
        gather(2 * t + 3, even)
        convolve(2 * t + 2, odd)
        return 0

    lax.fori_loop(0, (blocks - 4) // 2, step, 0)
    norm_edge(0)
    norm_edge(1)
    gather(blocks - 2, odd)
    convolve(blocks - 3, even)
    gather(0, even)
    convolve(blocks - 2, odd)
    gather(blocks - 1, odd)
    convolve(0, even)
    convolve(blocks - 1, odd)
    linear = linear_ref[1].T

    def norm(b):
        first = b * BLOCK
        live = live_lanes(first, BLOCK, rows, before, count, after)
        last[:, columns(first)] = norm_block(
            padded[:, columns(first + HALO)], conv[:, columns(first)], linear, live
        )

    in_turn(0, blocks, norm)

    shards, depth, _ = send_ref.shape
    capacity = rows // shards
    pieces = BLOCK // capacity

    def store(b, block):
        for p in range(pieces):
            send_ref[b * pieces + p, 0:capacity, :] = block[p * capacity : (p + 1) * capacity, :]

    reorder(last, perm_ref, store)
    held = capacity // 128
    pad = jnp.zeros((depth - capacity - 2 * held, 128), F32)
    for d in range(shards):
        at = slice(d * held, (d + 1) * held)
        extra = jnp.concatenate([place_high_ref[at, :], place_low_ref[at, :], pad], axis=0)
        send_ref[d, capacity:, :] = extra.astype(BF16)


def reorder(source, from_ref, store, dots=6, unroll=16):
    channels, rows = source.shape
    windows = rows // WINDOW

    def one(b):
        pair = from_ref[pl.ds(b * 2, 2), :]
        wanted = jnp.concatenate([pair[0:1, :], pair[1:2, :]], axis=1)
        total = jnp.zeros((channels, BLOCK), F32)
        halves = [jnp.zeros((channels, 128), BF16) for _ in range(2)]
        lanes = [pair[h : h + 1, :] & 127 for h in range(2)]
        chunks = [jnp.broadcast_to((pair[h : h + 1, :] >> 7).astype(jnp.int16), (channels, 128)) for h in range(2)]
        rest = [(j, h) for j in range(dots * WINDOW // 128, rows // 128) for h in range(2)]
        done = 0
        for w in range(dots):
            total = total + dot(source[:, w * WINDOW : (w + 1) * WINDOW], selector(wanted - w * WINDOW, WINDOW))
            until = len(rest) * (w + 1) // dots
            for j, h in rest[done:until]:
                halves[h] = jnp.where(
                    chunks[h] == j, lane_pick(source[:, j * 128 : (j + 1) * 128], lanes[h]), halves[h]
                )
            done = until
        store(b, (total + jnp.concatenate(halves, axis=1).astype(F32)).astype(BF16).T)

    def step(t, _):
        for u in range(unroll):
            one(t * unroll + u)
        return 0

    lax.fori_loop(0, rows // BLOCK // unroll, step, 0)


def final_kernel(got_ref, out_hbm, out_ref, turned, from_ref, sems):
    rows = out_ref.shape[0]
    shards = got_ref.shape[0]
    groups = rows // 128
    capacity = rows // shards
    held = capacity // 128
    lanes = lax.broadcasted_iota(jnp.int32, (1, capacity), 1)
    total = jnp.zeros((2 * groups, 128), F32)
    for s in range(shards):
        turned[:, s * capacity : (s + 1) * capacity] = got_ref[s, 0:capacity, :].T
        extra = got_ref[s, capacity:, :].astype(F32)
        place = (extra[0:held, :] * 64.0 + extra[held : 2 * held, :]).astype(jnp.int32)
        place = jnp.concatenate([place[h : h + 1, :] for h in range(held)], axis=1)
        total = total + scatter_term(place, (s * capacity + lanes,), groups)
    from_ref[...] = joined(total, 0, groups)

    def copy(b):
        at = pl.ds(pl.multiple_of(b * BLOCK, BLOCK), BLOCK)
        return pltpu.make_async_copy(out_ref.at[at, :], out_hbm.at[at, :], sems.at[b])

    def store(b, block):
        out_ref[pl.ds(pl.multiple_of(b * BLOCK, BLOCK), BLOCK), :] = block
        copy(b).start()

    reorder(turned, from_ref, store)
    for b in range(rows // BLOCK):
        copy(b).wait()


def local(voxels, counts, neighbours, conv_weight, linear_weight, destination):
    rows, channels = voxels.shape
    offsets = neighbours.shape[0]
    both = ("wide", "narrow")
    shards = lax.axis_size(both)
    own = lax.axis_index(both)
    place = jnp.reshape(own, (1,)).astype(jnp.int32)
    extent = 2 * HALO
    struct = jax.ShapeDtypeStruct
    vmem = pl.BlockSpec(memory_space=VMEM)
    smem = pl.BlockSpec(memory_space=SMEM)
    hbm = pl.BlockSpec(memory_space=pltpu.HBM)

    packed = struct((extent + 32, channels), BF16)
    to_pair, to_side = pl.pallas_call(
        edges_kernel,
        out_shape=(packed, packed),
        in_specs=[smem, hbm, hbm],
        out_specs=(vmem, vmem),
        scratch_shapes=[VMEM((offsets, HALO), jnp.int32), VMEM((offsets, HALO), jnp.int32), pltpu.SemaphoreType.DMA((4,))],
        cost_estimate=pl.CostEstimate(flops=20_000_000_000, bytes_accessed=500_000, transcendentals=0),
        compiler_params=params(60),
        name="edges",
    )(place, voxels, neighbours)
    others = [(0, 0), (shards - 1, shards - 1)]
    for i in range(1, shards - 1, 2):
        others += [(i, i + 1), (i + 1, i)]
    side = lax.ppermute(to_side, both, others)
    pair = lax.ppermute(to_pair, both, [(i, i ^ 1) for i in range(shards)])

    table = (rows // 128, 128)
    padded = (channels, rows + BLOCK)
    picked = VMEM((offsets * channels, BLOCK), BF16)
    turned = (2, channels, offsets * channels)
    act, inner, perm, place_high, place_low, weights = pl.pallas_call(
        functools.partial(inner_kernel, shards),
        out_shape=(
            struct((channels, rows), BF16), struct(padded, BF16), struct(table, jnp.int32), struct(table, F32),
            struct(table, F32), struct(turned, BF16),
        ),
        in_specs=[smem, smem, vmem, vmem, hbm, vmem, vmem],
        out_specs=(vmem,) * 6,
        scratch_shapes=[
            VMEM(conv_weight.shape, BF16), picked, picked, VMEM(padded, BF16), pltpu.SemaphoreType.DMA((2,)),
        ],
        compiler_params=params(),
        cost_estimate=pl.CostEstimate(flops=20_000_000_000, bytes_accessed=6_000_000, transcendentals=0),
        name="first_layer",
    )(place, counts, voxels, neighbours, conv_weight, linear_weight, destination.reshape(1, rows))

    depth = rows // shards + 16
    send = pl.pallas_call(
        outer_kernel,
        out_shape=struct((shards, depth, channels), BF16),
        in_specs=[smem, smem] + [vmem] * 10,
        out_specs=vmem,
        scratch_shapes=[
            VMEM(packed.shape, BF16),
            VMEM(packed.shape, BF16),
            picked,
            picked,
            VMEM((channels, 2 * WINDOW), BF16),
            VMEM((channels, 2 * BLOCK), BF16),
            VMEM(padded, BF16),
            VMEM((channels, rows), BF16),
            VMEM((channels, rows), BF16),
        ],
        compiler_params=params(),
        cost_estimate=pl.CostEstimate(flops=30_000_000_000, bytes_accessed=8_000_000, transcendentals=0),
        name="second_layer",
    )(place, counts, pair, side, act, inner, neighbours, weights, linear_weight, perm, place_high, place_low)

    got = lax.all_to_all(send, both, split_axis=0, concat_axis=0, tiled=True)
    return pl.pallas_call(
        final_kernel,
        out_shape=struct((rows, channels), BF16),
        in_specs=[vmem],
        out_specs=hbm,
        scratch_shapes=[
            VMEM((rows, channels), BF16), VMEM((channels, rows), BF16), VMEM(table, jnp.int32),
            pltpu.SemaphoreType.DMA((rows // BLOCK,)),
        ],
        compiler_params=params(),
        name="hilbert_order",
    )(got)


def solution(mesh):
    in_specs = (
        P(("groups", "wide", "narrow"), None),
        P("groups"),
        P(None, ("groups", "wide", "narrow")),
        P(),
        P(),
        P(("groups", "wide", "narrow")),
    )
    out_specs = P(("groups", "wide", "narrow"), None)
    return jax.shard_map(local, mesh=mesh, in_specs=in_specs, out_specs=out_specs, check_vma=False)
```

```python
import functools

import jax
import jax.numpy as jnp
from jax import lax
from jax.experimental import pallas as pl
from jax.experimental.pallas import tpu as pltpu
from jax.sharding import PartitionSpec as P

HALO = 128
BLOCK = 256
WINDOW = 512
BF16 = jnp.bfloat16
F32 = jnp.float32
ABSENT = 256
SMEM = pltpu.SMEM
VMEM = pltpu.VMEM


def params(mebibytes=48):
    return pltpu.CompilerParams(vmem_limit_bytes=mebibytes * 1024 * 1024)


def selector(row, depth):
    shape = (depth, row.shape[1])
    places = lax.broadcasted_iota(jnp.int16, shape, 0)
    wanted = jnp.broadcast_to(row.astype(jnp.int16), shape)
    return jnp.where(places == wanted, BF16(1), BF16(0))


def dot(a, b):
    return jnp.dot(a, b, preferred_element_type=F32)


def live_lanes(first, width, rows, before, own, after):
    at = first + lax.broadcasted_iota(jnp.int32, (1, width), 1)
    limit = jnp.where(at < 0, before - rows, jnp.where(at < rows, own, after + rows))
    return at < limit


def lane_pick(block, lanes):
    numbers = lax.GatherDimensionNumbers(
        offset_dims=(), collapsed_slice_dims=(1,), start_index_map=(1,),
        operand_batching_dims=(0,), start_indices_batching_dims=(0,),
    )
    index = jnp.broadcast_to(lanes.astype(jnp.int16), block.shape)
    return lax.gather(block, index[..., None], numbers, (1, 1), mode=lax.GatherScatterMode.PROMISE_IN_BOUNDS)


def gather_block(window, targets, picked):
    offsets = targets.shape[0]
    channels = picked.shape[0] // offsets
    static = {0: 0, offsets // 2: HALO, offsets - 1: 2 * HALO}
    turn = 0
    for k in range(offsets):
        at = slice(k * channels, (k + 1) * channels)
        if k in static:
            picked[at, :] = window(static[k], BLOCK)
            continue
        turn += 1
        row = targets[k : k + 1, :]
        if turn % 2:
            picked[at, :] = dot(window(0, WINDOW), selector(row, WINDOW)).astype(BF16)
            continue
        for half in range(2):
            part = row[:, half * HALO : (half + 1) * HALO]
            lanes = part & (HALO - 1)
            chunk = jnp.broadcast_to((part >> 7).astype(jnp.int16), (channels, HALO))
            total = jnp.zeros((channels, HALO), BF16)
            for j in range(half, half + 3):
                total = jnp.where(chunk == j, lane_pick(window(j * HALO, HALO), lanes), total)
            picked[at, half * HALO : (half + 1) * HALO] = total


def norm_block(current, convolved, linear, live):
    projected = dot(linear, convolved)
    average = jnp.mean(projected, axis=0, keepdims=True)
    centred = projected - average
    spread = jnp.mean(centred * centred, axis=0, keepdims=True)
    summed = current.astype(F32) + centred * lax.rsqrt(spread + 1e-05)
    return jnp.where(live, summed, 0.0).astype(BF16)


def columns(start):
    return pl.ds(pl.multiple_of(start, HALO), BLOCK)


def turn_weights(weight_ref, layer, turned):
    offsets, channels = weight_ref.shape[1], weight_ref.shape[2]
    for k in range(offsets):
        turned[:, k * channels : (k + 1) * channels] = weight_ref[layer, k].T


def device_counts(place_ref, counts_ref):
    own = place_ref[0]
    last = counts_ref.shape[0] - 1
    before = jnp.where(own > 0, counts_ref[jnp.maximum(own - 1, 0)], 0)
    after = jnp.where(own < last, counts_ref[jnp.minimum(own + 1, last)], 0)
    return own, before, counts_ref[own], after


def slots_table(destination_ref, shards):
    rows = destination_ref.shape[1]
    capacity = rows // shards
    groups = rows // 128
    tile = 256
    earlier = (
        lax.broadcasted_iota(jnp.int32, (tile, tile), 0) < lax.broadcasted_iota(jnp.int32, (tile, tile), 1)
    ).astype(F32).astype(BF16)
    devices = lax.broadcasted_iota(jnp.int32, (shards, tile), 0)
    tiles = rows // tile
    goals = [destination_ref[:, c * tile : (c + 1) * tile] for c in range(tiles)]
    members = [
        (jnp.broadcast_to(goal >> (rows.bit_length() - 1), (shards, tile)) == devices).astype(F32) for goal in goals
    ]
    stacked = jnp.concatenate([member.astype(BF16) for member in members], axis=0)
    ranks = dot(stacked, earlier)
    sums = dot(stacked, jnp.ones((tile, tile), BF16))
    before = (devices * capacity).astype(F32)
    total = jnp.zeros((4 * groups, 128), F32)
    for c in range(tiles):
        part = slice(c * shards, (c + 1) * shards)
        slot = jnp.sum(members[c] * (ranks[part, :] + before), axis=0, keepdims=True).astype(jnp.int32)
        before = before + sums[part, :]
        row = c * tile + lax.broadcasted_iota(jnp.int32, (1, tile), 1)
        total = total + scatter_term(slot, (row, goals[c] & (rows - 1)), groups)
    return total


def scatter_term(at, values, groups):
    high = selector(at >> 7, groups)
    parts = []
    for value in values:
        for part in (value >> 6, value & 63):
            parts.append(high * jnp.broadcast_to(part.astype(F32).astype(BF16), high.shape))
    left = jnp.concatenate(parts, axis=0)
    low = selector(at & 127, 128)
    return lax.dot_general(left, low, (((1,), (1,)), ((), ())), preferred_element_type=F32)


def joined(total, n, groups):
    high = total[2 * n * groups : (2 * n + 1) * groups, :]
    low = total[(2 * n + 1) * groups : (2 * n + 2) * groups, :]
    return (high * 64.0 + low).astype(jnp.int32)


def edges_kernel(place_ref, voxels_hbm, near_hbm, pair_ref, side_ref, near_pair, near_side, sems):
    rows = voxels_hbm.shape[0]
    extent = 2 * HALO
    own = place_ref[0]
    odd = own & 1
    parts = ((pair_ref, near_pair, 1 - odd), (side_ref, near_side, odd))
    copies = []
    for n, (out_ref, near_ref, upper) in enumerate(parts):
        near_at = pl.ds(pl.multiple_of(upper * (rows - HALO), HALO), HALO)
        voxels_at = pl.ds(pl.multiple_of(upper * (rows - extent), extent), extent)
        copies.append(pltpu.make_async_copy(near_hbm.at[:, near_at], near_ref, sems.at[n]))
        copies.append(pltpu.make_async_copy(voxels_hbm.at[voxels_at, :], out_ref.at[0:extent, :], sems.at[2 + n]))
    for copy in copies:
        copy.start()
    lanes = lax.broadcasted_iota(jnp.int32, (1, HALO), 1)
    for n, (out_ref, near_ref, upper) in enumerate(parts):
        copies[2 * n].wait()
        near = near_ref[...]
        relative = jnp.where(near >= 0, near - (own * rows + upper * (rows - HALO) + lanes), ABSENT).astype(F32)
        pad = jnp.zeros((out_ref.shape[0] - extent - near.shape[0], HALO), F32)
        out_ref[extent:, :] = jnp.concatenate([relative, pad], axis=0).astype(BF16)
    copies[1].wait()
    copies[3].wait()


def inner_kernel(
    shards, place_ref, counts_ref, voxels_ref, near_ref, weight_hbm, linear_ref, destination_ref,
    act_ref, next_ref, perm_ref, high_ref, low_ref, turned_ref,
    weight_ref, even, odd, conv, sems,
):
    weights_in = [
        pltpu.make_async_copy(weight_hbm.at[layer], weight_ref.at[layer], sems.at[layer]) for layer in range(2)
    ]
    weights_in[0].start()
    rows, channels = voxels_ref.shape
    own, before, count, after = device_counts(place_ref, counts_ref)
    groups = rows // 128
    total = slots_table(destination_ref, shards)
    perm_ref[...] = joined(total, 0, groups)
    high_ref[...] = total[2 * groups : 3 * groups, :]
    low_ref[...] = total[3 * groups :, :]
    for c in range(rows // BLOCK):
        live = live_lanes(c * BLOCK, BLOCK, rows, before, count, after)
        block = voxels_ref[c * BLOCK : (c + 1) * BLOCK, :].T
        act_ref[:, c * BLOCK : (c + 1) * BLOCK] = jnp.where(live, block.astype(F32), 0.0).astype(BF16)
    linear = linear_ref[0].T

    def gather(b, picked):
        first = (b - 1) * BLOCK
        targets = jnp.maximum(near_ref[:, columns(first + HALO)] - (own * rows + first), -1)
        gather_block(lambda at, n: act_ref[:, pl.ds(pl.multiple_of(first + at, HALO), n)], targets, picked)

    def convolve(b, picked):
        conv[:, columns(b * BLOCK)] = dot(turned_ref[0], picked[...]).astype(BF16)

    blocks = rows // BLOCK
    gather(1, even)
    weights_in[0].wait()
    weights_in[1].start()
    turn_weights(weight_ref, 0, turned_ref.at[0])

    def step(t, _):
        gather(2 * t + 2, odd)
        convolve(2 * t + 1, even)
        gather(2 * t + 3, even)
        convolve(2 * t + 2, odd)
        return 0

    lax.fori_loop(0, (blocks - 2) // 2, step, 0)
    convolve(blocks - 1, even)

    def norm(b):
        first = b * BLOCK - HALO
        live = live_lanes(first, BLOCK, rows, before, count, after)
        next_ref[:, columns(b * BLOCK)] = norm_block(
            act_ref[:, columns(first)], conv[:, columns(b * BLOCK)], linear, live
        )

    in_turn(1, blocks, norm)
    weights_in[1].wait()
    turn_weights(weight_ref, 1, turned_ref.at[1])


def in_turn(first, last, body, most=16):
    count = last - first
    unroll = max(u for u in range(1, most + 1) if count % u == 0)

    def step(t, _):
        for u in range(unroll):
            body(first + t * unroll + u)
        return 0

    lax.fori_loop(0, count // unroll, step, 0)


def outer_kernel(
    place_ref, counts_ref, pair_ref, side_ref, act_ref, inner_ref, near_ref, turned_ref, linear_ref,
    perm_ref, place_high_ref, place_low_ref, send_ref, low_ref, high_ref, even, odd, edge, edge_conv, padded, conv, last,
):
    channels, rows = act_ref.shape
    own, before, count, after = device_counts(place_ref, counts_ref)

    @pl.when(own & 1 == 0)
    def _():
        low_ref[...] = side_ref[...]
        high_ref[...] = pair_ref[...]

    @pl.when(own & 1 == 1)
    def _():
        low_ref[...] = pair_ref[...]
        high_ref[...] = side_ref[...]

    extent = 2 * HALO
    lanes = lax.broadcasted_iota(jnp.int32, (1, HALO), 1)

    def reached(halo_ref, base):
        relative = halo_ref[extent : extent + near_ref.shape[0], :].astype(F32).astype(jnp.int32)
        return jnp.where(relative == ABSENT, -1, relative + lanes + base)

    def masked(halo_ref, first):
        live = live_lanes(first, extent, rows, before, count, after)
        return jnp.where(live, halo_ref[0:extent, :].T.astype(F32), 0.0).astype(BF16)

    edges = (edge.at[:, 0:WINDOW], edge.at[:, WINDOW:])
    edges[0][:, 0:extent] = masked(low_ref, -extent)
    edges[0][:, extent:] = act_ref[:, 0:extent]
    edges[1][:, 0:extent] = act_ref[:, rows - extent : rows]
    edges[1][:, extent:] = masked(high_ref, rows)
    near = (
        jnp.concatenate(
            [reached(low_ref, HALO), jnp.maximum(near_ref[:, 0:HALO] - own * rows + extent, -1)], axis=1
        ),
        jnp.concatenate(
            [
                jnp.maximum(near_ref[:, rows - HALO : rows] - own * rows - (rows - extent), -1),
                reached(high_ref, 2 * HALO),
            ],
            axis=1,
        ),
    )
    blocks = rows // BLOCK
    padded[:, BLOCK:rows] = inner_ref[:, BLOCK:rows]

    def gather_edge(n, picked):
        gather_block(lambda at, size: edges[n][:, at : at + size], near[n], picked)

    def convolve_edge(n, picked):
        edge_conv[:, n * BLOCK : (n + 1) * BLOCK] = dot(turned_ref[0], picked[...]).astype(BF16)

    def norm_edge(n):
        at = n * rows
        live = live_lanes(at - HALO, BLOCK, rows, before, count, after)
        padded[:, at : at + BLOCK] = norm_block(
            edges[n][:, HALO : HALO + BLOCK], edge_conv[:, n * BLOCK : (n + 1) * BLOCK], linear_ref[0].T, live
        )

    def gather(b, picked):
        first = b * BLOCK
        targets = jnp.maximum(near_ref[:, columns(first)] - (own * rows + first - HALO), -1)
        gather_block(lambda at, n: padded[:, pl.ds(pl.multiple_of(first + at, HALO), n)], targets, picked)

    def convolve(b, picked):
        conv[:, columns(b * BLOCK)] = dot(turned_ref[1], picked[...]).astype(BF16)

    gather_edge(0, even)
    gather_edge(1, odd)
    convolve_edge(0, even)
    gather(1, even)
    convolve_edge(1, odd)

    def step(t, _):
        gather(2 * t + 2, odd)
        convolve(2 * t + 1, even)
        gather(2 * t + 3, even)
        convolve(2 * t + 2, odd)
        return 0

    lax.fori_loop(0, (blocks - 4) // 2, step, 0)
    norm_edge(0)
    norm_edge(1)
    gather(blocks - 2, odd)
    convolve(blocks - 3, even)
    gather(0, even)
    convolve(blocks - 2, odd)
    gather(blocks - 1, odd)
    convolve(0, even)
    convolve(blocks - 1, odd)
    linear = linear_ref[1].T

    def norm(b):
        first = b * BLOCK
        live = live_lanes(first, BLOCK, rows, before, count, after)
        last[:, columns(first)] = norm_block(
            padded[:, columns(first + HALO)], conv[:, columns(first)], linear, live
        )

    in_turn(0, blocks, norm)

    shards, depth, _ = send_ref.shape
    capacity = rows // shards
    pieces = BLOCK // capacity

    def store(b, block):
        for p in range(pieces):
            send_ref[b * pieces + p, 0:capacity, :] = block[p * capacity : (p + 1) * capacity, :]

    reorder(last, perm_ref, store)
    held = capacity // 128
    pad = jnp.zeros((depth - capacity - 2 * held, 128), F32)
    for d in range(shards):
        at = slice(d * held, (d + 1) * held)
        extra = jnp.concatenate([place_high_ref[at, :], place_low_ref[at, :], pad], axis=0)
        send_ref[d, capacity:, :] = extra.astype(BF16)


def reorder(source, from_ref, store, dots=6, unroll=16):
    channels, rows = source.shape
    windows = rows // WINDOW

    def one(b):
        pair = from_ref[pl.ds(b * 2, 2), :]
        wanted = jnp.concatenate([pair[0:1, :], pair[1:2, :]], axis=1)
        total = jnp.zeros((channels, BLOCK), F32)
        halves = [jnp.zeros((channels, 128), BF16) for _ in range(2)]
        lanes = [pair[h : h + 1, :] & 127 for h in range(2)]
        chunks = [jnp.broadcast_to((pair[h : h + 1, :] >> 7).astype(jnp.int16), (channels, 128)) for h in range(2)]
        rest = [(j, h) for j in range(dots * WINDOW // 128, rows // 128) for h in range(2)]
        done = 0
        for w in range(dots):
            total = total + dot(source[:, w * WINDOW : (w + 1) * WINDOW], selector(wanted - w * WINDOW, WINDOW))
            until = len(rest) * (w + 1) // dots
            for j, h in rest[done:until]:
                halves[h] = jnp.where(
                    chunks[h] == j, lane_pick(source[:, j * 128 : (j + 1) * 128], lanes[h]), halves[h]
                )
            done = until
        store(b, (total + jnp.concatenate(halves, axis=1).astype(F32)).astype(BF16).T)

    def step(t, _):
        for u in range(unroll):
            one(t * unroll + u)
        return 0

    lax.fori_loop(0, rows // BLOCK // unroll, step, 0)


def final_kernel(got_ref, out_hbm, out_ref, turned, from_ref, sems):
    rows = out_ref.shape[0]
    shards = got_ref.shape[0]
    groups = rows // 128
    capacity = rows // shards
    held = capacity // 128
    lanes = lax.broadcasted_iota(jnp.int32, (1, capacity), 1)
    total = jnp.zeros((2 * groups, 128), F32)
    for s in range(shards):
        turned[:, s * capacity : (s + 1) * capacity] = got_ref[s, 0:capacity, :].T
        extra = got_ref[s, capacity:, :].astype(F32)
        place = (extra[0:held, :] * 64.0 + extra[held : 2 * held, :]).astype(jnp.int32)
        place = jnp.concatenate([place[h : h + 1, :] for h in range(held)], axis=1)
        total = total + scatter_term(place, (s * capacity + lanes,), groups)
    from_ref[...] = joined(total, 0, groups)

    def copy(b):
        at = pl.ds(pl.multiple_of(b * BLOCK, BLOCK), BLOCK)
        return pltpu.make_async_copy(out_ref.at[at, :], out_hbm.at[at, :], sems.at[b])

    def store(b, block):
        out_ref[pl.ds(pl.multiple_of(b * BLOCK, BLOCK), BLOCK), :] = block
        copy(b).start()

    reorder(turned, from_ref, store)
    for b in range(rows // BLOCK):
        copy(b).wait()


def local(voxels, counts, neighbours, conv_weight, linear_weight, destination):
    rows, channels = voxels.shape
    offsets = neighbours.shape[0]
    both = ("wide", "narrow")
    shards = lax.axis_size(both)
    own = lax.axis_index(both)
    place = jnp.reshape(own, (1,)).astype(jnp.int32)
    extent = 2 * HALO
    struct = jax.ShapeDtypeStruct
    vmem = pl.BlockSpec(memory_space=VMEM)
    smem = pl.BlockSpec(memory_space=SMEM)
    hbm = pl.BlockSpec(memory_space=pltpu.HBM)

    packed = struct((extent + 32, channels), BF16)
    to_pair, to_side = pl.pallas_call(
        edges_kernel,
        out_shape=(packed, packed),
        in_specs=[smem, hbm, hbm],
        out_specs=(vmem, vmem),
        scratch_shapes=[VMEM((offsets, HALO), jnp.int32), VMEM((offsets, HALO), jnp.int32), pltpu.SemaphoreType.DMA((4,))],
        cost_estimate=pl.CostEstimate(flops=20_000_000_000, bytes_accessed=500_000, transcendentals=0),
        compiler_params=params(60),
        name="edges",
    )(place, voxels, neighbours)
    others = [(0, 0), (shards - 1, shards - 1)]
    for i in range(1, shards - 1, 2):
        others += [(i, i + 1), (i + 1, i)]
    side = lax.ppermute(to_side, both, others)
    pair = lax.ppermute(to_pair, both, [(i, i ^ 1) for i in range(shards)])

    table = (rows // 128, 128)
    padded = (channels, rows + BLOCK)
    picked = VMEM((offsets * channels, BLOCK), BF16)
    turned = (2, channels, offsets * channels)
    act, inner, perm, place_high, place_low, weights = pl.pallas_call(
        functools.partial(inner_kernel, shards),
        out_shape=(
            struct((channels, rows), BF16), struct(padded, BF16), struct(table, jnp.int32), struct(table, F32),
            struct(table, F32), struct(turned, BF16),
        ),
        in_specs=[smem, smem, vmem, vmem, hbm, vmem, vmem],
        out_specs=(vmem,) * 6,
        scratch_shapes=[
            VMEM(conv_weight.shape, BF16), picked, picked, VMEM(padded, BF16), pltpu.SemaphoreType.DMA((2,)),
        ],
        compiler_params=params(),
        cost_estimate=pl.CostEstimate(flops=20_000_000_000, bytes_accessed=6_000_000, transcendentals=0),
        name="first_layer",
    )(place, counts, voxels, neighbours, conv_weight, linear_weight, destination.reshape(1, rows))

    depth = rows // shards + 16
    send = pl.pallas_call(
        outer_kernel,
        out_shape=struct((shards, depth, channels), BF16),
        in_specs=[smem, smem] + [vmem] * 10,
        out_specs=vmem,
        scratch_shapes=[
            VMEM(packed.shape, BF16),
            VMEM(packed.shape, BF16),
            picked,
            picked,
            VMEM((channels, 2 * WINDOW), BF16),
            VMEM((channels, 2 * BLOCK), BF16),
            VMEM(padded, BF16),
            VMEM((channels, rows), BF16),
            VMEM((channels, rows), BF16),
        ],
        compiler_params=params(),
        cost_estimate=pl.CostEstimate(flops=30_000_000_000, bytes_accessed=8_000_000, transcendentals=0),
        name="second_layer",
    )(place, counts, pair, side, act, inner, neighbours, weights, linear_weight, perm, place_high, place_low)

    got = lax.all_to_all(send, both, split_axis=0, concat_axis=0, tiled=True)
    return pl.pallas_call(
        final_kernel,
        out_shape=struct((rows, channels), BF16),
        in_specs=[vmem],
        out_specs=hbm,
        scratch_shapes=[
            VMEM((rows, channels), BF16), VMEM((channels, rows), BF16), VMEM(table, jnp.int32),
            pltpu.SemaphoreType.DMA((rows // BLOCK,)),
        ],
        compiler_params=params(),
        name="hilbert_order",
    )(got)


def solution(mesh):
    in_specs = (
        P(("groups", "wide", "narrow"), None),
        P("groups"),
        P(None, ("groups", "wide", "narrow")),
        P(),
        P(),
        P(("groups", "wide", "narrow")),
    )
    out_specs = P(("groups", "wide", "narrow"), None)
    return jax.shard_map(local, mesh=mesh, in_specs=in_specs, out_specs=out_specs, check_vma=False)
```

```python
import functools

import jax
import jax.numpy as jnp
from jax import lax
from jax.experimental import pallas as pl
from jax.experimental.pallas import tpu as pltpu
from jax.sharding import PartitionSpec as P

HALO = 128
BLOCK = 256
WINDOW = 512
BF16 = jnp.bfloat16
F32 = jnp.float32
ABSENT = 256
SMEM = pltpu.SMEM
VMEM = pltpu.VMEM


def params(mebibytes=48):
    return pltpu.CompilerParams(vmem_limit_bytes=mebibytes * 1024 * 1024)


def selector(row, depth):
    shape = (depth, row.shape[1])
    places = lax.broadcasted_iota(jnp.int16, shape, 0)
    wanted = jnp.broadcast_to(row.astype(jnp.int16), shape)
    return jnp.where(places == wanted, BF16(1), BF16(0))


def dot(a, b):
    return jnp.dot(a, b, preferred_element_type=F32)


def live_lanes(first, width, rows, before, own, after):
    at = first + lax.broadcasted_iota(jnp.int32, (1, width), 1)
    limit = jnp.where(at < 0, before - rows, jnp.where(at < rows, own, after + rows))
    return at < limit


def lane_pick(block, lanes):
    numbers = lax.GatherDimensionNumbers(
        offset_dims=(), collapsed_slice_dims=(1,), start_index_map=(1,),
        operand_batching_dims=(0,), start_indices_batching_dims=(0,),
    )
    index = jnp.broadcast_to(lanes.astype(jnp.int16), block.shape)
    return lax.gather(block, index[..., None], numbers, (1, 1), mode=lax.GatherScatterMode.PROMISE_IN_BOUNDS)


def gather_block(window, targets, picked):
    offsets = targets.shape[0]
    channels = picked.shape[0] // offsets
    static = {0: 0, offsets // 2: HALO, offsets - 1: 2 * HALO}
    turn = 0
    for k in range(offsets):
        at = slice(k * channels, (k + 1) * channels)
        if k in static:
            picked[at, :] = window(static[k], BLOCK)
            continue
        turn += 1
        row = targets[k : k + 1, :]
        if turn % 2:
            picked[at, :] = dot(window(0, WINDOW), selector(row, WINDOW)).astype(BF16)
            continue
        for half in range(2):
            part = row[:, half * HALO : (half + 1) * HALO]
            lanes = part & (HALO - 1)
            chunk = jnp.broadcast_to((part >> 7).astype(jnp.int16), (channels, HALO))
            total = jnp.zeros((channels, HALO), BF16)
            for j in range(half, half + 3):
                total = jnp.where(chunk == j, lane_pick(window(j * HALO, HALO), lanes), total)
            picked[at, half * HALO : (half + 1) * HALO] = total


def norm_block(current, convolved, linear, live):
    projected = dot(linear, convolved)
    average = jnp.mean(projected, axis=0, keepdims=True)
    centred = projected - average
    spread = jnp.mean(centred * centred, axis=0, keepdims=True)
    summed = current.astype(F32) + centred * lax.rsqrt(spread + 1e-05)
    return jnp.where(live, summed, 0.0).astype(BF16)


def columns(start):
    return pl.ds(pl.multiple_of(start, HALO), BLOCK)


def turn_weights(weight_ref, layer, turned):
    offsets, channels = weight_ref.shape[1], weight_ref.shape[2]
    for k in range(offsets):
        turned[:, k * channels : (k + 1) * channels] = weight_ref[layer, k].T


def device_counts(place_ref, counts_ref):
    own = place_ref[0]
    last = counts_ref.shape[0] - 1
    before = jnp.where(own > 0, counts_ref[jnp.maximum(own - 1, 0)], 0)
    after = jnp.where(own < last, counts_ref[jnp.minimum(own + 1, last)], 0)
    return own, before, counts_ref[own], after


def slots_table(destination_ref, shards):
    rows = destination_ref.shape[1]
    capacity = rows // shards
    groups = rows // 128
    tile = 256
    earlier = (
        lax.broadcasted_iota(jnp.int32, (tile, tile), 0) < lax.broadcasted_iota(jnp.int32, (tile, tile), 1)
    ).astype(F32).astype(BF16)
    devices = lax.broadcasted_iota(jnp.int32, (shards, tile), 0)
    tiles = rows // tile
    goals = [destination_ref[:, c * tile : (c + 1) * tile] for c in range(tiles)]
    members = [
        (jnp.broadcast_to(goal >> (rows.bit_length() - 1), (shards, tile)) == devices).astype(F32) for goal in goals
    ]
    stacked = jnp.concatenate([member.astype(BF16) for member in members], axis=0)
    ranks = dot(stacked, earlier)
    sums = dot(stacked, jnp.ones((tile, tile), BF16))
    before = (devices * capacity).astype(F32)
    total = jnp.zeros((4 * groups, 128), F32)
    for c in range(tiles):
        part = slice(c * shards, (c + 1) * shards)
        slot = jnp.sum(members[c] * (ranks[part, :] + before), axis=0, keepdims=True).astype(jnp.int32)
        before = before + sums[part, :]
        row = c * tile + lax.broadcasted_iota(jnp.int32, (1, tile), 1)
        total = total + scatter_term(slot, (row, goals[c] & (rows - 1)), groups)
    return total


def scatter_term(at, values, groups):
    high = selector(at >> 7, groups)
    parts = []
    for value in values:
        for part in (value >> 6, value & 63):
            parts.append(high * jnp.broadcast_to(part.astype(F32).astype(BF16), high.shape))
    left = jnp.concatenate(parts, axis=0)
    low = selector(at & 127, 128)
    return lax.dot_general(left, low, (((1,), (1,)), ((), ())), preferred_element_type=F32)


def joined(total, n, groups):
    high = total[2 * n * groups : (2 * n + 1) * groups, :]
    low = total[(2 * n + 1) * groups : (2 * n + 2) * groups, :]
    return (high * 64.0 + low).astype(jnp.int32)


def edges_kernel(place_ref, voxels_hbm, near_hbm, pair_ref, side_ref, near_pair, near_side, sems):
    rows = voxels_hbm.shape[0]
    extent = 2 * HALO
    own = place_ref[0]
    odd = own & 1
    parts = ((pair_ref, near_pair, 1 - odd), (side_ref, near_side, odd))
    copies = []
    for n, (out_ref, near_ref, upper) in enumerate(parts):
        near_at = pl.ds(pl.multiple_of(upper * (rows - HALO), HALO), HALO)
        voxels_at = pl.ds(pl.multiple_of(upper * (rows - extent), extent), extent)
        copies.append(pltpu.make_async_copy(near_hbm.at[:, near_at], near_ref, sems.at[n]))
        copies.append(pltpu.make_async_copy(voxels_hbm.at[voxels_at, :], out_ref.at[0:extent, :], sems.at[2 + n]))
    for copy in copies:
        copy.start()
    lanes = lax.broadcasted_iota(jnp.int32, (1, HALO), 1)
    for n, (out_ref, near_ref, upper) in enumerate(parts):
        copies[2 * n].wait()
        near = near_ref[...]
        relative = jnp.where(near >= 0, near - (own * rows + upper * (rows - HALO) + lanes), ABSENT).astype(F32)
        pad = jnp.zeros((out_ref.shape[0] - extent - near.shape[0], HALO), F32)
        out_ref[extent:, :] = jnp.concatenate([relative, pad], axis=0).astype(BF16)
    copies[1].wait()
    copies[3].wait()


def inner_kernel(
    shards, place_ref, counts_ref, voxels_ref, near_ref, weight_hbm, linear_ref, destination_ref,
    act_ref, next_ref, perm_ref, high_ref, low_ref, turned_ref,
    weight_ref, even, odd, conv, sems,
):
    weights_in = [
        pltpu.make_async_copy(weight_hbm.at[layer], weight_ref.at[layer], sems.at[layer]) for layer in range(2)
    ]
    weights_in[0].start()
    rows, channels = voxels_ref.shape
    own, before, count, after = device_counts(place_ref, counts_ref)
    groups = rows // 128
    total = slots_table(destination_ref, shards)
    perm_ref[...] = joined(total, 0, groups)
    high_ref[...] = total[2 * groups : 3 * groups, :]
    low_ref[...] = total[3 * groups :, :]
    for c in range(rows // BLOCK):
        live = live_lanes(c * BLOCK, BLOCK, rows, before, count, after)
        block = voxels_ref[c * BLOCK : (c + 1) * BLOCK, :].T
        act_ref[:, c * BLOCK : (c + 1) * BLOCK] = jnp.where(live, block.astype(F32), 0.0).astype(BF16)
    linear = linear_ref[0].T

    def gather(b, picked):
        first = (b - 1) * BLOCK
        targets = jnp.maximum(near_ref[:, columns(first + HALO)] - (own * rows + first), -1)
        gather_block(lambda at, n: act_ref[:, pl.ds(pl.multiple_of(first + at, HALO), n)], targets, picked)

    def convolve(b, picked):
        conv[:, columns(b * BLOCK)] = dot(turned_ref[0], picked[...]).astype(BF16)

    blocks = rows // BLOCK
    gather(1, even)
    weights_in[0].wait()
    weights_in[1].start()
    turn_weights(weight_ref, 0, turned_ref.at[0])

    def step(t, _):
        gather(2 * t + 2, odd)
        convolve(2 * t + 1, even)
        gather(2 * t + 3, even)
        convolve(2 * t + 2, odd)
        return 0

    lax.fori_loop(0, (blocks - 2) // 2, step, 0)
    convolve(blocks - 1, even)

    def norm(b):
        first = b * BLOCK - HALO
        live = live_lanes(first, BLOCK, rows, before, count, after)
        next_ref[:, columns(b * BLOCK)] = norm_block(
            act_ref[:, columns(first)], conv[:, columns(b * BLOCK)], linear, live
        )

    weights_in[1].wait()
    turn_weights(weight_ref, 1, turned_ref.at[1])
    in_turn(1, blocks, norm)


def in_turn(first, last, body, most=16):
    count = last - first
    unroll = max(u for u in range(1, most + 1) if count % u == 0)
    if unroll == count:
        for b in range(first, last):
            body(b)
        return

    def step(t, _):
        for u in range(unroll):
            body(first + t * unroll + u)
        return 0

    lax.fori_loop(0, count // unroll, step, 0)


def outer_kernel(
    place_ref, counts_ref, pair_ref, side_ref, act_ref, inner_ref, near_ref, turned_ref, linear_ref,
    perm_ref, place_high_ref, place_low_ref, send_ref, low_ref, high_ref, even, odd, edge, edge_conv, padded, conv, last,
):
    channels, rows = act_ref.shape
    own, before, count, after = device_counts(place_ref, counts_ref)

    @pl.when(own & 1 == 0)
    def _():
        low_ref[...] = side_ref[...]
        high_ref[...] = pair_ref[...]

    @pl.when(own & 1 == 1)
    def _():
        low_ref[...] = pair_ref[...]
        high_ref[...] = side_ref[...]

    extent = 2 * HALO
    lanes = lax.broadcasted_iota(jnp.int32, (1, HALO), 1)

    def reached(halo_ref, base):
        relative = halo_ref[extent : extent + near_ref.shape[0], :].astype(F32).astype(jnp.int32)
        return jnp.where(relative == ABSENT, -1, relative + lanes + base)

    def masked(halo_ref, first):
        live = live_lanes(first, extent, rows, before, count, after)
        return jnp.where(live, halo_ref[0:extent, :].T.astype(F32), 0.0).astype(BF16)

    edges = (edge.at[:, 0:WINDOW], edge.at[:, WINDOW:])
    edges[0][:, 0:extent] = masked(low_ref, -extent)
    edges[0][:, extent:] = act_ref[:, 0:extent]
    edges[1][:, 0:extent] = act_ref[:, rows - extent : rows]
    edges[1][:, extent:] = masked(high_ref, rows)
    near = (
        jnp.concatenate(
            [reached(low_ref, HALO), jnp.maximum(near_ref[:, 0:HALO] - own * rows + extent, -1)], axis=1
        ),
        jnp.concatenate(
            [
                jnp.maximum(near_ref[:, rows - HALO : rows] - own * rows - (rows - extent), -1),
                reached(high_ref, 2 * HALO),
            ],
            axis=1,
        ),
    )
    blocks = rows // BLOCK
    padded[:, BLOCK:rows] = inner_ref[:, BLOCK:rows]

    def gather_edge(n, picked):
        gather_block(lambda at, size: edges[n][:, at : at + size], near[n], picked)

    def convolve_edge(n, picked):
        edge_conv[:, n * BLOCK : (n + 1) * BLOCK] = dot(turned_ref[0], picked[...]).astype(BF16)

    def norm_edge(n):
        at = n * rows
        live = live_lanes(at - HALO, BLOCK, rows, before, count, after)
        padded[:, at : at + BLOCK] = norm_block(
            edges[n][:, HALO : HALO + BLOCK], edge_conv[:, n * BLOCK : (n + 1) * BLOCK], linear_ref[0].T, live
        )

    def gather(b, picked):
        first = b * BLOCK
        targets = jnp.maximum(near_ref[:, columns(first)] - (own * rows + first - HALO), -1)
        gather_block(lambda at, n: padded[:, pl.ds(pl.multiple_of(first + at, HALO), n)], targets, picked)

    def convolve(b, picked):
        conv[:, columns(b * BLOCK)] = dot(turned_ref[1], picked[...]).astype(BF16)

    gather_edge(0, even)
    gather_edge(1, odd)
    convolve_edge(0, even)
    gather(1, even)
    convolve_edge(1, odd)

    def step(t, _):
        gather(2 * t + 2, odd)
        convolve(2 * t + 1, even)
        gather(2 * t + 3, even)
        convolve(2 * t + 2, odd)
        return 0

    lax.fori_loop(0, (blocks - 4) // 2, step, 0)
    norm_edge(0)
    norm_edge(1)
    gather(blocks - 2, odd)
    convolve(blocks - 3, even)
    gather(0, even)
    convolve(blocks - 2, odd)
    gather(blocks - 1, odd)
    convolve(0, even)
    convolve(blocks - 1, odd)
    linear = linear_ref[1].T

    def norm(b):
        first = b * BLOCK
        live = live_lanes(first, BLOCK, rows, before, count, after)
        last[:, columns(first)] = norm_block(
            padded[:, columns(first + HALO)], conv[:, columns(first)], linear, live
        )

    in_turn(0, blocks, norm)

    shards, depth, _ = send_ref.shape
    capacity = rows // shards
    pieces = BLOCK // capacity

    def store(b, block):
        for p in range(pieces):
            send_ref[b * pieces + p, 0:capacity, :] = block[p * capacity : (p + 1) * capacity, :]

    reorder(last, perm_ref, store)
    held = capacity // 128
    pad = jnp.zeros((depth - capacity - 2 * held, 128), F32)
    for d in range(shards):
        at = slice(d * held, (d + 1) * held)
        extra = jnp.concatenate([place_high_ref[at, :], place_low_ref[at, :], pad], axis=0)
        send_ref[d, capacity:, :] = extra.astype(BF16)


def reorder(source, from_ref, store, dots=6, unroll=16):
    channels, rows = source.shape
    windows = rows // WINDOW

    def one(b):
        pair = from_ref[pl.ds(b * 2, 2), :]
        wanted = jnp.concatenate([pair[0:1, :], pair[1:2, :]], axis=1)
        total = jnp.zeros((channels, BLOCK), F32)
        halves = [jnp.zeros((channels, 128), BF16) for _ in range(2)]
        lanes = [pair[h : h + 1, :] & 127 for h in range(2)]
        chunks = [jnp.broadcast_to((pair[h : h + 1, :] >> 7).astype(jnp.int16), (channels, 128)) for h in range(2)]
        rest = [(j, h) for j in range(dots * WINDOW // 128, rows // 128) for h in range(2)]
        done = 0
        for w in range(dots):
            total = total + dot(source[:, w * WINDOW : (w + 1) * WINDOW], selector(wanted - w * WINDOW, WINDOW))
            until = len(rest) * (w + 1) // dots
            for j, h in rest[done:until]:
                halves[h] = jnp.where(
                    chunks[h] == j, lane_pick(source[:, j * 128 : (j + 1) * 128], lanes[h]), halves[h]
                )
            done = until
        store(b, (total + jnp.concatenate(halves, axis=1).astype(F32)).astype(BF16).T)

    def step(t, _):
        for u in range(unroll):
            one(t * unroll + u)
        return 0

    lax.fori_loop(0, rows // BLOCK // unroll, step, 0)


def final_kernel(got_ref, out_hbm, out_ref, turned, from_ref, sems):
    rows = out_ref.shape[0]
    shards = got_ref.shape[0]
    groups = rows // 128
    capacity = rows // shards
    held = capacity // 128
    lanes = lax.broadcasted_iota(jnp.int32, (1, capacity), 1)
    total = jnp.zeros((2 * groups, 128), F32)
    for s in range(shards):
        turned[:, s * capacity : (s + 1) * capacity] = got_ref[s, 0:capacity, :].T
        extra = got_ref[s, capacity:, :].astype(F32)
        place = (extra[0:held, :] * 64.0 + extra[held : 2 * held, :]).astype(jnp.int32)
        place = jnp.concatenate([place[h : h + 1, :] for h in range(held)], axis=1)
        total = total + scatter_term(place, (s * capacity + lanes,), groups)
    from_ref[...] = joined(total, 0, groups)

    def copy(b):
        at = pl.ds(pl.multiple_of(b * BLOCK, BLOCK), BLOCK)
        return pltpu.make_async_copy(out_ref.at[at, :], out_hbm.at[at, :], sems.at[b])

    def store(b, block):
        out_ref[pl.ds(pl.multiple_of(b * BLOCK, BLOCK), BLOCK), :] = block
        copy(b).start()

    reorder(turned, from_ref, store)
    for b in range(rows // BLOCK):
        copy(b).wait()


def local(voxels, counts, neighbours, conv_weight, linear_weight, destination):
    rows, channels = voxels.shape
    offsets = neighbours.shape[0]
    both = ("wide", "narrow")
    shards = lax.axis_size(both)
    own = lax.axis_index(both)
    place = jnp.reshape(own, (1,)).astype(jnp.int32)
    extent = 2 * HALO
    struct = jax.ShapeDtypeStruct
    vmem = pl.BlockSpec(memory_space=VMEM)
    smem = pl.BlockSpec(memory_space=SMEM)
    hbm = pl.BlockSpec(memory_space=pltpu.HBM)

    packed = struct((extent + 32, channels), BF16)
    to_pair, to_side = pl.pallas_call(
        edges_kernel,
        out_shape=(packed, packed),
        in_specs=[smem, hbm, hbm],
        out_specs=(vmem, vmem),
        scratch_shapes=[VMEM((offsets, HALO), jnp.int32), VMEM((offsets, HALO), jnp.int32), pltpu.SemaphoreType.DMA((4,))],
        cost_estimate=pl.CostEstimate(flops=20_000_000_000, bytes_accessed=500_000, transcendentals=0),
        compiler_params=params(60),
        name="edges",
    )(place, voxels, neighbours)
    others = [(0, 0), (shards - 1, shards - 1)]
    for i in range(1, shards - 1, 2):
        others += [(i, i + 1), (i + 1, i)]
    side = lax.ppermute(to_side, both, others)
    pair = lax.ppermute(to_pair, both, [(i, i ^ 1) for i in range(shards)])

    table = (rows // 128, 128)
    padded = (channels, rows + BLOCK)
    picked = VMEM((offsets * channels, BLOCK), BF16)
    turned = (2, channels, offsets * channels)
    act, inner, perm, place_high, place_low, weights = pl.pallas_call(
        functools.partial(inner_kernel, shards),
        out_shape=(
            struct((channels, rows), BF16), struct(padded, BF16), struct(table, jnp.int32), struct(table, F32),
            struct(table, F32), struct(turned, BF16),
        ),
        in_specs=[smem, smem, vmem, vmem, hbm, vmem, vmem],
        out_specs=(vmem,) * 6,
        scratch_shapes=[
            VMEM(conv_weight.shape, BF16), picked, picked, VMEM(padded, BF16), pltpu.SemaphoreType.DMA((2,)),
        ],
        compiler_params=params(),
        cost_estimate=pl.CostEstimate(flops=20_000_000_000, bytes_accessed=6_000_000, transcendentals=0),
        name="first_layer",
    )(place, counts, voxels, neighbours, conv_weight, linear_weight, destination.reshape(1, rows))

    depth = rows // shards + 16
    send = pl.pallas_call(
        outer_kernel,
        out_shape=struct((shards, depth, channels), BF16),
        in_specs=[smem, smem] + [vmem] * 10,
        out_specs=vmem,
        scratch_shapes=[
            VMEM(packed.shape, BF16),
            VMEM(packed.shape, BF16),
            picked,
            picked,
            VMEM((channels, 2 * WINDOW), BF16),
            VMEM((channels, 2 * BLOCK), BF16),
            VMEM(padded, BF16),
            VMEM((channels, rows), BF16),
            VMEM((channels, rows), BF16),
        ],
        compiler_params=params(),
        cost_estimate=pl.CostEstimate(flops=30_000_000_000, bytes_accessed=8_000_000, transcendentals=0),
        name="second_layer",
    )(place, counts, pair, side, act, inner, neighbours, weights, linear_weight, perm, place_high, place_low)

    got = lax.all_to_all(send, both, split_axis=0, concat_axis=0, tiled=True)
    return pl.pallas_call(
        final_kernel,
        out_shape=struct((rows, channels), BF16),
        in_specs=[vmem],
        out_specs=hbm,
        scratch_shapes=[
            VMEM((rows, channels), BF16), VMEM((channels, rows), BF16), VMEM(table, jnp.int32),
            pltpu.SemaphoreType.DMA((rows // BLOCK,)),
        ],
        compiler_params=params(),
        name="hilbert_order",
    )(got)


def solution(mesh):
    in_specs = (
        P(("groups", "wide", "narrow"), None),
        P("groups"),
        P(None, ("groups", "wide", "narrow")),
        P(),
        P(),
        P(("groups", "wide", "narrow")),
    )
    out_specs = P(("groups", "wide", "narrow"), None)
    return jax.shard_map(local, mesh=mesh, in_specs=in_specs, out_specs=out_specs, check_vma=False)
```

```python
import functools

import jax
import jax.numpy as jnp
from jax import lax
from jax.experimental import pallas as pl
from jax.experimental.pallas import tpu as pltpu
from jax.sharding import PartitionSpec as P

HALO = 128
BLOCK = 256
WINDOW = 512
BF16 = jnp.bfloat16
F32 = jnp.float32
ABSENT = 256
SMEM = pltpu.SMEM
VMEM = pltpu.VMEM


def params(mebibytes=48):
    return pltpu.CompilerParams(vmem_limit_bytes=mebibytes * 1024 * 1024)


def selector(row, depth):
    shape = (depth, row.shape[1])
    places = lax.broadcasted_iota(jnp.int16, shape, 0)
    wanted = jnp.broadcast_to(row.astype(jnp.int16), shape)
    return jnp.where(places == wanted, BF16(1), BF16(0))


def dot(a, b):
    return jnp.dot(a, b, preferred_element_type=F32)


def live_lanes(first, width, rows, before, own, after):
    at = first + lax.broadcasted_iota(jnp.int32, (1, width), 1)
    limit = jnp.where(at < 0, before - rows, jnp.where(at < rows, own, after + rows))
    return at < limit


def lane_pick(block, lanes):
    numbers = lax.GatherDimensionNumbers(
        offset_dims=(), collapsed_slice_dims=(1,), start_index_map=(1,),
        operand_batching_dims=(0,), start_indices_batching_dims=(0,),
    )
    index = jnp.broadcast_to(lanes.astype(jnp.int16), block.shape)
    return lax.gather(block, index[..., None], numbers, (1, 1), mode=lax.GatherScatterMode.PROMISE_IN_BOUNDS)


def gather_block(window, targets, picked):
    offsets = targets.shape[0]
    channels = picked.shape[0] // offsets
    static = {0: 0, offsets // 2: HALO, offsets - 1: 2 * HALO}
    turn = 0
    for k in range(offsets):
        at = slice(k * channels, (k + 1) * channels)
        if k in static:
            picked[at, :] = window(static[k], BLOCK)
            continue
        turn += 1
        row = targets[k : k + 1, :]
        if turn % 2:
            picked[at, :] = dot(window(0, WINDOW), selector(row, WINDOW)).astype(BF16)
            continue
        for half in range(2):
            part = row[:, half * HALO : (half + 1) * HALO]
            lanes = part & (HALO - 1)
            chunk = jnp.broadcast_to((part >> 7).astype(jnp.int16), (channels, HALO))
            total = jnp.zeros((channels, HALO), BF16)
            for j in range(half, half + 3):
                total = jnp.where(chunk == j, lane_pick(window(j * HALO, HALO), lanes), total)
            picked[at, half * HALO : (half + 1) * HALO] = total


def norm_block(current, convolved, linear, live):
    projected = dot(linear, convolved)
    average = jnp.mean(projected, axis=0, keepdims=True)
    centred = projected - average
    spread = jnp.mean(centred * centred, axis=0, keepdims=True)
    summed = current.astype(F32) + centred * lax.rsqrt(spread + 1e-05)
    return jnp.where(live, summed, 0.0).astype(BF16)


def columns(start):
    return pl.ds(pl.multiple_of(start, HALO), BLOCK)


def turn_weights(weight_ref, layer, turned):
    offsets, channels = weight_ref.shape[1], weight_ref.shape[2]
    for k in range(offsets):
        turned[:, k * channels : (k + 1) * channels] = weight_ref[layer, k].T


def device_counts(place_ref, counts_ref):
    own = place_ref[0]
    last = counts_ref.shape[0] - 1
    before = jnp.where(own > 0, counts_ref[jnp.maximum(own - 1, 0)], 0)
    after = jnp.where(own < last, counts_ref[jnp.minimum(own + 1, last)], 0)
    return own, before, counts_ref[own], after


def slots_table(destination_ref, shards):
    rows = destination_ref.shape[1]
    capacity = rows // shards
    groups = rows // 128
    tile = 256
    earlier = (
        lax.broadcasted_iota(jnp.int32, (tile, tile), 0) < lax.broadcasted_iota(jnp.int32, (tile, tile), 1)
    ).astype(F32).astype(BF16)
    devices = lax.broadcasted_iota(jnp.int32, (shards, tile), 0)
    tiles = rows // tile
    goals = [destination_ref[:, c * tile : (c + 1) * tile] for c in range(tiles)]
    members = [
        (jnp.broadcast_to(goal >> (rows.bit_length() - 1), (shards, tile)) == devices).astype(F32) for goal in goals
    ]
    stacked = jnp.concatenate([member.astype(BF16) for member in members], axis=0)
    ranks = dot(stacked, earlier)
    sums = dot(stacked, jnp.ones((tile, tile), BF16))
    before = (devices * capacity).astype(F32)
    total = jnp.zeros((4 * groups, 128), F32)
    for c in range(tiles):
        part = slice(c * shards, (c + 1) * shards)
        slot = jnp.sum(members[c] * (ranks[part, :] + before), axis=0, keepdims=True).astype(jnp.int32)
        before = before + sums[part, :]
        row = c * tile + lax.broadcasted_iota(jnp.int32, (1, tile), 1)
        total = total + scatter_term(slot, (row, goals[c] & (rows - 1)), groups)
    return total


def scatter_term(at, values, groups):
    high = selector(at >> 7, groups)
    parts = []
    for value in values:
        for part in (value >> 6, value & 63):
            parts.append(high * jnp.broadcast_to(part.astype(F32).astype(BF16), high.shape))
    left = jnp.concatenate(parts, axis=0)
    low = selector(at & 127, 128)
    return lax.dot_general(left, low, (((1,), (1,)), ((), ())), preferred_element_type=F32)


def joined(total, n, groups):
    high = total[2 * n * groups : (2 * n + 1) * groups, :]
    low = total[(2 * n + 1) * groups : (2 * n + 2) * groups, :]
    return (high * 64.0 + low).astype(jnp.int32)


def edges_kernel(place_ref, voxels_hbm, near_hbm, pair_ref, side_ref, near_pair, near_side, sems):
    rows = voxels_hbm.shape[0]
    extent = 2 * HALO
    own = place_ref[0]
    odd = own & 1
    parts = ((pair_ref, near_pair, 1 - odd), (side_ref, near_side, odd))
    copies = []
    for n, (out_ref, near_ref, upper) in enumerate(parts):
        near_at = pl.ds(pl.multiple_of(upper * (rows - HALO), HALO), HALO)
        voxels_at = pl.ds(pl.multiple_of(upper * (rows - extent), extent), extent)
        copies.append(pltpu.make_async_copy(near_hbm.at[:, near_at], near_ref, sems.at[n]))
        copies.append(pltpu.make_async_copy(voxels_hbm.at[voxels_at, :], out_ref.at[0:extent, :], sems.at[2 + n]))
    for copy in copies:
        copy.start()
    lanes = lax.broadcasted_iota(jnp.int32, (1, HALO), 1)
    for n, (out_ref, near_ref, upper) in enumerate(parts):
        copies[2 * n].wait()
        near = near_ref[...]
        relative = jnp.where(near >= 0, near - (own * rows + upper * (rows - HALO) + lanes), ABSENT).astype(F32)
        pad = jnp.zeros((out_ref.shape[0] - extent - near.shape[0], HALO), F32)
        out_ref[extent:, :] = jnp.concatenate([relative, pad], axis=0).astype(BF16)
    copies[1].wait()
    copies[3].wait()


def inner_kernel(
    shards, place_ref, counts_ref, voxels_ref, near_ref, weight_hbm, linear_ref, destination_ref,
    act_ref, next_ref, perm_ref, high_ref, low_ref, turned_ref,
    weight_ref, even, odd, conv, sems,
):
    weights_in = [
        pltpu.make_async_copy(weight_hbm.at[layer], weight_ref.at[layer], sems.at[layer]) for layer in range(2)
    ]
    weights_in[0].start()
    rows, channels = voxels_ref.shape
    own, before, count, after = device_counts(place_ref, counts_ref)
    for c in range(rows // BLOCK):
        live = live_lanes(c * BLOCK, BLOCK, rows, before, count, after)
        block = voxels_ref[c * BLOCK : (c + 1) * BLOCK, :].T
        act_ref[:, c * BLOCK : (c + 1) * BLOCK] = jnp.where(live, block.astype(F32), 0.0).astype(BF16)
    linear = linear_ref[0].T

    def gather(b, picked):
        first = (b - 1) * BLOCK
        targets = jnp.maximum(near_ref[:, columns(first + HALO)] - (own * rows + first), -1)
        gather_block(lambda at, n: act_ref[:, pl.ds(pl.multiple_of(first + at, HALO), n)], targets, picked)

    def convolve(b, picked):
        conv[:, columns(b * BLOCK)] = dot(turned_ref[0], picked[...]).astype(BF16)

    blocks = rows // BLOCK
    gather(1, even)
    groups = rows // 128
    total = slots_table(destination_ref, shards)
    perm_ref[...] = joined(total, 0, groups)
    high_ref[...] = total[2 * groups : 3 * groups, :]
    low_ref[...] = total[3 * groups :, :]
    weights_in[0].wait()
    weights_in[1].start()
    turn_weights(weight_ref, 0, turned_ref.at[0])

    def step(t, _):
        gather(2 * t + 2, odd)
        convolve(2 * t + 1, even)
        gather(2 * t + 3, even)
        convolve(2 * t + 2, odd)
        return 0

    lax.fori_loop(0, (blocks - 2) // 2, step, 0)
    convolve(blocks - 1, even)

    def norm(b):
        first = b * BLOCK - HALO
        live = live_lanes(first, BLOCK, rows, before, count, after)
        next_ref[:, columns(b * BLOCK)] = norm_block(
            act_ref[:, columns(first)], conv[:, columns(b * BLOCK)], linear, live
        )

    in_turn(1, blocks, norm)
    weights_in[1].wait()
    turn_weights(weight_ref, 1, turned_ref.at[1])


def in_turn(first, last, body, most=16):
    count = last - first
    unroll = max(u for u in range(1, most + 1) if count % u == 0)

    def step(t, _):
        for u in range(unroll):
            body(first + t * unroll + u)
        return 0

    lax.fori_loop(0, count // unroll, step, 0)


def outer_kernel(
    place_ref, counts_ref, pair_ref, side_ref, act_ref, inner_ref, near_ref, turned_ref, linear_ref,
    perm_ref, place_high_ref, place_low_ref, send_ref, low_ref, high_ref, even, odd, edge, edge_conv, padded, conv, last,
):
    channels, rows = act_ref.shape
    own, before, count, after = device_counts(place_ref, counts_ref)

    @pl.when(own & 1 == 0)
    def _():
        low_ref[...] = side_ref[...]
        high_ref[...] = pair_ref[...]

    @pl.when(own & 1 == 1)
    def _():
        low_ref[...] = pair_ref[...]
        high_ref[...] = side_ref[...]

    extent = 2 * HALO
    lanes = lax.broadcasted_iota(jnp.int32, (1, HALO), 1)

    def reached(halo_ref, base):
        relative = halo_ref[extent : extent + near_ref.shape[0], :].astype(F32).astype(jnp.int32)
        return jnp.where(relative == ABSENT, -1, relative + lanes + base)

    def masked(halo_ref, first):
        live = live_lanes(first, extent, rows, before, count, after)
        return jnp.where(live, halo_ref[0:extent, :].T.astype(F32), 0.0).astype(BF16)

    edges = (edge.at[:, 0:WINDOW], edge.at[:, WINDOW:])
    edges[0][:, 0:extent] = masked(low_ref, -extent)
    edges[0][:, extent:] = act_ref[:, 0:extent]
    edges[1][:, 0:extent] = act_ref[:, rows - extent : rows]
    edges[1][:, extent:] = masked(high_ref, rows)
    near = (
        jnp.concatenate(
            [reached(low_ref, HALO), jnp.maximum(near_ref[:, 0:HALO] - own * rows + extent, -1)], axis=1
        ),
        jnp.concatenate(
            [
                jnp.maximum(near_ref[:, rows - HALO : rows] - own * rows - (rows - extent), -1),
                reached(high_ref, 2 * HALO),
            ],
            axis=1,
        ),
    )
    blocks = rows // BLOCK
    padded[:, BLOCK:rows] = inner_ref[:, BLOCK:rows]

    def gather_edge(n, picked):
        gather_block(lambda at, size: edges[n][:, at : at + size], near[n], picked)

    def convolve_edge(n, picked):
        edge_conv[:, n * BLOCK : (n + 1) * BLOCK] = dot(turned_ref[0], picked[...]).astype(BF16)

    def norm_edge(n):
        at = n * rows
        live = live_lanes(at - HALO, BLOCK, rows, before, count, after)
        padded[:, at : at + BLOCK] = norm_block(
            edges[n][:, HALO : HALO + BLOCK], edge_conv[:, n * BLOCK : (n + 1) * BLOCK], linear_ref[0].T, live
        )

    def gather(b, picked):
        first = b * BLOCK
        targets = jnp.maximum(near_ref[:, columns(first)] - (own * rows + first - HALO), -1)
        gather_block(lambda at, n: padded[:, pl.ds(pl.multiple_of(first + at, HALO), n)], targets, picked)

    def convolve(b, picked):
        conv[:, columns(b * BLOCK)] = dot(turned_ref[1], picked[...]).astype(BF16)

    gather_edge(0, even)
    gather_edge(1, odd)
    convolve_edge(0, even)
    gather(1, even)
    convolve_edge(1, odd)

    def step(t, _):
        gather(2 * t + 2, odd)
        convolve(2 * t + 1, even)
        gather(2 * t + 3, even)
        convolve(2 * t + 2, odd)
        return 0

    lax.fori_loop(0, (blocks - 4) // 2, step, 0)
    norm_edge(0)
    norm_edge(1)
    gather(blocks - 2, odd)
    convolve(blocks - 3, even)
    gather(0, even)
    convolve(blocks - 2, odd)
    gather(blocks - 1, odd)
    convolve(0, even)
    convolve(blocks - 1, odd)
    linear = linear_ref[1].T

    def norm(b):
        first = b * BLOCK
        live = live_lanes(first, BLOCK, rows, before, count, after)
        last[:, columns(first)] = norm_block(
            padded[:, columns(first + HALO)], conv[:, columns(first)], linear, live
        )

    in_turn(0, blocks, norm)

    shards, depth, _ = send_ref.shape
    capacity = rows // shards
    pieces = BLOCK // capacity

    def store(b, block):
        for p in range(pieces):
            send_ref[b * pieces + p, 0:capacity, :] = block[p * capacity : (p + 1) * capacity, :]

    reorder(last, perm_ref, store)
    held = capacity // 128
    pad = jnp.zeros((depth - capacity - 2 * held, 128), F32)
    for d in range(shards):
        at = slice(d * held, (d + 1) * held)
        extra = jnp.concatenate([place_high_ref[at, :], place_low_ref[at, :], pad], axis=0)
        send_ref[d, capacity:, :] = extra.astype(BF16)


def reorder(source, from_ref, store, dots=6, unroll=16):
    channels, rows = source.shape
    windows = rows // WINDOW

    def one(b):
        pair = from_ref[pl.ds(b * 2, 2), :]
        wanted = jnp.concatenate([pair[0:1, :], pair[1:2, :]], axis=1)
        total = jnp.zeros((channels, BLOCK), F32)
        halves = [jnp.zeros((channels, 128), BF16) for _ in range(2)]
        lanes = [pair[h : h + 1, :] & 127 for h in range(2)]
        chunks = [jnp.broadcast_to((pair[h : h + 1, :] >> 7).astype(jnp.int16), (channels, 128)) for h in range(2)]
        rest = [(j, h) for j in range(dots * WINDOW // 128, rows // 128) for h in range(2)]
        done = 0
        for w in range(dots):
            total = total + dot(source[:, w * WINDOW : (w + 1) * WINDOW], selector(wanted - w * WINDOW, WINDOW))
            until = len(rest) * (w + 1) // dots
            for j, h in rest[done:until]:
                halves[h] = jnp.where(
                    chunks[h] == j, lane_pick(source[:, j * 128 : (j + 1) * 128], lanes[h]), halves[h]
                )
            done = until
        store(b, (total + jnp.concatenate(halves, axis=1).astype(F32)).astype(BF16).T)

    def step(t, _):
        for u in range(unroll):
            one(t * unroll + u)
        return 0

    lax.fori_loop(0, rows // BLOCK // unroll, step, 0)


def final_kernel(got_ref, out_hbm, out_ref, turned, from_ref, sems):
    rows = out_ref.shape[0]
    shards = got_ref.shape[0]
    groups = rows // 128
    capacity = rows // shards
    held = capacity // 128
    lanes = lax.broadcasted_iota(jnp.int32, (1, capacity), 1)
    total = jnp.zeros((2 * groups, 128), F32)
    for s in range(shards):
        turned[:, s * capacity : (s + 1) * capacity] = got_ref[s, 0:capacity, :].T
        extra = got_ref[s, capacity:, :].astype(F32)
        place = (extra[0:held, :] * 64.0 + extra[held : 2 * held, :]).astype(jnp.int32)
        place = jnp.concatenate([place[h : h + 1, :] for h in range(held)], axis=1)
        total = total + scatter_term(place, (s * capacity + lanes,), groups)
    from_ref[...] = joined(total, 0, groups)

    def copy(b):
        at = pl.ds(pl.multiple_of(b * BLOCK, BLOCK), BLOCK)
        return pltpu.make_async_copy(out_ref.at[at, :], out_hbm.at[at, :], sems.at[b])

    def store(b, block):
        out_ref[pl.ds(pl.multiple_of(b * BLOCK, BLOCK), BLOCK), :] = block
        copy(b).start()

    reorder(turned, from_ref, store)
    for b in range(rows // BLOCK):
        copy(b).wait()


def local(voxels, counts, neighbours, conv_weight, linear_weight, destination):
    rows, channels = voxels.shape
    offsets = neighbours.shape[0]
    both = ("wide", "narrow")
    shards = lax.axis_size(both)
    own = lax.axis_index(both)
    place = jnp.reshape(own, (1,)).astype(jnp.int32)
    extent = 2 * HALO
    struct = jax.ShapeDtypeStruct
    vmem = pl.BlockSpec(memory_space=VMEM)
    smem = pl.BlockSpec(memory_space=SMEM)
    hbm = pl.BlockSpec(memory_space=pltpu.HBM)

    packed = struct((extent + 32, channels), BF16)
    to_pair, to_side = pl.pallas_call(
        edges_kernel,
        out_shape=(packed, packed),
        in_specs=[smem, hbm, hbm],
        out_specs=(vmem, vmem),
        scratch_shapes=[VMEM((offsets, HALO), jnp.int32), VMEM((offsets, HALO), jnp.int32), pltpu.SemaphoreType.DMA((4,))],
        cost_estimate=pl.CostEstimate(flops=20_000_000_000, bytes_accessed=500_000, transcendentals=0),
        compiler_params=params(60),
        name="edges",
    )(place, voxels, neighbours)
    others = [(0, 0), (shards - 1, shards - 1)]
    for i in range(1, shards - 1, 2):
        others += [(i, i + 1), (i + 1, i)]
    side = lax.ppermute(to_side, both, others)
    pair = lax.ppermute(to_pair, both, [(i, i ^ 1) for i in range(shards)])

    table = (rows // 128, 128)
    padded = (channels, rows + BLOCK)
    picked = VMEM((offsets * channels, BLOCK), BF16)
    turned = (2, channels, offsets * channels)
    act, inner, perm, place_high, place_low, weights = pl.pallas_call(
        functools.partial(inner_kernel, shards),
        out_shape=(
            struct((channels, rows), BF16), struct(padded, BF16), struct(table, jnp.int32), struct(table, F32),
            struct(table, F32), struct(turned, BF16),
        ),
        in_specs=[smem, smem, vmem, vmem, hbm, vmem, vmem],
        out_specs=(vmem,) * 6,
        scratch_shapes=[
            VMEM(conv_weight.shape, BF16), picked, picked, VMEM(padded, BF16), pltpu.SemaphoreType.DMA((2,)),
        ],
        compiler_params=params(),
        cost_estimate=pl.CostEstimate(flops=20_000_000_000, bytes_accessed=6_000_000, transcendentals=0),
        name="first_layer",
    )(place, counts, voxels, neighbours, conv_weight, linear_weight, destination.reshape(1, rows))

    depth = rows // shards + 16
    send = pl.pallas_call(
        outer_kernel,
        out_shape=struct((shards, depth, channels), BF16),
        in_specs=[smem, smem] + [vmem] * 10,
        out_specs=vmem,
        scratch_shapes=[
            VMEM(packed.shape, BF16),
            VMEM(packed.shape, BF16),
            picked,
            picked,
            VMEM((channels, 2 * WINDOW), BF16),
            VMEM((channels, 2 * BLOCK), BF16),
            VMEM(padded, BF16),
            VMEM((channels, rows), BF16),
            VMEM((channels, rows), BF16),
        ],
        compiler_params=params(),
        cost_estimate=pl.CostEstimate(flops=30_000_000_000, bytes_accessed=8_000_000, transcendentals=0),
        name="second_layer",
    )(place, counts, pair, side, act, inner, neighbours, weights, linear_weight, perm, place_high, place_low)

    got = lax.all_to_all(send, both, split_axis=0, concat_axis=0, tiled=True)
    return pl.pallas_call(
        final_kernel,
        out_shape=struct((rows, channels), BF16),
        in_specs=[vmem],
        out_specs=hbm,
        scratch_shapes=[
            VMEM((rows, channels), BF16), VMEM((channels, rows), BF16), VMEM(table, jnp.int32),
            pltpu.SemaphoreType.DMA((rows // BLOCK,)),
        ],
        compiler_params=params(),
        name="hilbert_order",
    )(got)


def solution(mesh):
    in_specs = (
        P(("groups", "wide", "narrow"), None),
        P("groups"),
        P(None, ("groups", "wide", "narrow")),
        P(),
        P(),
        P(("groups", "wide", "narrow")),
    )
    out_specs = P(("groups", "wide", "narrow"), None)
    return jax.shard_map(local, mesh=mesh, in_specs=in_specs, out_specs=out_specs, check_vma=False)
```
